32 devices in a mesh: batch: 16 (over z, y, core), head: 2 (over x).
Axes of the slice: x: 2, y: 2, z: 4, core: 2. Of those that a mesh axis runs over, the one named last changes fastest.
Arguments:
- tokens: bfloat16 [32768, 1024], P(('batch', 'head')), may hold values from -6 to 6
- first_values: bfloat16 [32768, 1024], P('batch', 'head'), may hold values from -6 to 6
- out_grad: bfloat16 [32768, 1024], P(('batch', 'head')), may hold values from -6 to 6
- lengths: int32 [16], P('batch'), may hold values from 128 to 2048, as said below
- gain_attn: float32 [1024], replicated, may hold values from 0.25 to 1.75
- gain_mlp: float32 [1024], replicated, may hold values from 0.25 to 1.75
- w_query: bfloat16 [1024, 1024], P(None, 'head'), may hold values from -0.1875 to 0.1875
- w_key: bfloat16 [1024, 1024], P(None, 'head'), may hold values from -0.1875 to 0.1875
- w_value: bfloat16 [1024, 1024], P(None, 'head'), may hold values from -0.1875 to 0.1875
- w_out: bfloat16 [1024, 1024], P('head'), may hold values from -4 to 4
- w_gate: bfloat16 [1024, 2816], P(None, 'head'), may hold values from -0.1875 to 0.1875
- w_up: bfloat16 [1024, 2816], P(None, 'head'), may hold values from -0.1875 to 0.1875
- w_down: bfloat16 [2816, 1024], P('head'), may hold values from -0.109375 to 0.109375
Outputs:
- output: bfloat16 [32768, 1024], P(('batch', 'head'))
- grad_tokens: bfloat16 [32768, 1024], P(('batch', 'head'))
- grad_first_values: bfloat16 [32768, 1024], P('batch', 'head')
- grad_gain_attn: float32 [1024], replicated
- grad_gain_mlp: float32 [1024], replicated
- grad_w_query: float32 [1024, 1024], P(None, 'head')
- grad_w_key: float32 [1024, 1024], P(None, 'head')
- grad_w_value: float32 [1024, 1024], P(None, 'head')
- grad_w_out: float32 [1024, 1024], P('head')
- grad_w_gate: float32 [1024, 2816], P(None, 'head')
- grad_w_up: float32 [1024, 2816], P(None, 'head')
- grad_w_down: float32 [2816, 1024], P('head')
The draws below stay inside these ranges and needn't reach their ends.
Inputs may be any that keep to these rules, and one draw needn't show every extreme that they name: lengths[b] counts the valid leading places of slot b; in every draw some slot has exactly 2048 and some exactly 128.
All inputs are finite; a program needn't handle non-finite values.
Results may differ from the reference program's by a relative error of at most 0.019.
Values may be sent and summed in bfloat16 or wider, within the bound.
A program may use at most 384 MiB of HBM per device.

```python
import math
import jax
import jax.numpy as jnp
from jax import lax

D = 1024
HEADS = 16
HEAD_DIM = 64
FF = 2816
SLOT = 2048
BLOCK = 512
SLOTS = 16
TOKENS = 32768


def draw_lengths(key, part):
    key = jax.random.fold_in(key, 7)
    first_key, second_key = jax.random.split(key)
    span = SLOT - SLOT // 16
    picks = jax.random.randint(first_key, (SLOTS,), 0, span + 1)
    cut = picks * picks // span * picks // span
    result = SLOT - cut
    order = jax.random.permutation(second_key, SLOTS)
    result = result.at[order[0]].set(SLOT)
    result = result.at[order[1]].set(SLOT // 16)
    return result.astype(jnp.int32)


def block_levels(stream_key, extent, shards, low, high):
    factor_of, own = 1.0, jax.random.fold_in(stream_key, 6)
    for axis_at, blocks in shards:
        steps = jnp.exp(jax.random.uniform(jax.random.fold_in(own, axis_at), (blocks,), jnp.float32, low / len(shards), high / len(shards)))
        factor_of = factor_of * jnp.repeat(steps, extent[axis_at] // blocks).reshape([-1 if axis == axis_at else 1 for axis in range(len(extent))])
    return factor_of


def scatter_about(rng, dims, deviation, most, cuts=(), kind=jnp.bfloat16):
    loudness = block_levels(rng, dims, cuts, -0.22, 0.18) if cuts else 1.0
    array = jax.random.normal(rng, dims, jnp.float32) * deviation * loudness
    return jnp.minimum(jnp.maximum(array, -most), most).astype(kind)


def setup_inputs(seed: int = 0) -> dict:
    key_of = jax.random.split(jax.random.key(seed), 14)
    tokens = scatter_about(key_of[0], (TOKENS, D), 1.0, 6.0, ((0, 32),))
    first_values = scatter_about(key_of[1], (TOKENS, D), 1.0, 6.0, ((0, 16), (1, 2)))
    out_grad = scatter_about(key_of[2], (TOKENS, D), 1.0, 6.0, ((0, 32),))
    lengths = draw_lengths(jax.random.fold_in(key_of[13], 71), 0)
    gain_attn = jnp.clip(1.0 + 0.15 * jax.random.normal(key_of[4], (D,), jnp.float32), 0.25, 1.75)
    gain_mlp = jnp.clip(1.0 + 0.15 * jax.random.normal(key_of[5], (D,), jnp.float32), 0.25, 1.75)
    w_query = scatter_about(key_of[6], (D, D), D ** -0.5, 0.1875, ((1, 2),))
    w_key = scatter_about(key_of[7], (D, D), D ** -0.5, 0.1875, ((1, 2),))
    w_value = scatter_about(key_of[8], (D, D), D ** -0.5, 0.1875, ((1, 2),))
    w_out = scatter_about(key_of[9], (D, D), (max(4 * D // SLOT, 1)) ** -0.5, 4.0, ((0, 2),))
    w_gate = scatter_about(key_of[10], (D, FF), D ** -0.5, 0.1875, ((1, 2),))
    w_up = scatter_about(key_of[11], (D, FF), D ** -0.5, 0.1875, ((1, 2),))
    w_down = scatter_about(key_of[12], (FF, D), FF ** -0.5, 0.109375, ((0, 2),))
    return dict(tokens=tokens, first_values=first_values, out_grad=out_grad, lengths=lengths, gain_attn=gain_attn, gain_mlp=gain_mlp, w_query=w_query, w_key=w_key, w_value=w_value, w_out=w_out, w_gate=w_gate, w_up=w_up, w_down=w_down)


EPSILON = 1e-05
NEGATIVE = -1e+30
HIGH = lax.Precision.HIGHEST

@jax.custom_vjp
def low(v):
    return lax.optimization_barrier(v.astype(jnp.bfloat16)).astype(jnp.float32)

@jax.custom_vjp
def low_back(v):
    return v

def low_keep(v):
    return (low(v), None)

def low_pass(kept, grad):
    return (grad,)

def back_keep(v):
    return (v, None)

def back_low(kept, grad):
    return (low(grad),)
low.defvjp(low_keep, low_pass)
low_back.defvjp(back_keep, back_low)

def product(left, right):
    return jnp.dot(left, right, precision=HIGH)

def normalize(values, gain):
    return values * lax.rsqrt(lax.optimization_barrier(jnp.mean(values * values, axis=-1, keepdims=True)) + EPSILON) * gain

def rope_tables(count):
    half = HEAD_DIM // 2
    position = (jnp.arange(count) % SLOT).astype(jnp.float32)
    frequency = jnp.exp(jnp.arange(half).astype(jnp.float32) * (-2.0 * math.log(10000.0) / HEAD_DIM))
    angles = position[:, None] * frequency[None, :]
    return (jnp.cos(angles)[:, None, :], jnp.sin(angles)[:, None, :])

def rotate(values, cosine, sine):
    half = values.shape[-1] // 2
    first = values[..., :half]
    second = values[..., half:]
    return jnp.concatenate([first * cosine - second * sine, second * cosine + first * sine], axis=-1)

def attend_block(start, queries, keys, values, length):
    query_block = lax.dynamic_slice_in_dim(queries, start, BLOCK, 0)
    scores = jnp.einsum('qhd,khd->hqk', query_block, keys, precision=HIGH) * (1.0 / math.sqrt(HEAD_DIM))
    scores = low_back(scores)
    rows = start + jnp.arange(BLOCK, dtype=jnp.int32)
    columns = jnp.arange(SLOT, dtype=jnp.int32)
    allowed = (columns[None, :] <= rows[:, None]) & (columns[None, :] < length)
    scores = jnp.where(allowed[None], scores, NEGATIVE)
    peak = lax.optimization_barrier(jnp.max(scores, axis=-1, keepdims=True))
    weights = jnp.exp(scores - peak)
    probs = weights / lax.optimization_barrier(jnp.sum(weights, axis=-1, keepdims=True))
    return jnp.einsum('hqk,khd->qhd', low(probs), values, precision=HIGH)

def slot_forward(inputs, first, length, gain_attn, gain_mlp, w_query, w_key, w_value, w_out, w_gate, w_up, w_down):
    cosine, sine = rope_tables(SLOT)
    hone = low(normalize(inputs, gain_attn))
    q_pre = low_back(product(hone, w_query)).reshape(SLOT, HEADS, HEAD_DIM)
    k_pre = low_back(product(hone, w_key)).reshape(SLOT, HEADS, HEAD_DIM)
    v_pre = low_back(product(hone, w_value))
    queries = low(rotate(q_pre, cosine, sine))
    keys = low(rotate(k_pre, cosine, sine))
    mixed = low(0.5 * v_pre + 0.5 * first).reshape(SLOT, HEADS, HEAD_DIM)
    starts = jnp.arange(SLOT // BLOCK, dtype=jnp.int32) * BLOCK
    checked = jax.checkpoint(attend_block)
    blocks = lax.map(lambda start: checked(start, queries, keys, mixed, length), starts)
    attended = low_back(low(blocks.reshape(SLOT, D)))
    middle = inputs + low_back(product(attended, w_out))
    htwo = low(normalize(middle, gain_mlp))
    gate = low_back(product(htwo, w_gate))
    upper = low_back(product(htwo, w_up))
    hidden = low(jax.nn.silu(gate) * upper)
    return middle + low_back(product(hidden, w_down))

def reference(tokens, first_values, out_grad, lengths, gain_attn, gain_mlp, w_query, w_key, w_value, w_out, w_gate, w_up, w_down):
    inputs = tokens.astype(jnp.float32).reshape(SLOTS, SLOT, D)
    firsts = first_values.astype(jnp.float32).reshape(SLOTS, SLOT, D)
    lengths = lengths.astype(jnp.int32)
    valid = (jnp.arange(SLOT, dtype=jnp.int32)[None, :] < lengths[:, None]).astype(jnp.float32)
    cotangent = out_grad.astype(jnp.float32).reshape(SLOTS, SLOT, D) * valid[:, :, None]
    weights = (gain_attn.astype(jnp.float32), gain_mlp.astype(jnp.float32), w_query.astype(jnp.float32), w_key.astype(jnp.float32), w_value.astype(jnp.float32), w_out.astype(jnp.float32), w_gate.astype(jnp.float32), w_up.astype(jnp.float32), w_down.astype(jnp.float32))

    def layer(all_inputs, all_firsts, *params):

        def step(carry, item):
            slot_inputs, slot_first, slot_length = item
            return (carry, slot_forward(slot_inputs, slot_first, slot_length, *params))
        _, outs = lax.scan(step, jnp.zeros((), jnp.float32), (all_inputs, all_firsts, lengths))
        return outs
    result, pull = jax.vjp(layer, inputs, firsts, *weights)
    grads = pull(cotangent)
    return (result.reshape(TOKENS, D).astype(jnp.bfloat16), grads[0].reshape(TOKENS, D).astype(jnp.bfloat16), grads[1].reshape(TOKENS, D).astype(jnp.bfloat16), grads[2], grads[3], grads[4], grads[5], grads[6], grads[7], grads[8], grads[9], grads[10])
```

```python
import functools, math
import jax, jax.numpy as jnp
from jax import lax
from jax.experimental import pallas as pl
from jax.experimental.pallas import tpu as pltpu
from jax.sharding import Mesh, PartitionSpec as P
SLOT=2048; HEAD_DIM=64
C2=math.log2(math.e)/8.0
NT=(((1,),(1,)),((),()))
TN=(((0,),(0,)),((),()))
NN=(((1,),(0,)),((),()))
def dot(a,b,dims=NN): return lax.dot_general(a,b,dims,preferred_element_type=jnp.float32)

def fwd_kernel(BQ,BK,len_ref,q_ref,k_ref,v_ref,o_ref,lse_ref,kb_ref,s_ref):
    length=len_ref[0]
    lane=lax.broadcasted_iota(jnp.int32,(SLOT,128),1)
    row=lax.broadcasted_iota(jnp.int32,(SLOT,128),0)
    k=k_ref[...]; v=v_ref[...]
    vs=[]
    for h in range(2):
        mine=(lane//64)==h
        first=lane==(64*(1-h))
        bias=jnp.where(first&(row>=length),-1e30,0.0).astype(jnp.bfloat16)
        kb_ref[h]=jnp.where(mine,k,bias)
        kb_ref[2+h]=jnp.where(mine,v,jnp.ones_like(v))
    laneq=lax.broadcasted_iota(jnp.int32,(BQ,128),1)
    for i in range(SLOT//BQ):
        rows=slice(i*BQ,(i+1)*BQ)
        q=q_ref[rows,:]
        outs=[]
        for h in range(2):
            mine=(laneq//64)==h
            qh=jnp.where(mine,q,jnp.ones_like(q))
            ext=(i+1)*BQ
            nb=(ext+BK-1)//BK
            mx=None
            for j in range(nb):
                w=min(BK,ext-j*BK)
                s=dot(qh,kb_ref[h,pl.ds(j*BK,w),:],NT)
                if j*BK+w>i*BQ+1:
                    r=lax.broadcasted_iota(jnp.int32,(BQ,w),0)+i*BQ
                    c=lax.broadcasted_iota(jnp.int32,(BQ,w),1)+j*BK
                    s=jnp.where(c<=r,s,-1e30)
                s_ref[h,:,pl.ds(j*BK,w)]=s
                m=jnp.max(s,axis=-1,keepdims=True)
                mx=m if mx is None else jnp.maximum(mx,m)
            mc=mx*C2
            acc=None
            for j in range(nb):
                w=min(BK,ext-j*BK)
                p=jnp.exp2(s_ref[h,:,pl.ds(j*BK,w)]*C2-mc).astype(jnp.bfloat16)
                a=dot(p,kb_ref[2+h,pl.ds(j*BK,w),:])
                acc=a if acc is None else acc+a
            other=64*(1-h)
            l=acc[:,other:other+1]
            outs.append((acc/l,mc+jnp.log2(l)))
        o_ref[rows,:]=jnp.where((laneq//64)==0,outs[0][0],outs[1][0]).astype(jnp.bfloat16)
        lse_ref[0,:,pl.ds(i*BQ,BQ)]=jnp.where(lax.broadcasted_iota(jnp.int32,(BQ,128),1)==0,outs[0][1],outs[1][1]).T[0:8]
def att_fwd(length,q,k,v,BQ=512,BK=512):
    W=q.shape[1]; n=W//128
    blk=pl.BlockSpec((SLOT,128),lambda p:(0,p))
    return pl.pallas_call(functools.partial(fwd_kernel,BQ,BK),grid=(n,),
        in_specs=[pl.BlockSpec(memory_space=pltpu.SMEM),blk,blk,blk],
        out_specs=[blk,pl.BlockSpec((1,8,SLOT),lambda p:(p,0,0))],
        out_shape=[jax.ShapeDtypeStruct((SLOT,W),jnp.bfloat16),jax.ShapeDtypeStruct((n,8,SLOT),jnp.float32)],
        scratch_shapes=[pltpu.VMEM((4,SLOT,128),jnp.bfloat16),pltpu.VMEM((2,BQ,SLOT),jnp.float32)],
        compiler_params=pltpu.CompilerParams(vmem_limit_bytes=56<<20),name="attfwd_%d_%d"%(BQ,BK))(length,q,k,v)

def bwd_kernel(BQ,BK,len_ref,q_ref,k_ref,v_ref,do_ref,lse_ref,dl_ref,cos_ref,sin_ref,dq_ref,dk_ref,dv_ref,qs,ks,vs,dqa):
    length=len_ref[0]
    lane=lax.broadcasted_iota(jnp.int32,(SLOT,128),1)
    row=lax.broadcasted_iota(jnp.int32,(SLOT,128),0)
    k=k_ref[0]; q=q_ref[0]; do=do_ref[...]
    for h in range(2):
        mine=(lane//64)==h
        first=lane==(64*(1-h))
        bias=jnp.where(first&(row>=length),-1e30,0.0).astype(jnp.bfloat16)
        ks[h]=jnp.where(mine,k,bias)
        ks[2+h]=jnp.where(mine,k,jnp.zeros_like(k))
        qs[h]=jnp.where(mine,q,jnp.ones_like(q))
        qs[2+h]=jnp.where(mine,q,jnp.zeros_like(q))
        vs[h]=jnp.where(mine,do,jnp.zeros_like(do))
    dqa[...]=jnp.zeros_like(dqa)
    nq=SLOT//BQ
    for j in range(SLOT//BK):
        cols=slice(j*BK,(j+1)*BK)
        v=v_ref[0,cols,:]
        dk=dv=None
        for i in range((j*BK)//BQ,nq):
            rows=slice(i*BQ,(i+1)*BQ)
            for h in range(2):
                st=dot(ks[h,cols,:],qs[h,rows,:],NT)
                if (j+1)*BK>i*BQ+1:
                    c=lax.broadcasted_iota(jnp.int32,(BK,BQ),0)+j*BK
                    r=lax.broadcasted_iota(jnp.int32,(BK,BQ),1)+i*BQ
                    st=jnp.where(c<=r,st,-1e30)
                pt=jnp.exp2(st*C2-lse_ref[0,h:h+1,rows])
                dpt=dot(v,vs[h,rows,:],NT)
                dst=(pt*(dpt-dl_ref[0,h:h+1,rows])).astype(jnp.bfloat16)
                a=dot(pt.astype(jnp.bfloat16),vs[h,rows,:])
                dv=a if dv is None else dv+a
                b=dot(dst,qs[2+h,rows,:])
                dk=b if dk is None else dk+b
                dqa[rows,:]+=dot(dst,ks[2+h,cols,:],TN)
        lf=(lax.broadcasted_iota(jnp.int32,(BK,128),1)%64)<32
        dk_ref[cols,:]=rot(dk*0.125,cos_ref[cols,:],-sin_ref[cols,:],lf).astype(dk_ref.dtype)
        dv_ref[cols,:]=(dv*0.5).astype(dv_ref.dtype)
    lf=(lax.broadcasted_iota(jnp.int32,(SLOT,128),1)%64)<32
    dq_ref[...]=rot(dqa[...]*0.125,cos_ref[...],-sin_ref[...],lf).astype(dq_ref.dtype)
def att_bwd(length,q,k,v,do,lse,delta,cos,sin,BQ=512,BK=512,odt=jnp.bfloat16):
    tab=pl.BlockSpec((SLOT,128),lambda p:(0,0),pipeline_mode=pl.Buffered(1))
    n=q.shape[0]; W=n*128
    blk=pl.BlockSpec((SLOT,128),lambda p:(0,p)); tri=pl.BlockSpec((1,SLOT,128),lambda p:(p,0,0))
    st=pl.BlockSpec((1,8,SLOT),lambda p:(p,0,0))
    return pl.pallas_call(functools.partial(bwd_kernel,BQ,BK),grid=(n,),
        in_specs=[pl.BlockSpec(memory_space=pltpu.SMEM),tri,tri,tri,blk,st,st,tab,tab],
        out_specs=[blk,blk,blk],
        out_shape=[jax.ShapeDtypeStruct((SLOT,W),odt)]*3,
        scratch_shapes=[pltpu.VMEM((4,SLOT,128),jnp.bfloat16),pltpu.VMEM((4,SLOT,128),jnp.bfloat16),pltpu.VMEM((2,SLOT,128),jnp.bfloat16),pltpu.VMEM((SLOT,128),jnp.float32)],
        compiler_params=pltpu.CompilerParams(vmem_limit_bytes=56<<20),name="attbwd_%d_%d"%(BQ,BK))(length,q,k,v,do,lse,delta,cos,sin)

EPS=1e-5
R2=256
def norm_block(x,gain):
    r=lax.rsqrt(jnp.mean(x*x,axis=-1,keepdims=True)+EPS)
    n=x*r
    return n,r
def rot(x,cos,sin,lane_first):
    up=pltpu.roll(x,96,1)
    dn=pltpu.roll(x,32,1)
    return x*cos+jnp.where(lane_first,up,dn)*sin

def qkv_kernel(R,t_ref,f_ref,g_ref,cos_ref,sin_ref,wq,wk,wv,q_ref,k_ref,m_ref):
    x=t_ref[...].astype(jnp.float32)
    n,_=norm_block(x,None)
    h=(n*g_ref[...]).astype(jnp.bfloat16)
    cos=cos_ref[...]; sin=sin_ref[...]
    lf=(lax.broadcasted_iota(jnp.int32,(R,128),1)%64)<32
    for w,o in ((wq,q_ref),(wk,k_ref)):
        y=dot(h,w[...])
        for c in range(y.shape[1]//128):
            o[:,c*128:(c+1)*128]=rot(y[:,c*128:(c+1)*128],cos,sin,lf).astype(jnp.bfloat16)
    y=dot(h,wv[...])
    m_ref[...]=(0.5*y+0.5*f_ref[...].astype(jnp.float32)).astype(jnp.bfloat16)
def qkv_fwd(t,f,gain,cos,sin,wq,wk,wv,R=256):
    N,D=t.shape; W=wq.shape[1]
    rb=lambda w:pl.BlockSpec((R,w),lambda i:(i,0))
    full=lambda a:pl.BlockSpec(a.shape,lambda i:(0,0),pipeline_mode=pl.Buffered(1))
    return pl.pallas_call(functools.partial(qkv_kernel,R),grid=(N//R,),
        in_specs=[rb(D),rb(W),full(gain),rb(128),rb(128),full(wq),full(wk),full(wv)],
        out_specs=[rb(W)]*3,out_shape=[jax.ShapeDtypeStruct((N,W),jnp.bfloat16)]*3,
        compiler_params=pltpu.CompilerParams(vmem_limit_bytes=56<<20),name="qkvfwd_%d"%R)(t,f,gain,cos,sin,wq,wk,wv)

def mlp_kernel(R,NS,FH,len_ref,t_ref,pa_ref,pb_ref,og_ref,g_ref,wg_h,wu_h,wd_h,wg_f,wu_f,wd_f,
               op_ref,gh_ref,comb_h,
               wgu,wd,agu,ad,stage,wsem,ssem):
    step=pl.program_id(0)
    D=t_ref.shape[1]
    diag=lax.axis_index("core")==lax.axis_index("head")
    load=lambda a,b,c:[pltpu.make_async_copy(a,wgu.at[:,pl.ds(0,FH)],wsem.at[0]),
         pltpu.make_async_copy(b,wgu.at[:,pl.ds(FH,FH)],wsem.at[1]),
         pltpu.make_async_copy(c,wd,wsem.at[2])]
    cps=load(wg_h,wu_h,wd_h); far=load(wg_f,wu_f,wd_f)
    @pl.when(step==0)
    def _():
        @pl.when(diag)
        def _():
            for c in cps: c.start()
        @pl.when(jnp.logical_not(diag))
        def _():
            for c in far: c.start()
        agu[...]=jnp.zeros_like(agu)
        ad[...]=jnp.zeros_like(ad)
        for c in cps: c.wait()
    x=t_ref[...].astype(jnp.float32)+(pa_ref[...].astype(jnp.float32)+pb_ref[...].astype(jnp.float32))
    n,_=norm_block(x,None)
    h=(n*g_ref[...]).astype(jnp.bfloat16)
    row=lax.broadcasted_iota(jnp.int32,(R,1),0)+step*R
    g=jnp.where(row<len_ref[0],og_ref[...],jnp.zeros((),jnp.bfloat16))
    gu=dot(h,wgu[...])
    gate=gu[:,:FH]; up=gu[:,FH:]
    gh=dot(g,wd[...],NT)
    sg=0.5*jnp.tanh(0.5*gate)+0.5
    silu=gate*sg
    hid=(silu*up).astype(jnp.bfloat16)
    gu_=(gh*silu).astype(jnp.bfloat16)
    gg_=(gh*up*(sg*(1.0+gate*(1.0-sg)))).astype(jnp.bfloat16)
    op_ref[...]=dot(hid,wd[...]).astype(jnp.bfloat16)
    gh_ref[...]=(dot(gg_,wgu[:,:FH],NT)+dot(gu_,wgu[:,FH:],NT)).astype(jnp.bfloat16)
    ad[...]+=dot(hid,g,TN)
    agu[:,:FH]+=dot(h,gg_,TN)
    agu[:,FH:]+=dot(h,gu_,TN)
    @pl.when(step==NS-1)
    def _():
        tiles=[(agu,c,c*D,D) for c in range(2*FH//128)]+[(ad,c,(2*FH//128)*D+c*FH,FH) for c in range(D//128)]
        pend=[None]*4
        for i,(a,c,off,ln) in enumerate(tiles):
            s=i%4
            if pend[s] is not None: pend[s].wait()
            stage[s,0:ln,:]=a[:,c*128:(c+1)*128].astype(jnp.bfloat16)
            cp=pltpu.make_async_copy(stage.at[s,pl.ds(0,ln)],comb_h.at[pl.ds(off,ln)],ssem.at[s])
            cp.start(); pend[s]=cp
        for p in pend: p.wait()
def mlp(length,t,pa,pb,og,gain,wg,wu,wd,wg_f,wu_f,wd_f,R=256):
    N,D=t.shape; FH=wg.shape[1]; NS=N//R
    rb=pl.BlockSpec((R,D),lambda i:(i,0))
    anyb=pl.BlockSpec(memory_space=pl.ANY)
    full=lambda a:pl.BlockSpec(a.shape,lambda i:(0,0),pipeline_mode=pl.Buffered(1))
    rows=(2*FH//128)*D+(D//128)*FH
    return pl.pallas_call(functools.partial(mlp_kernel,R,NS,FH),grid=(NS,),
        in_specs=[pl.BlockSpec(memory_space=pltpu.SMEM),rb,rb,rb,rb,full(gain)]+[anyb]*6,
        out_specs=[rb,rb,anyb],
        out_shape=[jax.ShapeDtypeStruct((N,D),jnp.bfloat16)]*2+[jax.ShapeDtypeStruct((rows,128),jnp.bfloat16)],
        scratch_shapes=[pltpu.VMEM((D,2*FH),jnp.bfloat16),pltpu.VMEM((FH,D),jnp.bfloat16),pltpu.VMEM((D,2*FH),jnp.float32),pltpu.VMEM((FH,D),jnp.float32),
            pltpu.VMEM((4,max(D,FH),128),jnp.bfloat16),pltpu.SemaphoreType.DMA((3,)),pltpu.SemaphoreType.DMA((4,))],
        compiler_params=pltpu.CompilerParams(vmem_limit_bytes=60<<20),name="mlp_%d"%R)(length,t,pa,pb,og,gain,wg,wu,wd,wg_f,wu_f,wd_f)

def mid_kernel(R,NS,len_ref,t_ref,pa_ref,pb_ref,og_ref,ga_ref,gb_ref,at_ref,g_ref,wo,
               gm_ref,gat_ref,dl_ref,gwo_ref,gg_ref,acc):
    step=pl.program_id(0)
    x=t_ref[...].astype(jnp.float32)+(pa_ref[...].astype(jnp.float32)+pb_ref[...].astype(jnp.float32))
    n,r=norm_block(x,None)
    gh2=ga_ref[...].astype(jnp.float32)+gb_ref[...].astype(jnp.float32)
    row=lax.broadcasted_iota(jnp.int32,(R,1),0)+step*R
    mg=jnp.where(row<len_ref[0],og_ref[...].astype(jnp.float32),0.0)
    gn=gh2*g_ref[...]
    inner=jnp.mean(gn*n,axis=-1,keepdims=True)
    gm=(mg+r*(gn-n*inner)).astype(jnp.bfloat16)
    gm_ref[...]=gm
    part=jnp.sum((gh2*n).reshape(R//8,8,-1),axis=0)
    at=at_ref[...]
    ga=dot(gm,wo[...],NT).astype(jnp.bfloat16)
    gat_ref[...]=ga
    xx=ga.astype(jnp.float32)*at.astype(jnp.float32)
    hi=xx.astype(jnp.bfloat16); lo=(xx-hi.astype(jnp.float32)).astype(jnp.bfloat16)
    W=at.shape[1]
    hr=lax.broadcasted_iota(jnp.int32,(8*(W//128),W),0); ln=lax.broadcasted_iota(jnp.int32,(8*(W//128),W),1)
    ind=((ln//64)==((hr//8)*2+hr%8)) & (hr%8<2)
    ind=jnp.where(ind,1.0,0.0).astype(jnp.bfloat16)
    d=dot(ind,hi,NT)+dot(ind,lo,NT)
    dl_ref[...]=d.reshape(W//128,8,R)
    w=dot(at,gm,TN)
    @pl.when(step==0)
    def _():
        acc[...]=w; gg_ref[...]=part
    @pl.when(step>0)
    def _():
        acc[...]+=w; gg_ref[...]+=part
    @pl.when(step==NS-1)
    def _():
        for c in range(acc.shape[1]//128):
            gwo_ref[c*W:(c+1)*W,:]=acc[:,c*128:(c+1)*128].astype(jnp.bfloat16)
def mid(length,t,pa,pb,og,ga,gb,at,gain,wo,R=256):
    N,D=t.shape; W=at.shape[1]; NS=N//R
    rb=lambda w:pl.BlockSpec((R,w),lambda i:(i,0))
    full=lambda a:pl.BlockSpec(a.shape,lambda i:(0,0),pipeline_mode=pl.Buffered(1))
    return pl.pallas_call(functools.partial(mid_kernel,R,NS),grid=(NS,),
        in_specs=[pl.BlockSpec(memory_space=pltpu.SMEM)]+[rb(D)]*6+[rb(W),full(gain),full(wo)],
        out_specs=[rb(D),rb(W),pl.BlockSpec((W//128,8,R),lambda i:(0,0,i)),pl.BlockSpec((W*D//128,128),lambda i:(0,0)),pl.BlockSpec((8,D),lambda i:(0,0))],
        out_shape=[jax.ShapeDtypeStruct((N,D),jnp.bfloat16),jax.ShapeDtypeStruct((N,W),jnp.bfloat16),jax.ShapeDtypeStruct((W//128,8,N),jnp.float32),
            jax.ShapeDtypeStruct((W*D//128,128),jnp.bfloat16),jax.ShapeDtypeStruct((8,D),jnp.float32)],
        scratch_shapes=[pltpu.VMEM((W,D),jnp.float32)],
        compiler_params=pltpu.CompilerParams(vmem_limit_bytes=56<<20),name="mid_%d"%R)(length,t,pa,pb,og,ga,gb,at,gain,wo)

def qkvb_kernel(R,NS,t_ref,q_ref,k_ref,v_ref,g_ref,wq,wk,wv,gh_ref,gw_ref,acc):
    step=pl.program_id(0)
    x=t_ref[...].astype(jnp.float32)
    n,_=norm_block(x,None)
    h=(n*g_ref[...]).astype(jnp.bfloat16)
    gq=q_ref[...]; gk=k_ref[...]; gv=v_ref[...]
    gh_ref[...]=(dot(gq,wq[...],NT)+dot(gk,wk[...],NT)+dot(gv,wv[...],NT)).astype(jnp.bfloat16)
    W=gq.shape[1]; D=x.shape[1]
    @pl.when(step==0)
    def _(): acc[...]=jnp.zeros_like(acc)
    for i,g in enumerate((gq,gk,gv)):
        acc[:,i*W:(i+1)*W]+=dot(h,g,TN)
    @pl.when(step==NS-1)
    def _():
        for c in range(3*W//128):
            gw_ref[c*D:(c+1)*D,:]=acc[:,c*128:(c+1)*128].astype(jnp.bfloat16)
def qkv_bwd(t,gq,gk,gv,gain,wq,wk,wv,R=256):
    N,D=t.shape; W=wq.shape[1]; NS=N//R
    rb=lambda w:pl.BlockSpec((R,w),lambda i:(i,0))
    full=lambda a:pl.BlockSpec(a.shape,lambda i:(0,0),pipeline_mode=pl.Buffered(1))
    return pl.pallas_call(functools.partial(qkvb_kernel,R,NS),grid=(NS,),
        in_specs=[rb(D),rb(W),rb(W),rb(W),full(gain),full(wq),full(wk),full(wv)],
        out_specs=[rb(D),pl.BlockSpec((3*W*D//128,128),lambda i:(0,0))],
        out_shape=[jax.ShapeDtypeStruct((N,D),jnp.bfloat16),jax.ShapeDtypeStruct((3*W*D//128,128),jnp.bfloat16)],
        scratch_shapes=[pltpu.VMEM((D,3*W),jnp.float32)],
        compiler_params=pltpu.CompilerParams(vmem_limit_bytes=56<<20),name="qkvb_%d"%R)(t,gq,gk,gv,gain,wq,wk,wv)

def unpack_kernel(b_ref,o_ref): o_ref[...]=b_ref[...].astype(jnp.float32)
def unpack(buf,off,D,W):
    o=off//D
    return pl.pallas_call(unpack_kernel,grid=(W//128,),in_specs=[pl.BlockSpec((D,128),lambda c:(o+c,0))],
       out_specs=pl.BlockSpec((D,128),lambda c:(0,c)),out_shape=jax.ShapeDtypeStruct((D,W),jnp.float32),name="unpack_%d"%W)(buf)


ALL=("zy","core","head")

class Links:
    def __init__(self,send,recv,local):
        self.send,self.recv,self.local=send,recv,local
        self.remote_count=0; self.local_count=0
    def remote(self,src,dst,device):
        at=self.remote_count; self.remote_count+=1
        return pltpu.make_async_remote_copy(src_ref=src,dst_ref=dst,send_sem=self.send.at[at],recv_sem=self.recv.at[at],
            device_id=device,device_id_type=pl.DeviceIdType.MESH)
    def copy(self,src,dst):
        at=self.local_count; self.local_count+=1
        return pltpu.make_async_copy(src,dst,self.local.at[at])

def spread_bits(groups):
    count=min(groups,8); bits=[]
    while count>1:
        count//=2; bits.append(count)
    return bits

class Spread:
    def __init__(self,links,home,full,bits,zy,swap_dev,peer):
        m=2**len(bits); rows=home.shape[0]//m
        place=0
        for level,b in enumerate(bits): place=place+((zy//b)%2)*(2**level)
        one=pl.ds(pl.multiple_of(place*rows,rows),rows)
        self.steps=[links.remote(home.at[one],full.at[one],swap_dev)]
        for level,b in enumerate(bits):
            size=2**level
            block=pl.ds(pl.multiple_of((place//size)*size*rows,size*rows),size*rows)
            self.steps.append(links.remote(full.at[block],full.at[block],peer(b)))

def front_kernel(groups,
        tok_h,fv_h,og_h,len_h,g_ref,ch_ref,sh_ref,cl_ref,sl_ref,wq_h,wk_h,wv_h,wo_h,wg_h,wu_h,wd_h,
        tok_o,og_o,len_o,q_o,k_o,m_o,att_o,lse_o,pa_o,pb_o,wq_o,wk_o,wv_o,wo_o,wg_o,wu_o,wd_o,
        tok_v,len_v,fv_v,wq_v,wk_v,wv_v,wo_v,cos_v,sin_v,qs,ks,vp,ms,kb_ref,s_ref,att_v,lse_v,pa_v,
        send_sem,recv_sem,local_sem):
    zy=lax.axis_index("zy"); core=lax.axis_index("core"); x=lax.axis_index("head")
    off=core!=x; diag=core==x
    L=Links(send_sem,recv_sem,local_sem)
    swap_dev=(zy,1-core,1-x); core_dev=(zy,1-core,x)
    bits=spread_bits(groups)
    peer=lambda b:(zy+b-2*b*((zy//b)%2),core,x)
    barrier=pltpu.get_barrier_semaphore()
    MESH=pl.DeviceIdType.MESH
    half=tok_h.shape[0]; D=tok_h.shape[1]; W=wq_h.shape[1]; NP=W//128
    CH=256; NC=half//CH
    sp={n:Spread(L,h,f,bits,zy,swap_dev,peer) for n,h,f in (("q",wq_h,wq_v),("k",wk_h,wk_v),("v",wv_h,wv_v),("o",wo_h,wo_v),("g",wg_h,wg_o),("u",wu_h,wu_o),("d",wd_h,wd_o))}
    mine=lambda k:pl.ds(pl.multiple_of(core*half+k*CH,CH),CH)
    swap_len=L.remote(len_h,len_v,swap_dev)
    there=lambda k:pl.ds(pl.multiple_of((1-core)*half+k*CH,CH),CH)
    swap_tok=[L.remote(tok_h.at[pl.ds(k*CH,CH)],tok_v.at[there(k)],swap_dev) for k in range(NC)]
    core_tok=[L.remote(tok_v.at[mine(k)],tok_v.at[mine(k)],core_dev) for k in range(NC)]
    swap_fv=[L.remote(fv_h.at[:,pl.ds(p*128,128)],fv_v.at[p],swap_dev) for p in range(NP)]
    HH=half//2
    part=lambda c,j:pl.ds(pl.multiple_of(c*half+j*HH,HH),HH)
    swap_og=[L.remote(og_h.at[pl.ds(j*HH,HH)],og_o.at[part(1-core,j)],swap_dev) for j in range(2)]
    my_half=pl.ds(pl.multiple_of(core*half,half),half)
    core_og=[L.remote(og_o.at[part(core,j)],og_o.at[part(core,j)],core_dev) for j in range(2)]
    PR=512
    core_pa=[L.remote(pa_v.at[pl.ds(r*PR,PR)],pb_o.at[pl.ds(r*PR,PR)],core_dev) for r in range(SLOT//PR)]
    out_pa=[L.copy(pa_v.at[pl.ds(r*PR,PR)],pa_o.at[pl.ds(r*PR,PR)]) for r in range(SLOT//PR)]
    own_tok=L.copy(tok_h,tok_v.at[my_half])
    own_len=L.copy(len_h,len_v)
    own_fv=[L.copy(fv_h.at[:,pl.ds(p*128,128)],fv_v.at[p]) for p in range(NP)]
    own_og=[L.copy(og_h,pa_v.at[pl.ds(0,half)]),L.copy(pa_v.at[pl.ds(0,half)],og_o.at[my_half])]
    core_og_own=[L.remote(og_h.at[pl.ds(j*HH,HH)],og_o.at[part(core,j)],core_dev) for j in range(2)]
    own_qkv=[L.copy(h,v) for h,v in ((wq_h,wq_v),(wk_h,wk_v),(wv_h,wv_v))]
    own_o=L.copy(wo_h,wo_v)
    outs=[L.copy(a,b) for a,b in ((tok_v,tok_o),(len_v,len_o),(qs,q_o),(ks,k_o),(wq_v,wq_o),(wk_v,wk_o),(wv_v,wv_o))]
    outs2=[L.copy(a,b) for a,b in ((ms,m_o),(att_v,att_o),(lse_v,lse_o),(wo_v,wo_o))]

    pl.semaphore_signal(barrier,inc=1,device_id=core_dev,device_id_type=MESH)
    @pl.when(off)
    def _():
        pl.semaphore_signal(barrier,inc=1,device_id=swap_dev,device_id_type=MESH)
        for b in bits: pl.semaphore_signal(barrier,inc=1,device_id=peer(b),device_id_type=MESH)
        pl.semaphore_wait(barrier,2+len(bits))
        for n in "qkvog": sp[n].steps[0].start()
        swap_len.start()
    @pl.when(diag)
    def _():
        pl.semaphore_wait(barrier,1)
        own_tok.start(); own_len.start()
        for c in own_qkv: c.start()
        own_tok.wait()
        for k in range(NC): core_tok[k].start()
        own_len.wait()
        for c in own_fv: c.start()
        own_o.start(); own_og[0].start()
        for c in core_og_own: c.start()
    sign=jnp.where((lax.broadcasted_iota(jnp.int32,(1,128),1)%64)<32,-1.0,1.0)
    cl=cl_ref[...]; sl=sl_ref[...]
    def table(a,_):
        rows=pl.ds(pl.multiple_of(a*32,32),32)
        ch=ch_ref[pl.ds(a,1),:]; sh=sh_ref[pl.ds(a,1),:]
        cos_v[rows,:]=ch*cl-sh*sl
        sin_v[rows,:]=(sh*cl+ch*sl)*sign
        return 0
    lax.fori_loop(0,SLOT//32,table,0)
    nl=len(bits)
    def advance(n,level):
        sp[n].steps[level].wait_recv(); sp[n].steps[level+1].start()
    @pl.when(off)
    def _():
        for level in range(nl):
            for n in ("qkvog" if level<max(nl-1,1) else "qkv"): advance(n,level)
            if level==0:
                for k in range(NC): swap_tok[k].start()
        swap_len.wait_recv()
    @pl.when(diag)
    def _():
        for c in own_qkv: c.wait()
        own_og[0].wait(); own_og[1].start()
    gain=g_ref[...]
    lf=(lax.broadcasted_iota(jnp.int32,(CH,128),1)%64)<32
    def project(block):
        rows=pl.ds(pl.multiple_of(block*CH,CH),CH)
        t=tok_v[rows,:].astype(jnp.float32)
        n,_=norm_block(t,None)
        h=(n*gain).astype(jnp.bfloat16)
        cos=cos_v[rows,:]; sin=sin_v[rows,:]
        for w,o in ((wq_v,qs),(wk_v,ks)):
            y=dot(h,w[...])
            for c in range(NP):
                o[c,rows,:]=rot(y[:,c*128:(c+1)*128],cos,sin,lf).astype(jnp.bfloat16)
        y=dot(h,wv_v[...])
        for c in range(NP): vp[c,rows,:]=y[:,c*128:(c+1)*128]
    for k in range(NC):
        if k==0:
            @pl.when(off)
            def _():
                for n in "qkv": sp[n].steps[nl].wait_recv()
        @pl.when(off)
        def _():
            core_tok[k].wait_recv()
        project(x*NC+k)
        @pl.when(off)
        def _():
            if k==0: sp["u"].steps[0].start(); swap_fv[0].start()
            if k==1 and nl>1: advance("o",nl-1)
            if k==2 and nl>1: advance("g",nl-1)
            if k==3: advance("u",0)
    for k in range(NC):
        @pl.when(off)
        def _():
            swap_tok[k].wait_recv()
            core_tok[k].start()
            if k==1: swap_fv[1].start(); sp["d"].steps[0].start()
        @pl.when(diag)
        def _():
            core_tok[k].wait_recv()
        project((1-x)*NC+k)
    @pl.when(off)
    def _():
        swap_fv[2].start(); swap_fv[3].start()
    for c in outs: c.start()
    plan={}
    todo=lambda slot,act: plan.setdefault(slot,[]).append(act)
    for level in range(1,nl): todo(4*(level-1),functools.partial(advance,"u",level))
    for level in range(nl): todo(3+4*level if level<2 else 10,functools.partial(advance,"d",level))
    todo(4,swap_og[0].start); todo(7,swap_og[1].start)
    todo(12,lambda:(swap_og[0].wait_recv(),core_og[0].start()))
    BQ,BK=512,512
    laneq=lax.broadcasted_iota(jnp.int32,(BQ,128),1)
    lane=lax.broadcasted_iota(jnp.int32,(SLOT,128),1)
    row=lax.broadcasted_iota(jnp.int32,(SLOT,128),0)
    def pair(p,_):
        for at in range(NP):
            @pl.when((p==at)&off)
            def _(): swap_fv[at].wait_recv()
            @pl.when((p==at)&diag)
            def _(): own_fv[at].wait()
        m=(0.5*vp[p]+0.5*fv_v[p].astype(jnp.float32)).astype(jnp.bfloat16)
        ms[p]=m
        k=ks[p]
        length=len_v[0:1,:]
        for h in range(2):
            own=(lane//64)==h
            first=lane==(64*(1-h))
            bias=jnp.where(first&(row>=length),-1e30,0.0).astype(jnp.bfloat16)
            kb_ref[h]=jnp.where(own,k,bias)
            kb_ref[2+h]=jnp.where(own,m,jnp.ones_like(m))
        for i in range(SLOT//BQ):
            for at in range(NP):
                acts=plan.get(at*4+i)
                if acts:
                    @pl.when((p==at)&off)
                    def _():
                        for a in acts: a()
            rows=slice(i*BQ,(i+1)*BQ)
            q=qs[p,rows,:]
            got=[]
            for h in range(2):
                own=(laneq//64)==h
                qh=jnp.where(own,q,jnp.ones_like(q))
                mx=None
                for j in range(i+1):
                    s=dot(qh,kb_ref[h,pl.ds(j*BK,BK),:],NT)
                    if j==i:
                        r=lax.broadcasted_iota(jnp.int32,(BQ,BK),0); c=lax.broadcasted_iota(jnp.int32,(BQ,BK),1)
                        s=jnp.where(c<=r,s,-1e30)
                    s_ref[h,:,pl.ds(j*BK,BK)]=s
                    m_=jnp.max(s,axis=-1,keepdims=True)
                    mx=m_ if mx is None else jnp.maximum(mx,m_)
                mc=mx*C2
                acc=None
                for j in range(i+1):
                    pr=jnp.exp2(s_ref[h,:,pl.ds(j*BK,BK)]*C2-mc).astype(jnp.bfloat16)
                    a=dot(pr,kb_ref[2+h,pl.ds(j*BK,BK),:])
                    acc=a if acc is None else acc+a
                other=64*(1-h)
                l=acc[:,other:other+1]
                got.append((acc/l,mc+jnp.log2(l)))
            att_v[rows,pl.ds(pl.multiple_of(p*128,128),128)]=jnp.where((laneq//64)==0,got[0][0],got[1][0]).astype(jnp.bfloat16)
            lse_v[p,:,i*BQ:(i+1)*BQ]=jnp.where(lax.broadcasted_iota(jnp.int32,(BQ,128),1)==0,got[0][1],got[1][1]).T[0:8]
        return 0
    lax.fori_loop(0,NP,pair,0)
    @pl.when(off)
    def _():
        sp["o"].steps[nl].wait_recv()
        swap_og[1].wait_recv(); core_og[1].start()
    @pl.when(diag)
    def _():
        own_o.wait(); own_og[1].wait()
    for c in outs2: c.start()
    for r in range(SLOT//PR):
        pa_v[r*PR:(r+1)*PR,:]=dot(att_v[r*PR:(r+1)*PR,:],wo_v[...]).astype(jnp.bfloat16)
        core_pa[r].start(); out_pa[r].start()
    for c in outs+outs2+out_pa: c.wait()
    for c in core_pa: c.wait()
    for k in range(NC): core_tok[k].wait_send()
    @pl.when(diag)
    def _():
        for c in core_og_own: c.wait_send()
        for c in core_og: c.wait_recv()
    @pl.when(off)
    def _():
        for c in core_og: c.wait_send()
        for c in core_og_own: c.wait_recv()
        for n in "gud": sp[n].steps[nl].wait_recv()
        for n in "qkvogud":
            for s in sp[n].steps: s.wait_send()
        swap_len.wait_send()
        for c in swap_tok+swap_fv+swap_og: c.wait_send()

def front(groups,tok,fv,og,length,gain,tables,ws):
    N=SLOT; D=tok.shape[1]; W=ws[0].shape[1]; NP=W//128; FH=ws[4].shape[1]
    bf=jnp.bfloat16; f32=jnp.float32
    S=jax.ShapeDtypeStruct
    outs=[S((N,D),bf),S((N,D),bf),S((8,128),jnp.int32),S((NP,N,128),bf),S((NP,N,128),bf),S((NP,N,128),bf),S((N,W),bf),S((NP,8,N),f32),S((N,D),bf),S((N,D),bf)]+[S(w.shape,bf) for w in ws]
    anyb=pl.BlockSpec(memory_space=pl.ANY); vm=pl.BlockSpec(memory_space=pltpu.VMEM)
    V=pltpu.VMEM
    scratch=[V((N,D),bf),V((8,128),jnp.int32),V((NP,N,128),bf),V((D,W),bf),V((D,W),bf),V((D,W),bf),V((W,D),bf),V((N,128),f32),V((N,128),f32),
        V((NP,N,128),bf),V((NP,N,128),bf),V((NP,N,128),f32),V((NP,N,128),bf),V((4,N,128),bf),V((2,512,N),f32),V((N,W),bf),V((NP,8,N),f32),V((N,D),bf),
        pltpu.SemaphoreType.DMA((56,)),pltpu.SemaphoreType.DMA((56,)),pltpu.SemaphoreType.DMA((32,))]
    return pl.pallas_call(functools.partial(front_kernel,groups),out_shape=outs,
        in_specs=[anyb]*4+[vm]*5+[anyb]*7,out_specs=[anyb]*len(outs),scratch_shapes=scratch,
        compiler_params=pltpu.CompilerParams(collective_id=0,has_side_effects=True,vmem_limit_bytes=58<<20),name="front")(tok,fv,og,length,gain,*tables,*ws)
def exchange(v,perm): return lax.ppermute(v,ALL,perm)
def halve(buf,perm,bit):
    half=buf.shape[0]//2
    keep=lax.dynamic_slice_in_dim(buf,bit*half,half,0)
    send=lax.dynamic_slice_in_dim(buf,(1-bit)*half,half,0)
    got=exchange(send,perm)
    return (keep.astype(jnp.float32)+got.astype(jnp.float32)).astype(jnp.bfloat16)

def per_device(groups,tokens,first_values,out_grad,lengths,gain_attn,gain_mlp,w_query,w_key,w_value,w_out,w_gate,w_up,w_down):
    bf=jnp.bfloat16; f32=jnp.float32
    n=groups
    lin=lambda i,c,x:(i*2+c)*2+x
    each=lambda fn:[(lin(i,c,x),lin(*fn(i,c,x))) for i in range(n) for c in range(2) for x in range(2)]
    swap=each(lambda i,c,x:(i,x,c))
    swap_some=[p for p in swap if p[0]!=p[1]]
    over_core=each(lambda i,c,x:(i,1-c,x))
    over_x=each(lambda i,c,x:(i,c,1-x))
    zy=lax.axis_index("zy"); core=lax.axis_index("core"); x_at=lax.axis_index("head")
    half=tokens.shape[0]
    D=tokens.shape[1]
    def mine_of(v): return lax.dynamic_slice_in_dim(v,core*half,half,0)
    def other_of(v): return lax.dynamic_slice_in_dim(v,(1-core)*half,half,0)
    def home(v):
        return jnp.where(core==x_at,v,exchange(v,swap_some))
    g1=gain_attn.reshape(1,D); g2=gain_mlp.reshape(1,D)
    lanes=jnp.arange(128)%(HEAD_DIM//2)
    frequency=jnp.exp(lanes.astype(f32)*(-2.0*math.log(10000.0)/HEAD_DIM))
    coarse=(jnp.arange(SLOT//32)*32).astype(f32)[:,None]*frequency[None,:]
    fine=jnp.arange(32).astype(f32)[:,None]*frequency[None,:]
    tables=(jnp.cos(coarse),jnp.sin(coarse),jnp.cos(fine),jnp.sin(fine))
    length8=jnp.broadcast_to(lengths.reshape(1,1),(8,128))
    (tok,og,len_full,q,k,mixed,att,lse,pa,pb,w_q,w_k,w_v,w_o,w_g,w_u,w_d)=front(n,tokens,first_values,out_grad,length8,g1,tables,(w_query,w_key,w_value,w_out,w_gate,w_up,w_down))
    length=len_full[0,:1]
    tok_half=mine_of(tok)
    angles=jnp.arange(SLOT).astype(f32)[:,None]*frequency[None,:]
    cos=jnp.cos(angles); sin=jnp.sin(angles)*jnp.where((jnp.arange(128)%64)<32,-1.0,1.0)
    op,gh2a,comb=mlp(length,tok,pa,pb,og,g2,w_gate,w_up,w_down,w_g,w_u,w_d)
    op_recv=exchange(other_of(op),over_core)
    middle=tok_half.astype(f32)+(mine_of(pa).astype(f32)+mine_of(pb).astype(f32))
    out=(middle+(mine_of(op).astype(f32)+op_recv.astype(f32))).astype(bf)
    out=home(out)
    gh2b=exchange(gh2a,over_core)
    gm,gat,delta,gwo,gg2=mid(length,tok,pa,pb,og,gh2a,gh2b,att,g2,w_o,512)
    dq,dk,dv=att_bwd(length,q,k,mixed,gat,lse,delta,cos,sin)
    grad_first=home(dv)
    gh1,gwqkv=qkv_bwd(tok,dq,dk,dv,g1,w_q,w_k,w_v,512)
    gh1_recv=exchange(other_of(gh1),over_core)
    gh1_full=mine_of(gh1).astype(f32)+gh1_recv.astype(f32)
    xt=tok_half.astype(f32)
    r1=lax.rsqrt(jnp.mean(xt*xt,axis=-1,keepdims=True)+EPS)
    n1=xt*r1
    gn=gh1_full*g1
    gt=mine_of(gm).astype(f32)+r1*(gn-n1*jnp.mean(gn*n1,axis=-1,keepdims=True))
    grad_tokens=home(gt.astype(bf))
    gg1=jnp.sum(gh1_full*n1,axis=0)
    gains=lax.psum(jnp.stack([gg1,0.5*jnp.sum(gg2,axis=0)]),ALL)
    bits=[]
    b=1
    while b<n:
        bits.append((each(lambda i,c,x,b=b:(i^b,c,x)),(zy//b)%2,b)); b*=2
    def reduce_all(buf):
        buf=halve(buf,over_x,x_at)
        for perm,bit,_ in bits: buf=halve(buf,perm,bit)
        piece=home(buf)
        got=lax.all_gather(piece,"zy",axis=0,tiled=False)
        order=[int(format(i,"0%db"%len(bits))[::-1],2) for i in range(n)]
        got=jnp.concatenate([got[o] for o in order],0)
        other=exchange(got,over_core)
        return jnp.where(core==0,jnp.concatenate([got,other],0),jnp.concatenate([other,got],0))
    FH=w_gate.shape[1]; W=w_query.shape[1]
    cut=(2*FH//128)*D
    cs=reduce_all(comb)
    os=reduce_all(jnp.concatenate([gwo,gwqkv],0))
    gwg=unpack(cs,0,D,FH); gwu=unpack(cs,cut//2,D,FH); gwd=unpack(cs[cut:],0,FH,D)
    rest=os.shape[0]-gwqkv.shape[0]
    gwo_=unpack(os,0,W,D)
    gq,gk,gv=[unpack(os,rest+j*(W//128)*D,D,W) for j in range(3)]
    return (out,grad_tokens,grad_first,gains[0],gains[1],gq,gk,gv,gwo_,gwg,gwu,gwd)

def solution(mesh):
    fine=Mesh(mesh.devices.reshape(-1,2,2),ALL)
    rows=P(ALL,None); slot=P(("zy","core"),"head"); col=P(None,"head"); row=P("head",None)
    return jax.shard_map(functools.partial(per_device,fine.devices.shape[0]),mesh=fine,
        in_specs=(rows,slot,rows,P(("zy","core")),P(),P(),col,col,col,row,col,col,row),
        out_specs=(rows,rows,slot,P(),P(),col,col,col,row,col,col,row),check_vma=False)
```

```python
import functools, math
import jax, jax.numpy as jnp
from jax import lax
from jax.experimental import pallas as pl
from jax.experimental.pallas import tpu as pltpu
from jax.sharding import Mesh, PartitionSpec as P
SLOT=2048; HEAD_DIM=64
C2=math.log2(math.e)/8.0
NT=(((1,),(1,)),((),()))
TN=(((0,),(0,)),((),()))
NN=(((1,),(0,)),((),()))
def dot(a,b,dims=NN): return lax.dot_general(a,b,dims,preferred_element_type=jnp.float32)

EPS=1e-5
R2=256
def norm_block(x,gain):
    r=lax.rsqrt(jnp.mean(x*x,axis=-1,keepdims=True)+EPS)
    n=x*r
    return n,r
def rot(x,cos,sin,lane_first):
    up=pltpu.roll(x,96,1)
    dn=pltpu.roll(x,32,1)
    return x*cos+jnp.where(lane_first,up,dn)*sin

def mlp_kernel(R,NS,FH,len_ref,t_ref,pa_ref,pb_ref,og_ref,g_ref,wg_h,wu_h,wd_h,wg_f,wu_f,wd_f,
               op_ref,gh_ref,comb_h,
               wgu,wd,agu,ad,stage,wsem,ssem):
    step=pl.program_id(0)
    D=t_ref.shape[1]
    diag=lax.axis_index("core")==lax.axis_index("head")
    load=lambda a,b,c:[pltpu.make_async_copy(a,wgu.at[:,pl.ds(0,FH)],wsem.at[0]),
         pltpu.make_async_copy(b,wgu.at[:,pl.ds(FH,FH)],wsem.at[1]),
         pltpu.make_async_copy(c,wd,wsem.at[2])]
    cps=load(wg_h,wu_h,wd_h); far=load(wg_f,wu_f,wd_f)
    @pl.when(step==0)
    def _():
        @pl.when(diag)
        def _():
            for c in cps: c.start()
        @pl.when(jnp.logical_not(diag))
        def _():
            for c in far: c.start()
        agu[...]=jnp.zeros_like(agu)
        ad[...]=jnp.zeros_like(ad)
        for c in cps: c.wait()
    x=t_ref[...].astype(jnp.float32)+(pa_ref[...].astype(jnp.float32)+pb_ref[...].astype(jnp.float32))
    n,_=norm_block(x,None)
    h=(n*g_ref[...]).astype(jnp.bfloat16)
    row=lax.broadcasted_iota(jnp.int32,(R,1),0)+step*R
    g=jnp.where(row<len_ref[0],og_ref[...],jnp.zeros((),jnp.bfloat16))
    gu=dot(h,wgu[...])
    gate=gu[:,:FH]; up=gu[:,FH:]
    gh=dot(g,wd[...],NT)
    sg=0.5*jnp.tanh(0.5*gate)+0.5
    silu=gate*sg
    hid=(silu*up).astype(jnp.bfloat16)
    gu_=(gh*silu).astype(jnp.bfloat16)
    gg_=(gh*up*(sg*(1.0+gate*(1.0-sg)))).astype(jnp.bfloat16)
    op_ref[...]=dot(hid,wd[...]).astype(jnp.bfloat16)
    gh_ref[...]=(dot(gg_,wgu[:,:FH],NT)+dot(gu_,wgu[:,FH:],NT)).astype(jnp.bfloat16)
    ad[...]+=dot(hid,g,TN)
    agu[:,:FH]+=dot(h,gg_,TN)
    agu[:,FH:]+=dot(h,gu_,TN)
    @pl.when(step==NS-1)
    def _():
        tiles=[(agu,c,c*D,D) for c in range(2*FH//128)]+[(ad,c,(2*FH//128)*D+c*FH,FH) for c in range(D//128)]
        pend=[None]*4
        for i,(a,c,off,ln) in enumerate(tiles):
            s=i%4
            if pend[s] is not None: pend[s].wait()
            stage[s,0:ln,:]=a[:,c*128:(c+1)*128].astype(jnp.bfloat16)
            cp=pltpu.make_async_copy(stage.at[s,pl.ds(0,ln)],comb_h.at[pl.ds(off,ln)],ssem.at[s])
            cp.start(); pend[s]=cp
        for p in pend: p.wait()
def mlp(length,t,pa,pb,og,gain,wg,wu,wd,wg_f,wu_f,wd_f,R=256):
    N,D=t.shape; FH=wg.shape[1]; NS=N//R
    rb=pl.BlockSpec((R,D),lambda i:(i,0))
    anyb=pl.BlockSpec(memory_space=pl.ANY)
    full=lambda a:pl.BlockSpec(a.shape,lambda i:(0,0),pipeline_mode=pl.Buffered(1))
    rows=(2*FH//128)*D+(D//128)*FH
    return pl.pallas_call(functools.partial(mlp_kernel,R,NS,FH),grid=(NS,),
        in_specs=[pl.BlockSpec(memory_space=pltpu.SMEM),rb,rb,rb,rb,full(gain)]+[anyb]*6,
        out_specs=[rb,rb,anyb],
        out_shape=[jax.ShapeDtypeStruct((N,D),jnp.bfloat16)]*2+[jax.ShapeDtypeStruct((rows,128),jnp.bfloat16)],
        scratch_shapes=[pltpu.VMEM((D,2*FH),jnp.bfloat16),pltpu.VMEM((FH,D),jnp.bfloat16),pltpu.VMEM((D,2*FH),jnp.float32),pltpu.VMEM((FH,D),jnp.float32),
            pltpu.VMEM((4,max(D,FH),128),jnp.bfloat16),pltpu.SemaphoreType.DMA((3,)),pltpu.SemaphoreType.DMA((4,))],
        compiler_params=pltpu.CompilerParams(vmem_limit_bytes=60<<20),name="mlp_%d"%R)(length,t,pa,pb,og,gain,wg,wu,wd,wg_f,wu_f,wd_f)


ALL=("zy","core","head")

class Links:
    def __init__(self,send,recv,local):
        self.send,self.recv,self.local=send,recv,local
        self.remote_count=0; self.local_count=0
    def remote(self,src,dst,device):
        at=self.remote_count; self.remote_count+=1
        return pltpu.make_async_remote_copy(src_ref=src,dst_ref=dst,send_sem=self.send.at[at],recv_sem=self.recv.at[at],
            device_id=device,device_id_type=pl.DeviceIdType.MESH)
    def copy(self,src,dst):
        at=self.local_count; self.local_count+=1
        return pltpu.make_async_copy(src,dst,self.local.at[at])

def spread_bits(groups):
    count=min(groups,8); bits=[]
    while count>1:
        count//=2; bits.append(count)
    return bits

class Spread:
    def __init__(self,links,home,full,bits,zy,swap_dev,peer):
        m=2**len(bits); rows=home.shape[0]//m
        place=0
        for level,b in enumerate(bits): place=place+((zy//b)%2)*(2**level)
        one=pl.ds(pl.multiple_of(place*rows,rows),rows)
        self.steps=[links.remote(home.at[one],full.at[one],swap_dev)]
        for level,b in enumerate(bits):
            size=2**level
            block=pl.ds(pl.multiple_of((place//size)*size*rows,size*rows),size*rows)
            self.steps.append(links.remote(full.at[block],full.at[block],peer(b)))

def front_kernel(groups,
        tok_h,fv_h,og_h,len_h,g_ref,ch_ref,sh_ref,cl_ref,sl_ref,wq_h,wk_h,wv_h,wo_h,wg_h,wu_h,wd_h,
        tok_o,og_o,len_o,q_o,k_o,m_o,att_o,lse_o,pa_o,pb_o,wq_o,wk_o,wv_o,wo_o,wg_o,wu_o,wd_o,
        tok_v,len_v,fv_v,wq_v,wk_v,wv_v,wo_v,cos_v,sin_v,qs,ks,vp,ms,kb_ref,s_ref,att_v,lse_v,pa_v,
        send_sem,recv_sem,local_sem):
    zy=lax.axis_index("zy"); core=lax.axis_index("core"); x=lax.axis_index("head")
    off=core!=x; diag=core==x
    L=Links(send_sem,recv_sem,local_sem)
    swap_dev=(zy,1-core,1-x); core_dev=(zy,1-core,x)
    bits=spread_bits(groups)
    peer=lambda b:(zy+b-2*b*((zy//b)%2),core,x)
    barrier=pltpu.get_barrier_semaphore()
    MESH=pl.DeviceIdType.MESH
    half=tok_h.shape[0]; D=tok_h.shape[1]; W=wq_h.shape[1]; NP=W//128
    CH=256; NC=half//CH
    sp={n:Spread(L,h,f,bits,zy,swap_dev,peer) for n,h,f in (("q",wq_h,wq_v),("k",wk_h,wk_v),("v",wv_h,wv_v),("o",wo_h,wo_v),("g",wg_h,wg_o),("u",wu_h,wu_o),("d",wd_h,wd_o))}
    mine=lambda k:pl.ds(pl.multiple_of(core*half+k*CH,CH),CH)
    swap_len=L.remote(len_h,len_v,swap_dev)
    there=lambda k:pl.ds(pl.multiple_of((1-core)*half+k*CH,CH),CH)
    swap_tok=[L.remote(tok_h.at[pl.ds(k*CH,CH)],tok_v.at[there(k)],swap_dev) for k in range(NC)]
    core_tok=[L.remote(tok_v.at[mine(k)],tok_v.at[mine(k)],core_dev) for k in range(NC)]
    swap_fv=[L.remote(fv_h.at[:,pl.ds(p*128,128)],fv_v.at[p],swap_dev) for p in range(NP)]
    HH=half//2
    part=lambda c,j:pl.ds(pl.multiple_of(c*half+j*HH,HH),HH)
    swap_og=[L.remote(og_h.at[pl.ds(j*HH,HH)],og_o.at[part(1-core,j)],swap_dev) for j in range(2)]
    my_half=pl.ds(pl.multiple_of(core*half,half),half)
    core_og=[L.remote(og_o.at[part(core,j)],og_o.at[part(core,j)],core_dev) for j in range(2)]
    PR=512
    core_pa=[L.remote(pa_v.at[pl.ds(r*PR,PR)],pb_o.at[pl.ds(r*PR,PR)],core_dev) for r in range(SLOT//PR)]
    out_pa=[L.copy(pa_v.at[pl.ds(r*PR,PR)],pa_o.at[pl.ds(r*PR,PR)]) for r in range(SLOT//PR)]
    own_tok=L.copy(tok_h,tok_v.at[my_half])
    own_len=L.copy(len_h,len_v)
    own_fv=[L.copy(fv_h.at[:,pl.ds(p*128,128)],fv_v.at[p]) for p in range(NP)]
    own_og=[L.copy(og_h,pa_v.at[pl.ds(0,half)]),L.copy(pa_v.at[pl.ds(0,half)],og_o.at[my_half])]
    core_og_own=[L.remote(og_h.at[pl.ds(j*HH,HH)],og_o.at[part(core,j)],core_dev) for j in range(2)]
    own_qkv=[L.copy(h,v) for h,v in ((wq_h,wq_v),(wk_h,wk_v),(wv_h,wv_v))]
    own_o=L.copy(wo_h,wo_v)
    outs=[L.copy(a,b) for a,b in ((tok_v,tok_o),(len_v,len_o),(qs,q_o),(ks,k_o),(wq_v,wq_o),(wk_v,wk_o),(wv_v,wv_o))]
    outs2=[L.copy(a,b) for a,b in ((ms,m_o),(att_v,att_o),(lse_v,lse_o),(wo_v,wo_o))]

    pl.semaphore_signal(barrier,inc=1,device_id=core_dev,device_id_type=MESH)
    @pl.when(off)
    def _():
        pl.semaphore_signal(barrier,inc=1,device_id=swap_dev,device_id_type=MESH)
        for b in bits: pl.semaphore_signal(barrier,inc=1,device_id=peer(b),device_id_type=MESH)
        pl.semaphore_wait(barrier,2+len(bits))
        for n in "qkvog": sp[n].steps[0].start()
        swap_len.start()
    @pl.when(diag)
    def _():
        pl.semaphore_wait(barrier,1)
        own_tok.start(); own_len.start()
        for c in own_qkv: c.start()
        own_tok.wait()
        for k in range(NC): core_tok[k].start()
        own_len.wait()
        for c in own_fv: c.start()
        own_o.start(); own_og[0].start()
        for c in core_og_own: c.start()
    sign=jnp.where((lax.broadcasted_iota(jnp.int32,(1,128),1)%64)<32,-1.0,1.0)
    cl=cl_ref[...]; sl=sl_ref[...]
    def table(a,_):
        rows=pl.ds(pl.multiple_of(a*32,32),32)
        ch=ch_ref[pl.ds(a,1),:]; sh=sh_ref[pl.ds(a,1),:]
        cos_v[rows,:]=ch*cl-sh*sl
        sin_v[rows,:]=(sh*cl+ch*sl)*sign
        return 0
    lax.fori_loop(0,SLOT//32,table,0)
    nl=len(bits)
    def advance(n,level):
        sp[n].steps[level].wait_recv(); sp[n].steps[level+1].start()
    @pl.when(off)
    def _():
        for level in range(nl):
            for n in ("qkvog" if level<max(nl-1,1) else "qkv"): advance(n,level)
            if level==0:
                for k in range(NC): swap_tok[k].start()
        swap_len.wait_recv()
    @pl.when(diag)
    def _():
        for c in own_qkv: c.wait()
        own_og[0].wait(); own_og[1].start()
    gain=g_ref[...]
    lf=(lax.broadcasted_iota(jnp.int32,(CH,128),1)%64)<32
    def project(block):
        rows=pl.ds(pl.multiple_of(block*CH,CH),CH)
        t=tok_v[rows,:].astype(jnp.float32)
        n,_=norm_block(t,None)
        h=(n*gain).astype(jnp.bfloat16)
        cos=cos_v[rows,:]; sin=sin_v[rows,:]
        for w,o in ((wq_v,qs),(wk_v,ks)):
            y=dot(h,w[...])
            for c in range(NP):
                o[c,rows,:]=rot(y[:,c*128:(c+1)*128],cos,sin,lf).astype(jnp.bfloat16)
        y=dot(h,wv_v[...])
        for c in range(NP): vp[c,rows,:]=y[:,c*128:(c+1)*128]
    for k in range(NC):
        if k==0:
            @pl.when(off)
            def _():
                for n in "qkv": sp[n].steps[nl].wait_recv()
        @pl.when(off)
        def _():
            core_tok[k].wait_recv()
        project(x*NC+k)
        @pl.when(off)
        def _():
            if k==0: sp["u"].steps[0].start(); swap_fv[0].start()
            if k==1 and nl>1: advance("o",nl-1)
            if k==2 and nl>1: advance("g",nl-1)
            if k==3: advance("u",0)
    for k in range(NC):
        @pl.when(off)
        def _():
            swap_tok[k].wait_recv()
            core_tok[k].start()
            if k==1: swap_fv[1].start(); sp["d"].steps[0].start()
        @pl.when(diag)
        def _():
            core_tok[k].wait_recv()
        project((1-x)*NC+k)
    @pl.when(off)
    def _():
        swap_fv[2].start(); swap_fv[3].start()
    for c in outs: c.start()
    plan={}
    todo=lambda slot,act: plan.setdefault(slot,[]).append(act)
    for level in range(1,nl): todo(4*(level-1),functools.partial(advance,"u",level))
    for level in range(nl): todo(3+4*level if level<2 else 10,functools.partial(advance,"d",level))
    todo(4,swap_og[0].start); todo(7,swap_og[1].start)
    todo(12,lambda:(swap_og[0].wait_recv(),core_og[0].start()))
    BQ,BK=512,512
    laneq=lax.broadcasted_iota(jnp.int32,(BQ,128),1)
    lane=lax.broadcasted_iota(jnp.int32,(SLOT,128),1)
    row=lax.broadcasted_iota(jnp.int32,(SLOT,128),0)
    def pair(p,_):
        for at in range(NP):
            @pl.when((p==at)&off)
            def _(): swap_fv[at].wait_recv()
            @pl.when((p==at)&diag)
            def _(): own_fv[at].wait()
        m=(0.5*vp[p]+0.5*fv_v[p].astype(jnp.float32)).astype(jnp.bfloat16)
        ms[p]=m
        k=ks[p]
        length=len_v[0:1,:]
        for h in range(2):
            own=(lane//64)==h
            first=lane==(64*(1-h))
            bias=jnp.where(first&(row>=length),-1e30,0.0).astype(jnp.bfloat16)
            kb_ref[h]=jnp.where(own,k,bias)
            kb_ref[2+h]=jnp.where(own,m,jnp.ones_like(m))
        for i in range(SLOT//BQ):
            for at in range(NP):
                acts=plan.get(at*4+i)
                if acts:
                    @pl.when((p==at)&off)
                    def _():
                        for a in acts: a()
            rows=slice(i*BQ,(i+1)*BQ)
            q=qs[p,rows,:]
            got=[]
            for h in range(2):
                own=(laneq//64)==h
                qh=jnp.where(own,q,jnp.ones_like(q))
                mx=None
                for j in range(i+1):
                    s=dot(qh,kb_ref[h,pl.ds(j*BK,BK),:],NT)
                    if j==i:
                        r=lax.broadcasted_iota(jnp.int32,(BQ,BK),0); c=lax.broadcasted_iota(jnp.int32,(BQ,BK),1)
                        s=jnp.where(c<=r,s,-1e30)
                    s_ref[h,:,pl.ds(j*BK,BK)]=s
                    m_=jnp.max(s,axis=-1,keepdims=True)
                    mx=m_ if mx is None else jnp.maximum(mx,m_)
                mc=mx*C2
                acc=None
                for j in range(i+1):
                    pr=jnp.exp2(s_ref[h,:,pl.ds(j*BK,BK)]*C2-mc).astype(jnp.bfloat16)
                    a=dot(pr,kb_ref[2+h,pl.ds(j*BK,BK),:])
                    acc=a if acc is None else acc+a
                other=64*(1-h)
                l=acc[:,other:other+1]
                got.append((acc/l,mc+jnp.log2(l)))
            att_v[rows,pl.ds(pl.multiple_of(p*128,128),128)]=jnp.where((laneq//64)==0,got[0][0],got[1][0]).astype(jnp.bfloat16)
            lse_v[p,:,i*BQ:(i+1)*BQ]=jnp.where(lax.broadcasted_iota(jnp.int32,(BQ,128),1)==0,got[0][1],got[1][1]).T[0:8]
        return 0
    lax.fori_loop(0,NP,pair,0)
    @pl.when(off)
    def _():
        sp["o"].steps[nl].wait_recv()
        swap_og[1].wait_recv(); core_og[1].start()
    @pl.when(diag)
    def _():
        own_o.wait(); own_og[1].wait()
    for c in outs2: c.start()
    for r in range(SLOT//PR):
        pa_v[r*PR:(r+1)*PR,:]=dot(att_v[r*PR:(r+1)*PR,:],wo_v[...]).astype(jnp.bfloat16)
        core_pa[r].start(); out_pa[r].start()
    for c in outs+outs2+out_pa: c.wait()
    for c in core_pa: c.wait()
    for k in range(NC): core_tok[k].wait_send()
    @pl.when(diag)
    def _():
        for c in core_og_own: c.wait_send()
        for c in core_og: c.wait_recv()
    @pl.when(off)
    def _():
        for c in core_og: c.wait_send()
        for c in core_og_own: c.wait_recv()
        for n in "gud": sp[n].steps[nl].wait_recv()
        for n in "qkvogud":
            for s in sp[n].steps: s.wait_send()
        swap_len.wait_send()
        for c in swap_tok+swap_fv+swap_og: c.wait_send()

def front(groups,tok,fv,og,length,gain,tables,ws):
    N=SLOT; D=tok.shape[1]; W=ws[0].shape[1]; NP=W//128; FH=ws[4].shape[1]
    bf=jnp.bfloat16; f32=jnp.float32
    S=jax.ShapeDtypeStruct
    outs=[S((N,D),bf),S((N,D),bf),S((8,128),jnp.int32),S((NP,N,128),bf),S((NP,N,128),bf),S((NP,N,128),bf),S((N,W),bf),S((NP,8,N),f32),S((N,D),bf),S((N,D),bf)]+[S(w.shape,bf) for w in ws]
    anyb=pl.BlockSpec(memory_space=pl.ANY); vm=pl.BlockSpec(memory_space=pltpu.VMEM)
    V=pltpu.VMEM
    scratch=[V((N,D),bf),V((8,128),jnp.int32),V((NP,N,128),bf),V((D,W),bf),V((D,W),bf),V((D,W),bf),V((W,D),bf),V((N,128),f32),V((N,128),f32),
        V((NP,N,128),bf),V((NP,N,128),bf),V((NP,N,128),f32),V((NP,N,128),bf),V((4,N,128),bf),V((2,512,N),f32),V((N,W),bf),V((NP,8,N),f32),V((N,D),bf),
        pltpu.SemaphoreType.DMA((56,)),pltpu.SemaphoreType.DMA((56,)),pltpu.SemaphoreType.DMA((32,))]
    return pl.pallas_call(functools.partial(front_kernel,groups),out_shape=outs,
        in_specs=[anyb]*4+[vm]*5+[anyb]*7,out_specs=[anyb]*len(outs),scratch_shapes=scratch,
        compiler_params=pltpu.CompilerParams(collective_id=0,has_side_effects=True,vmem_limit_bytes=58<<20),name="front")(tok,fv,og,length,gain,*tables,*ws)

class Reduce:
    def __init__(self,links,order,src,offset,rows,recv,recv_at,result,result_at,at,landing=None,held=None):
        self.links=links; self.order=order; self.rows=rows; self.src=src; self.offset=offset; self.at=at
        self.levels=len(order); self.bufs=[]; self.sends=[]
        for level in range(self.levels):
            size=rows>>(level+1)
            if level==0 and held is not None: self.bufs.append(held)
            else: self.bufs.append(recv.at[pl.ds(recv_at,size)]); recv_at+=size
        self.landing=landing; self.sent1=False
        self.recv_end=recv_at
        half=rows//2
        for level,name in enumerate(order):
            size=rows>>(level+1)
            bit=at.bit(name)
            if level==0:
                source=src.at[pl.ds(pl.multiple_of(offset+(1-bit)*half,16),half)]
            else:
                source=self.bufs[level-1].at[pl.ds(pl.multiple_of((1-bit)*size,16),size)]
            self.sends.append(links.remote(source,landing if level==0 and landing is not None else self.bufs[level],at.partner(name)))
        self.result=result; self.result_at=result_at
        leaf=rows>>self.levels; self.leaf=leaf
        weight={name:rows>>(i+1) for i,name in enumerate(order)}
        own=sum(at.bit(name)*weight[name] for name in order)
        spot=result.at[pl.ds(pl.multiple_of(result_at+own,16),leaf)]
        self.swap=links.remote(self.bufs[-1],spot,at.swap)
        self.keep=links.copy(self.bufs[-1],spot)
        self.gathers=[]; gathered=[]
        for name in sorted([n for n in order if n!="x"],reverse=True)+["x"]:
            unit=leaf; apart=[]
            for w in sorted(gathered):
                if w==unit: unit*=2
                else: apart.append(w)
            base=sum((at.core if n=="x" else at.bit(n))*weight[n] for n in order if weight[n] not in gathered)
            combos=[0]
            for w in apart: combos=combos+[c+w for c in combos]
            device=at.core_dev if name=="x" else at.partner(name)
            step=[]
            for c in combos:
                block=result.at[pl.ds(pl.multiple_of(result_at+base+c,16),unit)]
                step.append(links.remote(block,block,device))
            self.gathers.append(step); gathered.append(weight[name])
    def start(self): self.sends[0].start()
    def finish(self,level,got=None):
        if got is None: self.sends[level].wait_recv()
        size=self.rows>>(level+1)
        bit=self.at.bit(self.order[level])
        into=self.bufs[level]
        if level==0:
            mine=got if got is not None else self.src.at[pl.ds(pl.multiple_of(self.offset+bit*size,16),size)]
        else:
            mine=self.bufs[level-1].at[pl.ds(pl.multiple_of(bit*size,16),size)]
        step=math.gcd(size,512)
        def add(i,_):
            rows=pl.ds(pl.multiple_of(i*step,step),step)
            into[rows,:]=(into[rows,:].astype(jnp.float32)+mine[rows,:].astype(jnp.float32)).astype(jnp.bfloat16)
            return 0
        lax.fori_loop(0,size//step,add,0)
        if level+1<self.levels: self.sends[level+1].start()
        else:
            @pl.when(self.at.off)
            def _(): self.swap.start()
            @pl.when(self.at.diag)
            def _(): self.keep.start()
    def gather(self,step):
        if step==0:
            @pl.when(self.at.off)
            def _(): self.swap.wait_recv()
            @pl.when(self.at.diag)
            def _(): self.keep.wait()
        else:
            for c in self.gathers[step-1]: c.wait_recv()
        for c in self.gathers[step]: c.start()
    def drain(self):
        for c in self.gathers[-1]: c.wait_recv()
        for i,c in enumerate(self.sends):
            if not (i==1 and self.sent1): c.wait_send()
        @pl.when(self.at.off)
        def _(): self.swap.wait_send()
        for s in self.gathers:
            for c in s: c.wait_send()

class Place: pass
def place_of(groups):
    at=Place()
    at.zy=lax.axis_index("zy"); at.core=lax.axis_index("core"); at.x=lax.axis_index("head")
    at.off=at.core!=at.x; at.diag=at.core==at.x
    at.bit=lambda name: at.x if name=="x" else (at.zy//name)%2
    at.partner=lambda name: (at.zy,at.core,1-at.x) if name=="x" else (at.zy+name-2*name*((at.zy//name)%2),at.core,at.x)
    at.swap=(at.zy,1-at.core,1-at.x); at.core_dev=(at.zy,1-at.core,at.x)
    at.bits=[]
    b=1
    while b<groups: at.bits.append(b); b*=2
    return at

def back_kernel(groups,
        len_ref,tok_h,pa_h,pb_h,og_h,op_h,gh_h,att_h,comb_h,q_h,k_h,m_h,wq_h,wk_h,wv_h,wo_h,lse_ref,g1_ref,g2_ref,ch_ref,sh_ref,cl_ref,sl_ref,
        out_o,gt_o,gf_o,res_o,gains_o,land_o,
        tokb,pab,pbb,ogb,gab,atb,opb,oprv,ghb,h1_v,gm_v,gat_v,dl_v,qd,kd,md,ks,qs,vs,dqa,cos_v,sin_v,wo_v,acc,keep_v,got_v,recv_v,gwo_v,gw_v,gain_v,
        send_sem,recv_sem,local_sem,blk_sem,free_sem):
    at=place_of(groups); core=at.core; off=at.off; diag=at.diag
    L=Links(send_sem,recv_sem,local_sem)
    MESH=pl.DeviceIdType.MESH
    N,D=tok_h.shape; half=N//2; W=wo_h.shape[0]; NP=W//128; R=256; NB=N//R
    bits=at.bits
    order1=["x"]+bits; order2=bits[:1]+["x"]+bits[1:]; order3=bits[1:2]+bits[:1]+["x"]+bits[2:]
    total=comb_h.shape[0]; KB=1024; units=total//KB
    cut=[units//4,units//4,units//4,units-3*(units//4)]
    runs={}; pos=0; rp=0
    keep_slot={"A":0,"B":1,"E":0,"F":1}; follows={"E":"A","F":"B"}
    for name,c,order in (("A",cut[0],order1),("B",cut[3],order2),("E",cut[1],order1),("F",cut[2],order2)):
        runs[name]=Reduce(L,order,comb_h,pos,c*KB,recv_v,rp,res_o,pos,at,land_o.at[pl.ds(pos//2,c*KB//2)],keep_v.at[keep_slot[name],pl.ds(0,c*KB//2)]); rp=runs[name].recv_end; pos+=c*KB
    runs["C"]=Reduce(L,order3,gwo_v,0,gwo_v.shape[0],recv_v,rp,res_o,pos,at); rp=runs["C"].recv_end; pos+=gwo_v.shape[0]
    for p in range(NP):
        runs[p]=Reduce(L,order3,gw_v.at[p],0,gw_v.shape[1],recv_v,rp,res_o,pos,at); rp=runs[p].recv_end; pos+=gw_v.shape[1]
    def both_copies(name):
        r=runs[name]; h=r.rows//2
        mine=comb_h.at[pl.ds(pl.multiple_of(r.offset+at.bit(r.order[0])*h,16),h)]
        return (pltpu.make_async_copy(mine,r.bufs[0],blk_sem.at[16]),pltpu.make_async_copy(r.landing,got_v.at[pl.ds(0,h)],blk_sem.at[17]))
    def prep(name):
        if name in follows: runs[follows[name]].sends[1].wait_send(); runs[follows[name]].sent1=True
        runs[name].sends[0].wait_recv()
        for c in both_copies(name): c.start()
    def finish0(name):
        for c in both_copies(name): c.wait()
        runs[name].finish(0,got_v)
    first_rows=lambda b:pl.multiple_of(((core*(NB//2)+b)%NB)*R,R)
    blk=lambda b:pl.ds(first_rows(b),R)
    theirs=lambda b:pl.ds(pl.multiple_of((((1-core)*(NB//2)+b)%NB)*R,R),R)
    ex_gh=[L.remote(gh_h.at[theirs(b)],ghb.at[theirs(b)],at.core_dev) for b in range(NB)]
    ex_op=[L.remote(op_h.at[theirs(b)],oprv.at[pl.ds(b*R,R)],at.core_dev) for b in range(NB//2)]
    sw_out=[L.remote(opb.at[pl.ds(b*R,R)],out_o.at[pl.ds(b*R,R)],at.swap) for b in range(NB//2)]
    lo_out=[L.copy(opb.at[pl.ds(b*R,R)],out_o.at[pl.ds(b*R,R)]) for b in range(NB//2)]
    sw_gf=[L.remote(md.at[p],gf_o.at[:,pl.ds(p*128,128)],at.swap) for p in range(NP)]
    lo_gf=[L.copy(md.at[p],gf_o.at[:,pl.ds(p*128,128)]) for p in range(NP)]
    ex_g1=[L.remote(ghb.at[theirs(b)],oprv.at[pl.ds(b*R,R)],at.core_dev) for b in range(NB//2)]
    sw_gt=[L.remote(gm_v.at[pl.ds(b*R,R)],gt_o.at[pl.ds(b*R,R)],at.swap) for b in range(NB//2)]
    lo_gt=[L.copy(gm_v.at[pl.ds(b*R,R)],gt_o.at[pl.ds(b*R,R)]) for b in range(NB//2)]
    names=["c","x"]+bits
    ex_gain=[L.remote(gain_v.at[0] if i==0 else gain_v.at[2*i],gain_v.at[2*i+1],at.core_dev if n=="c" else at.partner(n)) for i,n in enumerate(names)]
    loads=[L.copy(a,b) for a,b in ((wo_h,wo_v),(q_h,qd),(k_h,kd),(m_h,md))]
    proj=[L.copy(w.at[pl.ds(i*256,256)],v.at[i//2,:,pl.ds((i%2)*W,W)]) for w,v in ((wq_h,pab),(wk_h,pbb),(wv_h,ogb)) for i in range(D//256)]
    barrier=pltpu.get_barrier_semaphore()
    for d in [at.core_dev]+[at.partner(n) for n in ["x"]+bits]:
        pl.semaphore_signal(barrier,inc=1,device_id=d,device_id_type=MESH)
    @pl.when(off)
    def _():
        pl.semaphore_signal(barrier,inc=1,device_id=at.swap,device_id_type=MESH)
        pl.semaphore_wait(barrier,3+len(bits))
    @pl.when(diag)
    def _(): pl.semaphore_wait(barrier,2+len(bits))
    for c in ex_gh[:2]: c.start()
    ex_op[0].start()
    for b in range(2,NB): ex_gh[b].start()
    for c in ex_op[1:]: c.start()
    runs["A"].start(); runs["B"].start()
    def block_loads(b):
        s=b%2
        pairs=[(tok_h,tokb),(pa_h,pab),(pb_h,pbb),(og_h,ogb),(gh_h,gab),(att_h,atb)]
        cps=[pltpu.make_async_copy(h.at[blk(b)],v.at[s],blk_sem.at[s*8+i]) for i,(h,v) in enumerate(pairs)]
        if b<NB//2: cps.append(pltpu.make_async_copy(op_h.at[blk(b)],opb.at[pl.ds(b*R,R)],blk_sem.at[s*8+6]))
        return cps
    for c in block_loads(0): c.start()
    for c in loads: c.start()
    sign=jnp.where((lax.broadcasted_iota(jnp.int32,(1,128),1)%64)<32,-1.0,1.0)
    cl=cl_ref[...]; sl=sl_ref[...]
    def table(a,_):
        rows=pl.ds(pl.multiple_of(a*32,32),32)
        ch=ch_ref[pl.ds(a,1),:]; sh=sh_ref[pl.ds(a,1),:]
        cos_v[rows,:]=ch*cl-sh*sl
        sin_v[rows,:]=(sh*cl+ch*sl)*sign
        return 0
    lax.fori_loop(0,N//32,table,0)
    g1=g1_ref[...]; g2=g2_ref[...]
    length=len_ref[0:1,0:1]
    hr=lax.broadcasted_iota(jnp.int32,(8*NP,W),0); ln=lax.broadcasted_iota(jnp.int32,(8*NP,W),1)
    ind=jnp.where(((ln//64)==((hr//8)*2+hr%8))&(hr%8<2),1.0,0.0).astype(jnp.bfloat16)
    loads[0].wait()
    gsum=None
    plan={}
    todo=lambda t,*acts: plan.setdefault(t,[]).extend(acts)
    for k,v in make_schedule(1+len(bits),NP).items():
        for name,what,*arg in v:
            if what=="start": todo(k,runs[name].start)
            elif what=="prep": todo(k,functools.partial(prep,name))
            elif what=="f": todo(k,functools.partial(finish0,name) if (arg[0]==0 and name in keep_slot) else functools.partial(runs[name].finish,arg[0]))
            elif what=="g": todo(k,functools.partial(runs[name].gather,arg[0]))
    for b in range(NB):
        for a in plan.get(("m",b),[]): a()
        if b+1<NB:
            for c in block_loads(b+1): c.start()
        for c in block_loads(b): c.wait()
        ex_gh[b].wait_recv()
        s=b%2; r0=first_rows(b)
        t=tokb[s].astype(jnp.float32)
        n1,_=norm_block(t,None)
        h1_v[blk(b),:]=(n1*g1).astype(jnp.bfloat16)
        mid=t+(pab[s].astype(jnp.float32)+pbb[s].astype(jnp.float32))
        n,r=norm_block(mid,None)
        gh2=gab[s].astype(jnp.float32)+ghb[blk(b),:].astype(jnp.float32)
        row=lax.broadcasted_iota(jnp.int32,(R,1),0)+r0
        mg=jnp.where(row<length,ogb[s].astype(jnp.float32),0.0)
        gn=gh2*g2
        inner=jnp.mean(gn*n,axis=-1,keepdims=True)
        gm=(mg+r*(gn-n*inner)).astype(jnp.bfloat16)
        part=jnp.sum((gh2*n).reshape(R//8,8,D),axis=0)
        gsum=part if gsum is None else gsum+part
        if b<NB//2:
            gm_v[b*R:(b+1)*R,:]=gm
            ex_op[b].wait_recv()
            mine=slice(b*R,(b+1)*R)
            opb[mine,:]=(mid+(opb[mine,:].astype(jnp.float32)+oprv[mine,:].astype(jnp.float32))).astype(jnp.bfloat16)
        at_b=atb[s]
        ga=dot(gm,wo_v[...],NT).astype(jnp.bfloat16)
        for p in range(NP): gat_v[p,blk(b),:]=ga[:,p*128:(p+1)*128]
        xx=ga.astype(jnp.float32)*at_b.astype(jnp.float32)
        hi=xx.astype(jnp.bfloat16); lo=(xx-hi.astype(jnp.float32)).astype(jnp.bfloat16)
        dl_v[:,:,blk(b)]=(dot(ind,hi,NT)+dot(ind,lo,NT)).reshape(NP,8,R)
        w=dot(at_b,gm,TN)
        if b==0: acc[...]=w
        else: acc[...]+=w
    for c in range(D//128): gwo_v[c*W:(c+1)*W,:]=acc[:,c*128:(c+1)*128].astype(jnp.bfloat16)
    gain_v[0,8:16,:]=gsum*0.5
    runs["C"].start()
    pl.semaphore_signal(free_sem,inc=1,device_id=at.core_dev,device_id_type=MESH)
    for c in proj: c.start()
    for c in loads[1:]: c.wait()
    BQ=BK=512
    lane=lax.broadcasted_iota(jnp.int32,(N,128),1)
    rowi=lax.broadcasted_iota(jnp.int32,(N,128),0)
    lf=(lax.broadcasted_iota(jnp.int32,(BK,128),1)%64)<32
    def pair(p,_):
        k=kd[p]; q=qd[p]; do=gat_v[p]
        for h in range(2):
            own=(lane//64)==h
            first=lane==(64*(1-h))
            bias=jnp.where(first&(rowi>=length),-1e30,0.0).astype(jnp.bfloat16)
            ks[h]=jnp.where(own,k,bias)
            ks[2+h]=jnp.where(own,k,jnp.zeros_like(k))
            qs[h]=jnp.where(own,q,jnp.ones_like(q))
            qs[2+h]=jnp.where(own,q,jnp.zeros_like(q))
            vs[h]=jnp.where(own,do,jnp.zeros_like(do))
        dqa[...]=jnp.zeros_like(dqa)
        hook=0
        for j in range(N//BK):
            cols=slice(j*BK,(j+1)*BK)
            v=md[p,cols,:]
            dk=dv=None
            for i in range(j,N//BQ):
                for P_ in range(NP):
                    acts=plan.get((P_,hook))
                    if acts:
                        @pl.when(p==P_)
                        def _():
                            for a in acts: a()
                hook+=1
                rows=slice(i*BQ,(i+1)*BQ)
                for h in range(2):
                    st=dot(ks[h,cols,:],qs[h,rows,:],NT)
                    if i==j:
                        c=lax.broadcasted_iota(jnp.int32,(BK,BQ),0); r=lax.broadcasted_iota(jnp.int32,(BK,BQ),1)
                        st=jnp.where(c<=r,st,-1e30)
                    pt=jnp.exp2(st*C2-lse_ref[p,h:h+1,rows])
                    dpt=dot(v,vs[h,rows,:],NT)
                    dst=(pt*(dpt-dl_v[p,h:h+1,rows])).astype(jnp.bfloat16)
                    a=dot(pt.astype(jnp.bfloat16),vs[h,rows,:])
                    dv=a if dv is None else dv+a
                    b_=dot(dst,qs[2+h,rows,:])
                    dk=b_ if dk is None else dk+b_
                    dqa[rows,:]+=dot(dst,ks[2+h,cols,:],TN)
            kd[p,cols,:]=rot(dk*0.125,cos_v[cols,:],-sin_v[cols,:],lf).astype(jnp.bfloat16)
            md[p,cols,:]=(dv*0.5).astype(jnp.bfloat16)
        for j in range(N//BK):
            cols=slice(j*BK,(j+1)*BK)
            qd[p,cols,:]=rot(dqa[cols,:]*0.125,cos_v[cols,:],-sin_v[cols,:],lf).astype(jnp.bfloat16)
        joint=jnp.concatenate([qd[p],kd[p],md[p]],axis=1)
        g=dot(h1_v[...],joint,TN)
        for c in range(3): gw_v[p,c*D:(c+1)*D,:]=g[:,c*128:(c+1)*128].astype(jnp.bfloat16)
        for P_ in range(NP):
            @pl.when(p==P_)
            def _():
                runs[P_].start()
                @pl.when(off)
                def _(): sw_gf[P_].start()
                @pl.when(diag)
                def _(): lo_gf[P_].start()
                if P_==0:
                    @pl.when(off)
                    def _():
                        for c in sw_out: c.start()
                    @pl.when(diag)
                    def _():
                        for c in lo_out: c.start()
        return 0
    lax.fori_loop(0,NP,pair,0)
    for c in proj: c.wait()
    pl.semaphore_wait(free_sem,1)
    def tok_load(b): return pltpu.make_async_copy(tok_h.at[blk(b)],tokb.at[b%2],blk_sem.at[b%2])
    tok_load(0).start(); tok_load(1).start()
    def input_grad(b,rows):
        gs=[jnp.concatenate([d[p,rows,:] for p in range(NP)],axis=1) for d in (qd,kd,md)]
        out=[]
        for i in range(D//256):
            ws=[v[i//2,:,(i%2)*W:(i%2+1)*W] for v in (pab,pbb,ogb)]
            out.append(dot(gs[0],ws[0],NT)+dot(gs[1],ws[1],NT)+dot(gs[2],ws[2],NT))
        return jnp.concatenate(out,axis=1)
    for b in range(NB//2):
        ghb[theirs(b),:]=input_grad(b,theirs(b)).astype(jnp.bfloat16)
        ex_g1[b].start()
        for a in plan.get(("t",b),[]): a()
    gsum=None
    for b in range(NB//2):
        mine=input_grad(b,blk(b)).astype(jnp.bfloat16).astype(jnp.float32)
        for a in plan.get(("u",b),[]): a()
        ex_g1[b].wait_recv()
        gh=mine+oprv[b*R:(b+1)*R,:].astype(jnp.float32)
        tok_load(b).wait()
        t=tokb[b%2].astype(jnp.float32)
        n,r=norm_block(t,None)
        gn=gh*g1
        part=jnp.sum((gh*n).reshape(R//8,8,D),axis=0)
        gsum=part if gsum is None else gsum+part
        gm_v[b*R:(b+1)*R,:]=(gm_v[b*R:(b+1)*R,:].astype(jnp.float32)+r*(gn-n*jnp.mean(gn*n,axis=-1,keepdims=True))).astype(jnp.bfloat16)
        if b+2<NB//2: tok_load(b+2).start()
        @pl.when(off)
        def _(): sw_gt[b].start()
        @pl.when(diag)
        def _(): lo_gt[b].start()
    gain_v[0,0:8,:]=gsum
    ex_gain[0].start()
    last=plan.get("end",[])
    gain_steps=len(names)
    def gain_step(i):
        ex_gain[i].wait_recv()
        prev=gain_v[0] if i==0 else gain_v[2*i]
        gain_v[2*i+2]=prev+gain_v[2*i+1]
        if i+1<gain_steps: ex_gain[i+1].start()
    gi=0
    for i,a in enumerate(last):
        a()
        if i%3==2 and gi<gain_steps: gain_step(gi); gi+=1
    while gi<gain_steps: gain_step(gi); gi+=1
    gout=pltpu.make_async_copy(gain_v.at[2*gain_steps],gains_o,blk_sem.at[0])
    gout.start()
    for r in runs.values(): r.drain()
    gout.wait()
    for c in ex_gh+ex_op+ex_g1+ex_gain: c.wait_send()
    @pl.when(off)
    def _():
        for c in sw_out+sw_gf+sw_gt: c.wait()
    @pl.when(diag)
    def _():
        for c in lo_out+lo_gf+lo_gt: c.wait()

def back(groups,length8,tok,pa,pb,og,op,gh,att,comb,q,k,m,wq,wk,wv,wo,lse,g1,g2,tables):
    bf=jnp.bfloat16; f32=jnp.float32; S=jax.ShapeDtypeStruct; V=pltpu.VMEM
    N,D=tok.shape; half=N//2; W=wo.shape[0]; NP=W//128; R=256
    KB=1024; units=comb.shape[0]//KB
    rows=comb.shape[0]+W*D//128+3*W*D//128
    levels=1+int(math.log2(groups))
    per=lambda n:sum(n>>(l+1) for l in range(levels))
    cut=[units//4]*3+[units-3*(units//4)]
    recv=sum(per(c*KB)-c*KB//2 for c in cut)+per(W*D//128)+NP*per(3*D)
    anyb=pl.BlockSpec(memory_space=pl.ANY); vm=pl.BlockSpec(memory_space=pltpu.VMEM)
    outs=[S((half,D),bf),S((half,D),bf),S((N,W),bf),S((rows,128),bf),S((16,D),f32),S((comb.shape[0]//2,128),bf)]
    gains=2*(2+levels-1)+1
    scratch=[V((2,R,D),bf)]*5+[V((2,R,W),bf),V((half,D),bf),V((half,D),bf),V((N,D),bf),V((N,D),bf),V((half,D),bf),V((NP,N,128),bf),V((NP,8,N),f32),
        V((NP,N,128),bf),V((NP,N,128),bf),V((NP,N,128),bf),V((4,N,128),bf),V((4,N,128),bf),V((2,N,128),bf),V((N,128),f32),V((N,128),f32),V((N,128),f32),
        V((W,D),bf),V((W,D),f32),V((2,max(cut)*KB//2,128),bf),V((max(cut)*KB//2,128),bf),V((recv,128),bf),V((W*D//128,128),bf),V((NP,3*D,128),bf),V((gains,16,D),f32),
        pltpu.SemaphoreType.DMA((160,)),pltpu.SemaphoreType.DMA((160,)),pltpu.SemaphoreType.DMA((48,)),pltpu.SemaphoreType.DMA((18,)),pltpu.SemaphoreType.REGULAR]
    return pl.pallas_call(functools.partial(back_kernel,groups),out_shape=outs,
        in_specs=[vm]+[anyb]*15+[vm]*7,out_specs=[anyb]*6,scratch_shapes=scratch,
        compiler_params=pltpu.CompilerParams(collective_id=1,has_side_effects=True,vmem_limit_bytes=63<<20),name="back")(
        length8,tok,pa,pb,og,op,gh,att,comb,q,k,m,wq,wk,wv,wo,lse,g1,g2,*tables)

def make_schedule(levels,pairs):
    plan={}
    def put(key,*what): plan.setdefault(key,[]).append(what)
    put(("m",5),"E","start"); put(("m",5),"F","start")
    put((0,0),"A","prep"); put((0,1),"A","f",0); put((0,1),"B","prep"); put((0,2),"B","f",0)
    put((1,4),"E","prep"); put((1,5),"E","f",0); put((1,5),"F","prep"); put((1,6),"F","f",0)
    late={"A":[(1,2),(1,8),(2,2)],"B":[(1,3),(1,9),(2,3)],"E":[(2,2),(2,7),(3,0)],"F":[(2,3),(2,8),(3,1)],
          "C":[(0,6),(1,0),(1,4),(1,7)],0:[(1,8),(2,1),(2,5),(2,9)],1:[(2,6),(3,0),(3,4),(3,7)],2:[(3,5),(3,9),("t",1),("u",0)]}
    gather={"A":[(2,6),(3,0),(3,3),(3,9)],"B":[(2,7),(3,1),(3,4),("t",0)],"C":[(2,4),(2,8),(3,2),(3,6)],
            "E":[(3,4),(3,8),("t",1),("u",2)],"F":[(3,5),(3,9),("t",2),("u",3)],0:[(3,3),(3,7),("t",0),("u",0)],1:[("t",0),("t",3),("u",1)]}
    rest=[]
    for name in ["C","A","B",0,"E","F",1,2,3]:
        first=1 if name in ("A","B","E","F") else 0
        keys=late.get(name,[])
        more=levels-first-len(keys)
        for i in range(levels-first):
            if i<len(keys): put(keys[i],name,"f",first+i)
            else: rest.append((name,"f",first+i))
        keys=gather.get(name,[]) if more<=0 else []
        for i in range(levels):
            if i<len(keys): put(keys[i],name,"g",i)
            else: rest.append((name,"g",i))
    queues={}
    for r in rest: queues.setdefault(r[0],[]).append(r)
    while queues:
        for n in list(queues):
            put("end",*queues[n].pop(0))
            if not queues[n]: del queues[n]
    return plan

def unpack_kernel(jobs,slots,*refs):
    src=refs[0]; n=max(j[2] for j in jobs)+1
    outs=refs[4:4+n]; raw,wide,in_sem,out_sem,r0,r1,r2,row_in,row_out=refs[4+n+3:]
    rows_in=[pltpu.make_async_copy(a,b,row_in.at[i]) for i,(a,b) in enumerate(zip(refs[1:4],(r0,r1,r2)))]
    rows_out=[pltpu.make_async_copy(b,a,row_out.at[i]) for i,(a,b) in enumerate(zip(refs[4+n:4+n+3],(r0,r1,r2)))]
    for c in rows_in: c.start()
    load=lambda i:pltpu.make_async_copy(src.at[pl.ds(jobs[i][0],jobs[i][1])],raw.at[i%slots,pl.ds(0,jobs[i][1])],in_sem.at[i%slots])
    def store(i):
        _,rows,out,row,col=jobs[i]
        return pltpu.make_async_copy(wide.at[i%slots,pl.ds(0,rows)],outs[out].at[pl.ds(row,rows),pl.ds(col*128,128)],out_sem.at[i%slots])
    for i in range(min(slots,len(jobs))): load(i).start()
    for i in range(len(jobs)):
        rows=jobs[i][1]
        load(i).wait()
        if i>=slots: store(i-slots).wait()
        wide[i%slots,0:rows,:]=raw[i%slots,0:rows,:].astype(jnp.float32)
        store(i).start()
        if i+slots<len(jobs): load(i+slots).start()
        if i==len(jobs)//4:
            for a,b in zip(rows_in,rows_out): a.wait(); b.start()
    for i in range(max(0,len(jobs)-slots),len(jobs)): store(i).wait()
    for c in rows_out: c.wait()

def unpack_all(buf,rows,D,FH,W):
    t=FH//128; n=W//128; d=D//128; slots=8
    jobs=[(c*D,D,0,0,c) for c in range(t)]+[((t+c)*D,D,1,0,c) for c in range(t)]
    pos=2*t*D
    jobs+=[(pos+c*FH,FH,2,0,c) for c in range(d)]; pos+=d*FH
    jobs+=[(pos+c*W,W,3,0,c) for c in range(d)]; pos+=d*W
    jobs+=[(pos+(p*3+j)*D,D,4+j,0,p) for p in range(n) for j in range(3)]
    shapes=[(D,FH),(D,FH),(FH,D),(W,D),(D,W),(D,W),(D,W)]
    most=max(j[1] for j in jobs)
    anyb=pl.BlockSpec(memory_space=pl.ANY)
    return pl.pallas_call(functools.partial(unpack_kernel,jobs,slots),in_specs=[anyb]*4,out_specs=[anyb]*10,
        out_shape=[jax.ShapeDtypeStruct(s,jnp.float32) for s in shapes]+[jax.ShapeDtypeStruct(r.shape,r.dtype) for r in rows],
        scratch_shapes=[pltpu.VMEM((slots,most,128),jnp.bfloat16),pltpu.VMEM((slots,most,128),jnp.float32),pltpu.SemaphoreType.DMA((slots,)),pltpu.SemaphoreType.DMA((slots,))]
            +[pltpu.VMEM(r.shape,r.dtype) for r in rows]+[pltpu.SemaphoreType.DMA((3,)),pltpu.SemaphoreType.DMA((3,))],
        compiler_params=pltpu.CompilerParams(vmem_limit_bytes=60<<20),name="unpack")(buf,*rows)

def per_device(groups,tokens,first_values,out_grad,lengths,gain_attn,gain_mlp,w_query,w_key,w_value,w_out,w_gate,w_up,w_down):
    bf=jnp.bfloat16; f32=jnp.float32
    n=groups
    D=tokens.shape[1]
    g1=gain_attn.reshape(1,D); g2=gain_mlp.reshape(1,D)
    lanes=jnp.arange(128)%(HEAD_DIM//2)
    frequency=jnp.exp(lanes.astype(f32)*(-2.0*math.log(10000.0)/HEAD_DIM))
    coarse=(jnp.arange(SLOT//32)*32).astype(f32)[:,None]*frequency[None,:]
    fine=jnp.arange(32).astype(f32)[:,None]*frequency[None,:]
    tables=(jnp.cos(coarse),jnp.sin(coarse),jnp.cos(fine),jnp.sin(fine))
    length8=jnp.broadcast_to(lengths.reshape(1,1),(8,128))
    (tok,og,len_full,q,k,mixed,att,lse,pa,pb,w_q,w_k,w_v,w_o,w_g,w_u,w_d)=front(n,tokens,first_values,out_grad,length8,g1,tables,(w_query,w_key,w_value,w_out,w_gate,w_up,w_down))
    length=len_full[0,:1]
    op,gh2a,comb=mlp(length,tok,pa,pb,og,g2,w_gate,w_up,w_down,w_g,w_u,w_d)
    out,grad_tokens,grad_first,packed,gains,_=back(n,len_full,tok,pa,pb,og,op,gh2a,att,comb,q,k,mixed,w_q,w_k,w_v,w_o,lse,g1,g2,tables)
    gains=jnp.sum(gains.reshape(2,8,D),axis=1)
    FH=w_gate.shape[1]; W=w_query.shape[1]
    gwg,gwu,gwd,gwo,gwq,gwk,gwv,out,grad_tokens,grad_first=unpack_all(packed,(out,grad_tokens,grad_first),D,FH,W)
    return (out,grad_tokens,grad_first,gains[0],gains[1],gwq,gwk,gwv,gwo,gwg,gwu,gwd)

def solution(mesh):
    fine=Mesh(mesh.devices.reshape(-1,2,2),ALL)
    rows=P(ALL,None); slot=P(("zy","core"),"head"); col=P(None,"head"); row=P("head",None)
    return jax.shard_map(functools.partial(per_device,fine.devices.shape[0]),mesh=fine,
        in_specs=(rows,slot,rows,P(("zy","core")),P(),P(),col,col,col,row,col,col,row),
        out_specs=(rows,rows,slot,P(),P(),col,col,col,row,col,col,row),check_vma=False)
```

```python
import functools, math
import jax, jax.numpy as jnp
from jax import lax
from jax.experimental import pallas as pl
from jax.experimental.pallas import tpu as pltpu
from jax.sharding import Mesh, PartitionSpec as P
SLOT=2048; HEAD_DIM=64
C2=math.log2(math.e)/8.0
NT=(((1,),(1,)),((),()))
TN=(((0,),(0,)),((),()))
NN=(((1,),(0,)),((),()))
def dot(a,b,dims=NN): return lax.dot_general(a,b,dims,preferred_element_type=jnp.float32)

EPS=1e-5
R2=256
def norm_block(x,gain):
    r=lax.rsqrt(jnp.mean(x*x,axis=-1,keepdims=True)+EPS)
    n=x*r
    return n,r
def rot(x,cos,sin,lane_first):
    up=pltpu.roll(x,96,1)
    dn=pltpu.roll(x,32,1)
    return x*cos+jnp.where(lane_first,up,dn)*sin


ALL=("zy","core","head")

class Links:
    def __init__(self,send,recv,local):
        self.send,self.recv,self.local=send,recv,local
        self.remote_count=0; self.local_count=0
    def remote(self,src,dst,device):
        at=self.remote_count; self.remote_count+=1
        return pltpu.make_async_remote_copy(src_ref=src,dst_ref=dst,send_sem=self.send.at[at],recv_sem=self.recv.at[at],
            device_id=device,device_id_type=pl.DeviceIdType.MESH)
    def copy(self,src,dst):
        at=self.local_count; self.local_count+=1
        return pltpu.make_async_copy(src,dst,self.local.at[at])

def spread_bits(groups):
    count=min(groups,8); bits=[]
    while count>1:
        count//=2; bits.append(count)
    return bits

class Spread:
    def __init__(self,links,home,full,bits,zy,swap_dev,peer):
        m=2**len(bits); rows=home.shape[0]//m
        place=0
        for level,b in enumerate(bits): place=place+((zy//b)%2)*(2**level)
        one=pl.ds(pl.multiple_of(place*rows,rows),rows)
        self.steps=[links.remote(home.at[one],full.at[one],swap_dev)]
        for level,b in enumerate(bits):
            size=2**level
            block=pl.ds(pl.multiple_of((place//size)*size*rows,size*rows),size*rows)
            self.steps.append(links.remote(full.at[block],full.at[block],peer(b)))

def front_kernel(groups,
        tok_h,fv_h,og_h,len_h,g_ref,ch_ref,sh_ref,cl_ref,sl_ref,wq_h,wk_h,wv_h,wo_h,wg_h,wu_h,wd_h,
        tok_o,og_o,len_o,q_o,k_o,m_o,att_o,lse_o,pa_o,pb_o,wq_o,wk_o,wv_o,wo_o,wg_o,wu_o,wd_o,
        tok_v,len_v,fv_v,wq_v,wk_v,wv_v,wo_v,cos_v,sin_v,qs,ks,vp,ms,kb_ref,s_ref,att_v,lse_v,pa_v,
        send_sem,recv_sem,local_sem):
    zy=lax.axis_index("zy"); core=lax.axis_index("core"); x=lax.axis_index("head")
    off=core!=x; diag=core==x
    L=Links(send_sem,recv_sem,local_sem)
    swap_dev=(zy,1-core,1-x); core_dev=(zy,1-core,x)
    bits=spread_bits(groups)
    peer=lambda b:(zy+b-2*b*((zy//b)%2),core,x)
    barrier=pltpu.get_barrier_semaphore()
    MESH=pl.DeviceIdType.MESH
    half=tok_h.shape[0]; D=tok_h.shape[1]; W=wq_h.shape[1]; NP=W//128
    CH=256; NC=half//CH
    sp={n:Spread(L,h,f,bits,zy,swap_dev,peer) for n,h,f in (("q",wq_h,wq_v),("k",wk_h,wk_v),("v",wv_h,wv_v),("o",wo_h,wo_v),("g",wg_h,wg_o),("u",wu_h,wu_o),("d",wd_h,wd_o))}
    mine=lambda k:pl.ds(pl.multiple_of(core*half+k*CH,CH),CH)
    swap_len=L.remote(len_h,len_v,swap_dev)
    there=lambda k:pl.ds(pl.multiple_of((1-core)*half+k*CH,CH),CH)
    swap_tok=[L.remote(tok_h.at[pl.ds(k*CH,CH)],tok_v.at[there(k)],swap_dev) for k in range(NC)]
    core_tok=[L.remote(tok_v.at[mine(k)],tok_v.at[mine(k)],core_dev) for k in range(NC)]
    swap_fv=[L.remote(fv_h.at[:,pl.ds(p*128,128)],fv_v.at[p],swap_dev) for p in range(NP)]
    HH=half//2
    part=lambda c,j:pl.ds(pl.multiple_of(c*half+j*HH,HH),HH)
    swap_og=[L.remote(og_h.at[pl.ds(j*HH,HH)],og_o.at[part(1-core,j)],swap_dev) for j in range(2)]
    my_half=pl.ds(pl.multiple_of(core*half,half),half)
    core_og=[L.remote(og_o.at[part(core,j)],og_o.at[part(core,j)],core_dev) for j in range(2)]
    PR=512
    core_pa=[L.remote(pa_v.at[pl.ds(r*PR,PR)],pb_o.at[pl.ds(r*PR,PR)],core_dev) for r in range(SLOT//PR)]
    out_pa=[L.copy(pa_v.at[pl.ds(r*PR,PR)],pa_o.at[pl.ds(r*PR,PR)]) for r in range(SLOT//PR)]
    own_tok=L.copy(tok_h,tok_v.at[my_half])
    own_len=L.copy(len_h,len_v)
    own_fv=[L.copy(fv_h.at[:,pl.ds(p*128,128)],fv_v.at[p]) for p in range(NP)]
    own_og=[L.copy(og_h,pa_v.at[pl.ds(0,half)]),L.copy(pa_v.at[pl.ds(0,half)],og_o.at[my_half])]
    core_og_own=[L.remote(og_h.at[pl.ds(j*HH,HH)],og_o.at[part(core,j)],core_dev) for j in range(2)]
    own_qkv=[L.copy(h,v) for h,v in ((wq_h,wq_v),(wk_h,wk_v),(wv_h,wv_v))]
    own_o=L.copy(wo_h,wo_v)
    outs=[L.copy(a,b) for a,b in ((tok_v,tok_o),(len_v,len_o),(qs,q_o),(ks,k_o),(wq_v,wq_o),(wk_v,wk_o),(wv_v,wv_o))]
    outs2=[L.copy(a,b) for a,b in ((ms,m_o),(att_v,att_o),(lse_v,lse_o),(wo_v,wo_o))]

    pl.semaphore_signal(barrier,inc=1,device_id=core_dev,device_id_type=MESH)
    @pl.when(off)
    def _():
        pl.semaphore_signal(barrier,inc=1,device_id=swap_dev,device_id_type=MESH)
        for b in bits: pl.semaphore_signal(barrier,inc=1,device_id=peer(b),device_id_type=MESH)
        pl.semaphore_wait(barrier,2+len(bits))
        for n in "qkvog": sp[n].steps[0].start()
        swap_len.start()
    @pl.when(diag)
    def _():
        pl.semaphore_wait(barrier,1)
        own_tok.start(); own_len.start()
        for c in own_qkv: c.start()
        own_tok.wait()
        for k in range(NC): core_tok[k].start()
        own_len.wait()
        for c in own_fv: c.start()
        own_o.start(); own_og[0].start()
        for c in core_og_own: c.start()
    sign=jnp.where((lax.broadcasted_iota(jnp.int32,(1,128),1)%64)<32,-1.0,1.0)
    cl=cl_ref[...]; sl=sl_ref[...]
    def table(a,_):
        rows=pl.ds(pl.multiple_of(a*32,32),32)
        ch=ch_ref[pl.ds(a,1),:]; sh=sh_ref[pl.ds(a,1),:]
        cos_v[rows,:]=ch*cl-sh*sl
        sin_v[rows,:]=(sh*cl+ch*sl)*sign
        return 0
    lax.fori_loop(0,SLOT//32,table,0)
    nl=len(bits)
    def advance(n,level):
        sp[n].steps[level].wait_recv(); sp[n].steps[level+1].start()
    @pl.when(off)
    def _():
        for level in range(nl):
            for n in ("qkvog" if level<max(nl-1,1) else "qkv"): advance(n,level)
            if level==0:
                for k in range(NC): swap_tok[k].start()
        swap_len.wait_recv()
    @pl.when(diag)
    def _():
        for c in own_qkv: c.wait()
        own_og[0].wait(); own_og[1].start()
    gain=g_ref[...]
    lf=(lax.broadcasted_iota(jnp.int32,(CH,128),1)%64)<32
    def project(block):
        rows=pl.ds(pl.multiple_of(block*CH,CH),CH)
        t=tok_v[rows,:].astype(jnp.float32)
        n,_=norm_block(t,None)
        h=(n*gain).astype(jnp.bfloat16)
        cos=cos_v[rows,:]; sin=sin_v[rows,:]
        for w,o in ((wq_v,qs),(wk_v,ks)):
            y=dot(h,w[...])
            for c in range(NP):
                o[c,rows,:]=rot(y[:,c*128:(c+1)*128],cos,sin,lf).astype(jnp.bfloat16)
        y=dot(h,wv_v[...])
        for c in range(NP): vp[c,rows,:]=y[:,c*128:(c+1)*128]
    for k in range(NC):
        if k==0:
            @pl.when(off)
            def _():
                for n in "qkv": sp[n].steps[nl].wait_recv()
        @pl.when(off)
        def _():
            core_tok[k].wait_recv()
        project(x*NC+k)
        @pl.when(off)
        def _():
            if k==0: sp["u"].steps[0].start(); swap_fv[0].start()
            if k==1 and nl>1: advance("o",nl-1)
            if k==2 and nl>1: advance("g",nl-1)
            if k==3: advance("u",0)
    for k in range(NC):
        @pl.when(off)
        def _():
            swap_tok[k].wait_recv()
            core_tok[k].start()
            if k==1: swap_fv[1].start(); sp["d"].steps[0].start()
        @pl.when(diag)
        def _():
            core_tok[k].wait_recv()
        project((1-x)*NC+k)
    @pl.when(off)
    def _():
        swap_fv[2].start(); swap_fv[3].start()
    for c in outs: c.start()
    plan={}
    todo=lambda slot,act: plan.setdefault(slot,[]).append(act)
    for level in range(1,nl): todo(4*(level-1),functools.partial(advance,"u",level))
    for level in range(nl): todo(3+4*level if level<2 else 10,functools.partial(advance,"d",level))
    todo(4,swap_og[0].start); todo(7,swap_og[1].start)
    todo(12,lambda:(swap_og[0].wait_recv(),core_og[0].start()))
    BQ,BK=512,512
    laneq=lax.broadcasted_iota(jnp.int32,(BQ,128),1)
    lane=lax.broadcasted_iota(jnp.int32,(SLOT,128),1)
    row=lax.broadcasted_iota(jnp.int32,(SLOT,128),0)
    def pair(p,_):
        for at in range(NP):
            @pl.when((p==at)&off)
            def _(): swap_fv[at].wait_recv()
            @pl.when((p==at)&diag)
            def _(): own_fv[at].wait()
        m=(0.5*vp[p]+0.5*fv_v[p].astype(jnp.float32)).astype(jnp.bfloat16)
        ms[p]=m
        k=ks[p]
        length=len_v[0:1,:]
        for h in range(2):
            own=(lane//64)==h
            first=lane==(64*(1-h))
            bias=jnp.where(first&(row>=length),-1e30,0.0).astype(jnp.bfloat16)
            kb_ref[h]=jnp.where(own,k,bias)
            kb_ref[2+h]=jnp.where(own,m,jnp.ones_like(m))
        for i in range(SLOT//BQ):
            for at in range(NP):
                acts=plan.get(at*4+i)
                if acts:
                    @pl.when((p==at)&off)
                    def _():
                        for a in acts: a()
            rows=slice(i*BQ,(i+1)*BQ)
            q=qs[p,rows,:]
            got=[]
            for h in range(2):
                own=(laneq//64)==h
                qh=jnp.where(own,q,jnp.ones_like(q))
                mx=None
                for j in range(i+1):
                    s=dot(qh,kb_ref[h,pl.ds(j*BK,BK),:],NT)
                    if j==i:
                        r=lax.broadcasted_iota(jnp.int32,(BQ,BK),0); c=lax.broadcasted_iota(jnp.int32,(BQ,BK),1)
                        s=jnp.where(c<=r,s,-1e30)
                    s_ref[h,:,pl.ds(j*BK,BK)]=s
                    m_=jnp.max(s,axis=-1,keepdims=True)
                    mx=m_ if mx is None else jnp.maximum(mx,m_)
                mc=mx*C2
                acc=None
                for j in range(i+1):
                    pr=jnp.exp2(s_ref[h,:,pl.ds(j*BK,BK)]*C2-mc).astype(jnp.bfloat16)
                    a=dot(pr,kb_ref[2+h,pl.ds(j*BK,BK),:])
                    acc=a if acc is None else acc+a
                other=64*(1-h)
                l=acc[:,other:other+1]
                got.append((acc/l,mc+jnp.log2(l)))
            att_v[rows,pl.ds(pl.multiple_of(p*128,128),128)]=jnp.where((laneq//64)==0,got[0][0],got[1][0]).astype(jnp.bfloat16)
            lse_v[p,:,i*BQ:(i+1)*BQ]=jnp.where(lax.broadcasted_iota(jnp.int32,(BQ,128),1)==0,got[0][1],got[1][1]).T[0:8]
        return 0
    lax.fori_loop(0,NP,pair,0)
    @pl.when(off)
    def _():
        sp["o"].steps[nl].wait_recv()
        swap_og[1].wait_recv(); core_og[1].start()
    @pl.when(diag)
    def _():
        own_o.wait(); own_og[1].wait()
    for c in outs2: c.start()
    for r in range(SLOT//PR):
        pa_v[r*PR:(r+1)*PR,:]=dot(att_v[r*PR:(r+1)*PR,:],wo_v[...]).astype(jnp.bfloat16)
        core_pa[r].start(); out_pa[r].start()
    for c in outs+outs2+out_pa: c.wait()
    for c in core_pa: c.wait()
    for k in range(NC): core_tok[k].wait_send()
    @pl.when(diag)
    def _():
        for c in core_og_own: c.wait_send()
        for c in core_og: c.wait_recv()
    @pl.when(off)
    def _():
        for c in core_og: c.wait_send()
        for c in core_og_own: c.wait_recv()
        for n in "gud": sp[n].steps[nl].wait_recv()
        for n in "qkvogud":
            for s in sp[n].steps: s.wait_send()
        swap_len.wait_send()
        for c in swap_tok+swap_fv+swap_og: c.wait_send()

def front(groups,tok,fv,og,length,gain,tables,ws):
    N=SLOT; D=tok.shape[1]; W=ws[0].shape[1]; NP=W//128; FH=ws[4].shape[1]
    bf=jnp.bfloat16; f32=jnp.float32
    S=jax.ShapeDtypeStruct
    outs=[S((N,D),bf),S((N,D),bf),S((8,128),jnp.int32),S((NP,N,128),bf),S((NP,N,128),bf),S((NP,N,128),bf),S((N,W),bf),S((NP,8,N),f32),S((N,D),bf),S((N,D),bf)]+[S(w.shape,bf) for w in ws]
    anyb=pl.BlockSpec(memory_space=pl.ANY); vm=pl.BlockSpec(memory_space=pltpu.VMEM)
    V=pltpu.VMEM
    scratch=[V((N,D),bf),V((8,128),jnp.int32),V((NP,N,128),bf),V((D,W),bf),V((D,W),bf),V((D,W),bf),V((W,D),bf),V((N,128),f32),V((N,128),f32),
        V((NP,N,128),bf),V((NP,N,128),bf),V((NP,N,128),f32),V((NP,N,128),bf),V((4,N,128),bf),V((2,512,N),f32),V((N,W),bf),V((NP,8,N),f32),V((N,D),bf),
        pltpu.SemaphoreType.DMA((56,)),pltpu.SemaphoreType.DMA((56,)),pltpu.SemaphoreType.DMA((32,))]
    return pl.pallas_call(functools.partial(front_kernel,groups),out_shape=outs,
        in_specs=[anyb]*4+[vm]*5+[anyb]*7,out_specs=[anyb]*len(outs),scratch_shapes=scratch,
        compiler_params=pltpu.CompilerParams(collective_id=0,has_side_effects=True,vmem_limit_bytes=58<<20),name="front")(tok,fv,og,length,gain,*tables,*ws)

class Reduce:
    def __init__(self,links,order,src,offset,rows,recv,recv_at,at,keep=None):
        self.order=order; self.rows=rows; self.offset=offset; self.at=at; self.then=None
        self.keep=src if keep is None else keep
        self.levels=len(order); self.leaf=rows>>self.levels; self.bufs=[]; self.sends=[]
        for level,name in enumerate(order):
            size=rows>>(level+1); bit=at.bit(name)
            self.bufs.append(recv.at[pl.ds(recv_at,size)]); recv_at+=size
            if level==0: source=src.at[pl.ds(pl.multiple_of(offset+(1-bit)*size,16),size)]
            else: source=self.bufs[level-1].at[pl.ds(pl.multiple_of((1-bit)*size,16),size)]
            self.sends.append(links.remote(source,self.bufs[level],at.partner(name)))
        self.recv_end=recv_at
    def start(self): self.sends[0].start()
    def finish(self,level):
        self.sends[level].wait_recv()
        size=self.rows>>(level+1); bit=self.at.bit(self.order[level])
        into=self.bufs[level]
        if level==0: mine=self.keep.at[pl.ds(pl.multiple_of(self.offset+bit*size,16),size)]
        else: mine=self.bufs[level-1].at[pl.ds(pl.multiple_of(bit*size,16),size)]
        step=math.gcd(size,512)
        def add(i,_):
            rows=pl.ds(pl.multiple_of(i*step,step),step)
            into[rows,:]=(into[rows,:].astype(jnp.float32)+mine[rows,:].astype(jnp.float32)).astype(jnp.bfloat16)
            return 0
        lax.fori_loop(0,size//step,add,0)
        if level+1<self.levels: self.sends[level+1].start()
        elif self.then is not None: self.then()
    def drain_sends(self):
        for c in self.sends: c.wait_send()

class Gather:
    def __init__(self,links,order,leaf,rows,result,result_at,at):
        self.at=at; self.steps=len(order); size=rows>>self.steps
        weight={name:rows>>(i+1) for i,name in enumerate(order)}
        own=sum(at.bit(name)*weight[name] for name in order)
        spot=result.at[pl.ds(pl.multiple_of(result_at+own,16),size)]
        self.swap=links.remote(leaf,spot,at.swap)
        self.keep=links.copy(leaf,spot)
        self.gathers=[]; gathered=[]
        for name in sorted([n for n in order if n!="x"],reverse=True)+["x"]:
            unit=size; apart=[]
            for w in sorted(gathered):
                if w==unit: unit*=2
                else: apart.append(w)
            base=sum((at.core if n=="x" else at.bit(n))*weight[n] for n in order if weight[n] not in gathered)
            combos=[0]
            for w in apart: combos=combos+[c+w for c in combos]
            device=at.core_dev if name=="x" else at.partner(name)
            step=[]
            for c in combos:
                block=result.at[pl.ds(pl.multiple_of(result_at+base+c,16),unit)]
                step.append(links.remote(block,block,device))
            self.gathers.append(step); gathered.append(weight[name])
    def begin(self):
        @pl.when(self.at.off)
        def _(): self.swap.start()
        @pl.when(self.at.diag)
        def _(): self.keep.start()
    def go(self,step):
        if step==0:
            @pl.when(self.at.off)
            def _(): self.swap.wait_recv()
            @pl.when(self.at.diag)
            def _(): self.keep.wait()
        else:
            for c in self.gathers[step-1]: c.wait_recv()
        for c in self.gathers[step]: c.start()
    def drain(self):
        for c in self.gathers[-1]: c.wait_recv()
        @pl.when(self.at.off)
        def _(): self.swap.wait_send()
        for s in self.gathers:
            for c in s: c.wait_send()

class Place: pass
def place_of(groups):
    at=Place()
    at.zy=lax.axis_index("zy"); at.core=lax.axis_index("core"); at.x=lax.axis_index("head")
    at.off=at.core!=at.x; at.diag=at.core==at.x
    at.bit=lambda name: at.x if name=="x" else (at.zy//name)%2
    at.partner=lambda name: (at.zy,at.core,1-at.x) if name=="x" else (at.zy+name-2*name*((at.zy//name)%2),at.core,at.x)
    at.swap=(at.zy,1-at.core,1-at.x); at.core_dev=(at.zy,1-at.core,at.x)
    at.bits=[]
    b=1
    while b<groups: at.bits.append(b); b*=2
    return at

def passes_of(tiles):
    a=(4*tiles+10)//11; b=(3*tiles+10)//11; c=(tiles-a-b+1)//2
    return (a,b,c,tiles-a-b-c)
def runs_of(tiles,d_tiles):
    KB=1024; pos=0; out=[]
    for t,n in enumerate(passes_of(tiles)):
        units=(2*n*d_tiles*128+d_tiles*128*n)//KB
        parts=[[units//2,units-units//2],[units//3,units//3,units-2*(units//3)],[units],[0,units]][t]
        for i,u in enumerate(parts):
            if u: out.append((t,"abc"[i]+str(t),i,pos,u*KB))
            pos+=u*KB
    return out
def orders_of(bits):
    return [["x"]+bits,bits[:1]+["x"]+bits[1:],bits[1:2]+bits[:1]+["x"]+bits[2:]]

MLP_PLAN={
    (2, 0):[('a0',0),('b0',0)],
    (2, 6):[('a1',0),('b1',0),('c1',0)],
    (3, 2):[('a0',1),('b0',1)],
    (3, 4):[('a1',1),('b1',1)],
    (3, 5):[('c1',1),('a0',2)],
    (3, 7):[('b0',2)],
}
def mlp_kernel(groups,len_ref,tok_h,pa_h,pb_h,og_h,g_ref,wg_h,wu_h,wd_h,wg_f,wu_f,wd_f,
        op_o,opr_o,gh_o,ghr_o,rest_o,leaf_o,
        tokb,pab,pbb,h_v,g_v,oacc,gacc,wgu,wd,agu,ad,comb,recv_v,
        send_sem,recv_sem,local_sem,blk_sem,w_sem,out_sem,ex_send,ex_recv):
    at=place_of(groups); core=at.core; diag=at.diag
    MESH=pl.DeviceIdType.MESH
    N,D=tok_h.shape; FH=wg_h.shape[1]; R=256; NB=N//R
    passes=passes_of(FH//128); T=len(passes)
    L=Links(send_sem,recv_sem,local_sem)
    orders=orders_of(at.bits)
    runs={}; rp=0; lp=0; leaves=[]
    for t,name,kind,pos,rows in runs_of(FH//128,D//128):
        if t<2:
            r=Reduce(L,orders[kind],comb,pos,rows,recv_v,rp,at); rp=r.recv_end
            runs[name]=(t,r)
            leaves.append(L.copy(r.bufs[-1],leaf_o.at[pl.ds(lp,r.leaf)])); lp+=r.leaf
    out_rest=L.copy(comb.at[pl.ds(comb.shape[0]-rest_o.shape[0],rest_o.shape[0])],rest_o)
    barrier=pltpu.get_barrier_semaphore()
    partners=[at.core_dev]+[at.partner(n) for n in ["x"]+at.bits]
    for d in partners: pl.semaphore_signal(barrier,inc=1,device_id=d,device_id_type=MESH)
    pl.semaphore_wait(barrier,len(partners))
    firsts=[sum(passes[:t]) for t in range(T)]
    def w_copies(t,src):
        n=passes[t]*128; f=firsts[t]*128; s=t%2
        a,b,c=src
        return [pltpu.make_async_copy(a.at[:,pl.ds(f,n)],wgu.at[s,:,pl.ds(0,n)],w_sem.at[0]),
            pltpu.make_async_copy(b.at[:,pl.ds(f,n)],wgu.at[s,:,pl.ds(n,n)],w_sem.at[1]),
            pltpu.make_async_copy(c.at[pl.ds(f,n)],wd.at[s,pl.ds(0,n)],w_sem.at[2])]
    def w_start(t):
        @pl.when(diag)
        def _():
            for c in w_copies(t,(wg_h,wu_h,wd_h)): c.start()
        @pl.when(at.off)
        def _():
            for c in w_copies(t,(wg_f,wu_f,wd_f)): c.start()
    def w_wait(t):
        for c in w_copies(t,(wg_h,wu_h,wd_h)): c.wait()
    w_start(0)
    rowsof=lambda b:pl.ds(pl.multiple_of(((core*(NB//2)+b)%NB)*R,R),R)
    def loads(b):
        s=b%2
        return [pltpu.make_async_copy(h.at[rowsof(b)],v.at[s],blk_sem.at[s,i]) for i,(h,v) in enumerate(((tok_h,tokb),(pa_h,pab),(pb_h,pbb)))]+[
            pltpu.make_async_copy(og_h.at[rowsof(b)],g_v.at[rowsof(b)],blk_sem.at[s,3])]
    for c in loads(0): c.start()
    w_wait(0)
    gain=g_ref[...]; length=len_ref[0:1,0:1]
    def to_partner(b):
        send=[pltpu.make_async_remote_copy(src_ref=g_v.at[rowsof(b)],dst_ref=ghr_o.at[rowsof(b)],send_sem=ex_send.at[0,b],recv_sem=ex_recv.at[0,b],device_id=at.core_dev,device_id_type=MESH)]
        k=b-NB//2
        last=pltpu.make_async_remote_copy(src_ref=h_v.at[rowsof(b)],dst_ref=opr_o.at[pl.ds(pl.multiple_of(k*R,R),R)],send_sem=ex_send.at[1,b],recv_sem=ex_recv.at[1,b],device_id=at.core_dev,device_id_type=MESH)
        return send,last
    def outs(b): return [pltpu.make_async_copy(h_v.at[rowsof(b)],op_o.at[rowsof(b)],out_sem.at[0,b]),pltpu.make_async_copy(g_v.at[rowsof(b)],gh_o.at[rowsof(b)],out_sem.at[1,b])]
    for t,n in enumerate(passes):
        s=t%2; w=n*128
        def block(b,_):
            for B in range(NB):
                acts=MLP_PLAN.get((t,B))
                if acts:
                    @pl.when(b==B)
                    def _():
                        for name,level in acts:
                            if name in runs and level<runs[name][1].levels: runs[name][1].finish(level)
            rows=rowsof(b)
            if t==0:
                @pl.when(b+1<NB)
                def _():
                    for c in loads(b+1): c.start()
                for c in loads(b): c.wait()
                i=b%2
                x=tokb[i].astype(jnp.float32)+(pab[i].astype(jnp.float32)+pbb[i].astype(jnp.float32))
                nn,_=norm_block(x,None)
                h=(nn*gain).astype(jnp.bfloat16)
                h_v[rows,:]=h
                row=lax.broadcasted_iota(jnp.int32,(R,1),0)+((core*(NB//2)+b)%NB)*R
                g=jnp.where(row<length,g_v[rows,:],jnp.zeros((),jnp.bfloat16))
                g_v[rows,:]=g
            else:
                h=h_v[rows,:]; g=g_v[rows,:]
            gu=dot(h,wgu[s,:,0:2*w])
            gate=gu[:,:w]; up=gu[:,w:]
            gh=dot(g,wd[s,0:w,:],NT)
            sg=0.5*jnp.tanh(0.5*gate)+0.5
            silu=gate*sg
            hid=(silu*up).astype(jnp.bfloat16)
            both=jnp.concatenate([(gh*up*(sg*(1.0+gate*(1.0-sg)))).astype(jnp.bfloat16),(gh*silu).astype(jnp.bfloat16)],axis=1)
            o=dot(hid,wd[s,0:w,:])
            q=dot(both,wgu[s,:,0:2*w],NT)
            da=dot(hid,g,TN); dg=dot(h,both,TN)
            if t==0: oacc[rows,:]=o; gacc[rows,:]=q
            elif t<T-1: oacc[rows,:]+=o; gacc[rows,:]+=q
            else:
                h_v[rows,:]=(oacc[rows,:]+o).astype(jnp.bfloat16)
                g_v[rows,:]=(gacc[rows,:]+q).astype(jnp.bfloat16)
                for c in outs(b): c.start()
                send,last=to_partner(b)
                for c in send: c.start()
                @pl.when(b>=NB//2)
                def _(): last.start()
            @pl.when(b==0)
            def _(): ad[0:w,:]=da; agu[:,0:2*w]=dg
            @pl.when(b>0)
            def _(): ad[0:w,:]+=da; agu[:,0:2*w]+=dg
            if t+1<T:
                @pl.when(b==NB-2)
                def _(): w_start(t+1)
            return 0
        lax.fori_loop(0,NB,block,0)
        base=firsts[t]*(2*D+D)
        for c in range(2*n): comb[base+c*D:base+(c+1)*D,:]=agu[:,c*128:(c+1)*128].astype(jnp.bfloat16)
        base+=2*n*D
        for c in range(D//128): comb[base+c*w:base+(c+1)*w,:]=ad[0:w,c*128:(c+1)*128].astype(jnp.bfloat16)
        for name,(rt,r) in runs.items():
            if rt==t: r.start()
        if t+1<T: w_wait(t+1)
    out_rest.start()
    planned={(a,l) for v in MLP_PLAN.values() for a,l in v}
    queues=[[(r,l) for l in range(r.levels) if (name,l) not in planned] for name,(rt,r) in runs.items()]
    while any(queues):
        for q in queues:
            if q:
                r,l=q.pop(0); r.finish(l)
    for c in leaves: c.start()
    def settle(b,_):
        for c in outs(b): c.wait()
        send,last=to_partner(b)
        for c in send: c.wait()
        @pl.when(b>=NB//2)
        def _(): last.wait()
        return 0
    lax.fori_loop(0,NB,settle,0)
    for c in leaves: c.wait()
    out_rest.wait()
    for _,r in runs.values(): r.drain_sends()

def mlp(groups,length8,tok,pa,pb,og,gain,ws,full):
    bf=jnp.bfloat16; f32=jnp.float32; S=jax.ShapeDtypeStruct; V=pltpu.VMEM
    N,D=tok.shape; FH=ws[0].shape[1]; R=256
    anyb=pl.BlockSpec(memory_space=pl.ANY); vm=pl.BlockSpec(memory_space=pltpu.VMEM)
    levels=1+int(math.log2(groups))
    all_runs=runs_of(FH//128,D//128)
    early=[r for r in all_runs if r[0]<2]
    recv=sum(r[4]>>(l+1) for r in early for l in range(levels))
    leaf=sum(r[4]>>levels for r in early)
    total=sum(r[4] for r in all_runs); rest=sum(r[4] for r in all_runs if r[0]>=2)
    w=max(passes_of(FH//128))*128
    outs=[S((N,D),bf),S((N//2,D),bf),S((N,D),bf),S((N,D),bf),S((rest,128),bf),S((leaf,128),bf)]
    DM=pltpu.SemaphoreType.DMA
    return pl.pallas_call(functools.partial(mlp_kernel,groups),out_shape=outs,in_specs=[vm]+[anyb]*4+[vm]+[anyb]*6,out_specs=[anyb]*6,
        scratch_shapes=[V((2,R,D),bf)]*3+[V((N,D),bf),V((N,D),bf),V((N,D),f32),V((N,D),f32),V((2,D,2*w),bf),V((2,w,D),bf),V((D,2*w),f32),V((w,D),f32),V((total,128),bf),V((recv,128),bf),
            DM((48,)),DM((48,)),DM((16,)),DM((2,4)),DM((3,)),DM((2,N//R)),DM((2,N//R)),DM((2,N//R))],
        compiler_params=pltpu.CompilerParams(collective_id=2,has_side_effects=True,vmem_limit_bytes=63<<20),name="mlp")(length8,tok,pa,pb,og,gain,*ws,*full)

def back_kernel(groups,
        len_ref,tok_h,pa_h,pb_h,og_h,op_h,opr_h,gh_h,ghr_h,att_h,rest_h,leaf_h,q_h,k_h,m_h,wq_h,wk_h,wv_h,wo_h,lse_ref,g1_ref,g2_ref,ch_ref,sh_ref,cl_ref,sl_ref,
        out_o,gt_o,gf_o,res_o,gains_o,
        tokb,pab,pbb,ogb,gab,grb,orb,atb,opb,oprv,ghb,h1_v,gm_v,gat_v,dl_v,qd,kd,md,ks,qs,vs,dqa,cos_v,sin_v,wo_v,acc,src_v,leaf_v,recv_v,gwo_v,gw_v,gain_v,
        send_sem,recv_sem,local_sem,blk_sem):
    at=place_of(groups); core=at.core; off=at.off; diag=at.diag
    L=Links(send_sem,recv_sem,local_sem)
    MESH=pl.DeviceIdType.MESH
    N,D=tok_h.shape; half=N//2; W=wo_h.shape[0]; NP=W//128; R=256; NB=N//R
    bits=at.bits
    orders=orders_of(bits); FH=rest_h.shape[0]; all_runs=runs_of(FF_TILES(res_o.shape[0],W,D),D//128)
    total=sum(r[4] for r in all_runs); rest_at=total-rest_h.shape[0]
    runs={}; gathers={}; rp=0; lp=0
    for t,name,kind,pos,rows in all_runs:
        if t<2:
            size=rows>>(1+len(bits))
            gathers[name]=Gather(L,orders[kind],leaf_v.at[pl.ds(lp,size)],rows,res_o,pos,at); lp+=size
        else: runs[name]=Reduce(L,orders[kind],rest_h,pos-rest_at,rows,recv_v,rp,at,keep=src_v); rp=runs[name].recv_end
    early=list(gathers); late=list(runs)
    runs["C"]=Reduce(L,orders[2],gwo_v,0,gwo_v.shape[0],recv_v,rp,at); rp=runs["C"].recv_end
    for p in range(NP): runs[p]=Reduce(L,orders[2],gw_v.at[p],0,gw_v.shape[1],recv_v,rp,at); rp=runs[p].recv_end
    places={name:(orders[kind],rows,pos) for t,name,kind,pos,rows in all_runs}
    places["C"]=(orders[2],gwo_v.shape[0],total)
    for p in range(NP): places[p]=(orders[2],gw_v.shape[1],total+gwo_v.shape[0]+p*gw_v.shape[1])
    for name,r in runs.items():
        order,rows,pos=places[name]
        gathers[name]=Gather(L,order,r.bufs[-1],rows,res_o,pos,at); r.then=gathers[name].begin
    first_rows=lambda b:pl.multiple_of(((core*(NB//2)+b)%NB)*R,R)
    blk=lambda b:pl.ds(first_rows(b),R)
    theirs=lambda b:pl.ds(pl.multiple_of((((1-core)*(NB//2)+b)%NB)*R,R),R)
    piece=half//8
    sw_out=[L.remote(opb.at[pl.ds(i*piece,piece)],out_o.at[pl.ds(i*piece,piece)],at.swap) for i in range(8)]
    lo_out=[L.copy(opb.at[pl.ds(i*piece,piece)],out_o.at[pl.ds(i*piece,piece)]) for i in range(8)]
    sw_gf=[[L.remote(md.at[p,pl.ds(i*half,half)],gf_o.at[pl.ds(i*half,half),pl.ds(p*128,128)],at.swap) for i in range(2)] for p in range(NP)]
    lo_gf=[[L.copy(md.at[p,pl.ds(i*half,half)],gf_o.at[pl.ds(i*half,half),pl.ds(p*128,128)]) for i in range(2)] for p in range(NP)]
    def home(name,i):
        a,b=(sw_out[i],lo_out[i]) if name=="out" else (sw_gf[name[1]][i],lo_gf[name[1]][i])
        @pl.when(off)
        def _(): a.start()
        @pl.when(diag)
        def _(): b.start()
    ex_g1=[L.remote(ghb.at[pl.ds(b*R,R)],oprv.at[pl.ds(b*R,R)],at.core_dev) for b in range(NB//2)]
    sw_gt=[L.remote(gm_v.at[pl.ds(b*R,R)],gt_o.at[pl.ds(b*R,R)],at.swap) for b in range(NB//2)]
    lo_gt=[L.copy(gm_v.at[pl.ds(b*R,R)],gt_o.at[pl.ds(b*R,R)]) for b in range(NB//2)]
    names=["c","x"]+bits
    ex_gain=[L.remote(gain_v.at[0] if i==0 else gain_v.at[2*i],gain_v.at[2*i+1],at.core_dev if n=="c" else at.partner(n)) for i,n in enumerate(names)]
    loads=[L.copy(a,b) for a,b in ((wo_h,wo_v),(q_h,qd),(k_h,kd),(m_h,md))]
    proj=[L.copy(w.at[pl.ds(i*256,256)],v.at[i//2,:,pl.ds((i%2)*W,W)]) for w,v in ((wq_h,pab),(wk_h,pbb),(wv_h,ogb)) for i in range(D//256)]
    barrier=pltpu.get_barrier_semaphore()
    for d in [at.core_dev]+[at.partner(n) for n in ["x"]+bits]:
        pl.semaphore_signal(barrier,inc=1,device_id=d,device_id_type=MESH)
    @pl.when(off)
    def _():
        pl.semaphore_signal(barrier,inc=1,device_id=at.swap,device_id_type=MESH)
        pl.semaphore_wait(barrier,3+len(bits))
    @pl.when(diag)
    def _(): pl.semaphore_wait(barrier,2+len(bits))
    for name in late: runs[name].start()
    own_rest=L.copy(rest_h,src_v); own_leaf=L.copy(leaf_h,leaf_v)
    own_leaf.start()
    def block_loads(b):
        s=b%2
        pairs=[(tok_h,tokb),(pa_h,pab),(pb_h,pbb),(og_h,ogb),(gh_h,gab),(ghr_h,grb),(att_h,atb)]
        cps=[pltpu.make_async_copy(h.at[blk(b)],v.at[s],blk_sem.at[s*9+i]) for i,(h,v) in enumerate(pairs)]
        if b<NB//2:
            cps.append(pltpu.make_async_copy(op_h.at[blk(b)],opb.at[pl.ds(b*R,R)],blk_sem.at[s*9+7]))
            cps.append(pltpu.make_async_copy(opr_h.at[pl.ds(b*R,R)],orb.at[s],blk_sem.at[s*9+8]))
        return cps
    for c in block_loads(0): c.start()
    for c in loads: c.start()
    own_rest.start()
    own_leaf.wait()
    for name in early: gathers[name].begin()
    sign=jnp.where((lax.broadcasted_iota(jnp.int32,(1,128),1)%64)<32,-1.0,1.0)
    cl=cl_ref[...]; sl=sl_ref[...]
    def table(a,_):
        rows=pl.ds(pl.multiple_of(a*32,32),32)
        ch=ch_ref[pl.ds(a,1),:]; sh=sh_ref[pl.ds(a,1),:]
        cos_v[rows,:]=ch*cl-sh*sl
        sin_v[rows,:]=(sh*cl+ch*sl)*sign
        return 0
    lax.fori_loop(0,N//32,table,0)
    g1=g1_ref[...]; g2=g2_ref[...]
    length=len_ref[0:1,0:1]
    hr=lax.broadcasted_iota(jnp.int32,(8*NP,W),0); ln=lax.broadcasted_iota(jnp.int32,(8*NP,W),1)
    ind=jnp.where(((ln//64)==((hr//8)*2+hr%8))&(hr%8<2),1.0,0.0).astype(jnp.bfloat16)
    loads[0].wait(); own_rest.wait()
    gsum=None
    plan={}
    todo=lambda t,*acts: plan.setdefault(t,[]).extend(acts)
    def action(name,what,level): return functools.partial(runs[name].finish if what=="f" else gathers[name].go,level)
    done=set()
    levels=1+len(bits)
    for key,items in BACK_PLAN.items():
        for item in items:
            if item[1]=="s": todo(key,functools.partial(home,item[0],item[2])); done.add(item)
            elif levels==4 or item[1]=="f": todo(key,action(*item)); done.add(item)
    left=[i for i in BACK_END if levels==4 and i not in done]
    done.update(left)
    for i in range(2*levels):
        for name in list(gathers):
            what,level=("f",i) if i<levels else ("g",i-levels)
            if (what=="g" or name in runs) and (name,what,level) not in done: left.append((name,what,level))
    for item in left: todo("end",action(*item))
    for name,i in [("out",i) for i in range(8)]+[(("gf",p),i) for p in range(NP) for i in range(2)]:
        if (name,"s",i) not in done: todo(("u",0),functools.partial(home,name,i))
    for b in range(NB):
        for a in plan.get(("m",b),[]): a()
        if b+1<NB:
            for c in block_loads(b+1): c.start()
        for c in block_loads(b): c.wait()
        s=b%2; r0=first_rows(b)
        t=tokb[s].astype(jnp.float32)
        n1,_=norm_block(t,None)
        h1_v[blk(b),:]=(n1*g1).astype(jnp.bfloat16)
        mid=t+(pab[s].astype(jnp.float32)+pbb[s].astype(jnp.float32))
        n,r=norm_block(mid,None)
        gh2=gab[s].astype(jnp.float32)+grb[s].astype(jnp.float32)
        row=lax.broadcasted_iota(jnp.int32,(R,1),0)+r0
        mg=jnp.where(row<length,ogb[s].astype(jnp.float32),0.0)
        gn=gh2*g2
        inner=jnp.mean(gn*n,axis=-1,keepdims=True)
        gm=(mg+r*(gn-n*inner)).astype(jnp.bfloat16)
        part=jnp.sum((gh2*n).reshape(R//8,8,D),axis=0)
        gsum=part if gsum is None else gsum+part
        if b<NB//2:
            gm_v[b*R:(b+1)*R,:]=gm
            mine=slice(b*R,(b+1)*R)
            opb[mine,:]=(mid+(opb[mine,:].astype(jnp.float32)+orb[s].astype(jnp.float32))).astype(jnp.bfloat16)
        at_b=atb[s]
        ga=dot(gm,wo_v[...],NT).astype(jnp.bfloat16)
        for p in range(NP): gat_v[p,blk(b),:]=ga[:,p*128:(p+1)*128]
        xx=ga.astype(jnp.float32)*at_b.astype(jnp.float32)
        hi=xx.astype(jnp.bfloat16); lo=(xx-hi.astype(jnp.float32)).astype(jnp.bfloat16)
        dl_v[:,:,blk(b)]=(dot(ind,hi,NT)+dot(ind,lo,NT)).reshape(NP,8,R)
        w=dot(at_b,gm,TN)
        if b==0: acc[...]=w
        else: acc[...]+=w
    for c in range(D//128): gwo_v[c*W:(c+1)*W,:]=acc[:,c*128:(c+1)*128].astype(jnp.bfloat16)
    gain_v[0,8:16,:]=gsum*0.5
    runs["C"].start()
    for c in proj: c.start()
    for c in loads[1:]: c.wait()
    BQ=BK=512
    lane=lax.broadcasted_iota(jnp.int32,(N,128),1)
    rowi=lax.broadcasted_iota(jnp.int32,(N,128),0)
    lf=(lax.broadcasted_iota(jnp.int32,(BK,128),1)%64)<32
    def pair(p,_):
        k=kd[p]; q=qd[p]; do=gat_v[p]
        for h in range(2):
            own=(lane//64)==h
            first=lane==(64*(1-h))
            bias=jnp.where(first&(rowi>=length),-1e30,0.0).astype(jnp.bfloat16)
            ks[h]=jnp.where(own,k,bias)
            ks[2+h]=jnp.where(own,k,jnp.zeros_like(k))
            qs[h]=jnp.where(own,q,jnp.ones_like(q))
            qs[2+h]=jnp.where(own,q,jnp.zeros_like(q))
            vs[h]=jnp.where(own,do,jnp.zeros_like(do))
        dqa[...]=jnp.zeros_like(dqa)
        hook=0
        for j in range(N//BK):
            cols=slice(j*BK,(j+1)*BK)
            v=md[p,cols,:]
            dk=dv=None
            for i in range(j,N//BQ):
                for P_ in range(NP):
                    acts=plan.get((P_,hook))
                    if acts:
                        @pl.when(p==P_)
                        def _():
                            for a in acts: a()
                hook+=1
                rows=slice(i*BQ,(i+1)*BQ)
                for h in range(2):
                    st=dot(ks[h,cols,:],qs[h,rows,:],NT)
                    if i==j:
                        c=lax.broadcasted_iota(jnp.int32,(BK,BQ),0); r=lax.broadcasted_iota(jnp.int32,(BK,BQ),1)
                        st=jnp.where(c<=r,st,-1e30)
                    pt=jnp.exp2(st*C2-lse_ref[p,h:h+1,rows])
                    dpt=dot(v,vs[h,rows,:],NT)
                    dst=(pt*(dpt-dl_v[p,h:h+1,rows])).astype(jnp.bfloat16)
                    a=dot(pt.astype(jnp.bfloat16),vs[h,rows,:])
                    dv=a if dv is None else dv+a
                    b_=dot(dst,qs[2+h,rows,:])
                    dk=b_ if dk is None else dk+b_
                    dqa[rows,:]+=dot(dst,ks[2+h,cols,:],TN)
            kd[p,cols,:]=rot(dk*0.125,cos_v[cols,:],-sin_v[cols,:],lf).astype(jnp.bfloat16)
            md[p,cols,:]=(dv*0.5).astype(jnp.bfloat16)
        for j in range(N//BK):
            cols=slice(j*BK,(j+1)*BK)
            qd[p,cols,:]=rot(dqa[cols,:]*0.125,cos_v[cols,:],-sin_v[cols,:],lf).astype(jnp.bfloat16)
        joint=jnp.concatenate([qd[p],kd[p],md[p]],axis=1)
        g=dot(h1_v[...],joint,TN)
        for c in range(3): gw_v[p,c*D:(c+1)*D,:]=g[:,c*128:(c+1)*128].astype(jnp.bfloat16)
        for P_ in range(NP):
            @pl.when(p==P_)
            def _():
                runs[P_].start()
        return 0
    lax.fori_loop(0,NP,pair,0)
    for c in proj: c.wait()
    def tok_load(b): return pltpu.make_async_copy(tok_h.at[blk(b)],tokb.at[b%2],blk_sem.at[b%2])
    tok_load(0).start(); tok_load(1).start()
    def input_grad(b,rows):
        gs=[jnp.concatenate([d[p,rows,:] for p in range(NP)],axis=1) for d in (qd,kd,md)]
        out=[]
        for i in range(D//256):
            ws=[v[i//2,:,(i%2)*W:(i%2+1)*W] for v in (pab,pbb,ogb)]
            out.append(dot(gs[0],ws[0],NT)+dot(gs[1],ws[1],NT)+dot(gs[2],ws[2],NT))
        return jnp.concatenate(out,axis=1)
    for b in range(NB//2):
        ghb[b*R:(b+1)*R,:]=input_grad(b,theirs(b)).astype(jnp.bfloat16)
        ex_g1[b].start()
        for a in plan.get(("t",b),[]): a()
    gsum=None
    for b in range(NB//2):
        mine=input_grad(b,blk(b)).astype(jnp.bfloat16).astype(jnp.float32)
        for a in plan.get(("u",b),[]): a()
        ex_g1[b].wait_recv()
        gh=mine+oprv[b*R:(b+1)*R,:].astype(jnp.float32)
        tok_load(b).wait()
        t=tokb[b%2].astype(jnp.float32)
        n,r=norm_block(t,None)
        gn=gh*g1
        part=jnp.sum((gh*n).reshape(R//8,8,D),axis=0)
        gsum=part if gsum is None else gsum+part
        gm_v[b*R:(b+1)*R,:]=(gm_v[b*R:(b+1)*R,:].astype(jnp.float32)+r*(gn-n*jnp.mean(gn*n,axis=-1,keepdims=True))).astype(jnp.bfloat16)
        if b+2<NB//2: tok_load(b+2).start()
        @pl.when(off)
        def _(): sw_gt[b].start()
        @pl.when(diag)
        def _(): lo_gt[b].start()
    gain_v[0,0:8,:]=gsum
    ex_gain[0].start()
    last=plan.get("end",[])
    gain_steps=len(names)
    def gain_step(i):
        ex_gain[i].wait_recv()
        prev=gain_v[0] if i==0 else gain_v[2*i]
        gain_v[2*i+2]=prev+gain_v[2*i+1]
        if i+1<gain_steps: ex_gain[i+1].start()
    gi=0
    for i,a in enumerate(last):
        a()
        if i%3==2 and gi<gain_steps: gain_step(gi); gi+=1
    while gi<gain_steps: gain_step(gi); gi+=1
    gout=pltpu.make_async_copy(gain_v.at[2*gain_steps],gains_o,blk_sem.at[0])
    gout.start()
    for g in gathers.values(): g.drain()
    for r in runs.values(): r.drain_sends()
    gout.wait()
    for c in ex_g1+ex_gain: c.wait_send()
    @pl.when(off)
    def _():
        for c in sw_out+sum(sw_gf,[])+sw_gt: c.wait()
    @pl.when(diag)
    def _():
        for c in lo_out+sum(lo_gf,[])+lo_gt: c.wait()

def FF_TILES(rows,W,D):
    return (rows-4*W*D//128)//(3*D)

def back(groups,length8,tok,pa,pb,og,op,opr,gh,ghr,att,rest,leaf,q,k,m,wq,wk,wv,wo,lse,g1,g2,tables,tiles):
    bf=jnp.bfloat16; f32=jnp.float32; S=jax.ShapeDtypeStruct; V=pltpu.VMEM
    N,D=tok.shape; half=N//2; W=wo.shape[0]; NP=W//128; R=256
    rows=3*tiles*D+W*D//128+3*W*D//128
    levels=1+int(math.log2(groups))
    per=lambda n:sum(n>>(l+1) for l in range(levels))
    recv=sum(per(r[4]) for r in runs_of(tiles,D//128) if r[0]>=2)+per(W*D//128)+NP*per(3*D)
    anyb=pl.BlockSpec(memory_space=pl.ANY); vm=pl.BlockSpec(memory_space=pltpu.VMEM)
    outs=[S((half,D),bf),S((half,D),bf),S((N,W),bf),S((rows,128),bf),S((16,D),f32)]
    gains=2*(2+levels-1)+1
    scratch=[V((2,R,D),bf)]*7+[V((2,R,W),bf),V((half,D),bf),V((half,D),bf),V((half,D),bf),V((N,D),bf),V((half,D),bf),V((NP,N,128),bf),V((NP,8,N),f32),
        V((NP,N,128),bf),V((NP,N,128),bf),V((NP,N,128),bf),V((4,N,128),bf),V((4,N,128),bf),V((2,N,128),bf),V((N,128),f32),V((N,128),f32),V((N,128),f32),
        V((W,D),bf),V((W,D),f32),V(rest.shape,bf),V(leaf.shape,bf),V((recv,128),bf),V((W*D//128,128),bf),V((NP,3*D,128),bf),V((gains,16,D),f32),
        pltpu.SemaphoreType.DMA((192,)),pltpu.SemaphoreType.DMA((192,)),pltpu.SemaphoreType.DMA((64,)),pltpu.SemaphoreType.DMA((18,))]
    return pl.pallas_call(functools.partial(back_kernel,groups),out_shape=outs,
        in_specs=[vm]+[anyb]*18+[vm]*7,out_specs=[anyb]*5,scratch_shapes=scratch,
        compiler_params=pltpu.CompilerParams(collective_id=1,has_side_effects=True,vmem_limit_bytes=63<<20),name="back")(
        length8,tok,pa,pb,og,op,opr,gh,ghr,att,rest,leaf,q,k,m,wq,wk,wv,wo,lse,g1,g2,*tables)

BACK_PLAN={
    ('m', 7):[('c1','g',0)],
    (0, 0):[('a2','f',0),('b3','f',0),('a0','g',0),('a1','g',0),('b0','g',0)],
    (0, 3):[('b1','g',0),('out','s',0)],
    (0, 4):[('out','s',1)],
    (0, 5):[('out','s',2)],
    (0, 6):[('b3','f',1),('out','s',3)],
    (0, 7):[('C','f',0),('out','s',4)],
    (0, 8):[('a0','g',1),('out','s',5)],
    (0, 9):[('b0','g',1),('out','s',6)],
    (1, 0):[('C','f',1),('a2','f',1),('a1','g',1),('out','s',7)],
    (1, 1):[('b1','g',1),(('gf',0),'s',0)],
    (1, 2):[('a0','g',2),(('gf',0),'s',1)],
    (1, 3):[('b3','f',2)],
    (1, 4):[('c1','g',1)],
    (1, 6):[('C','f',2)],
    (1, 7):[('b0','g',2),('a0','g',3)],
    (1, 9):[('a2','f',2)],
    (2, 1):[(0,'f',0),('b0','g',3),(('gf',1),'s',0)],
    (2, 2):[(('gf',1),'s',1)],
    (2, 3):[('b1','g',2),('c1','g',2)],
    (2, 4):[(0,'f',1),('a2','f',3)],
    (2, 5):[('b3','f',3),('a1','g',2)],
    (2, 6):[('C','f',3),('a2','g',0)],
    (2, 7):[(0,'f',2),('b3','g',0),('b1','g',3),('c1','g',3)],
    (2, 8):[('C','g',0),('a1','g',3)],
    (3, 0):[(1,'f',0)],
    (3, 1):[(0,'f',3),(0,'g',0),('b3','g',1),(('gf',2),'s',0)],
    (3, 2):[('a2','g',1),(('gf',2),'s',1)],
    (3, 3):[('C','g',1)],
    (3, 5):[(1,'f',1),(1,'f',2)],
    (3, 8):[(2,'f',0)],
    ('t', 0):[(0,'g',1),('a2','g',2),('b3','g',2),(('gf',3),'s',0)],
    ('t', 1):[(2,'f',1),(('gf',3),'s',1)],
    ('t', 3):[('C','g',2)],
    ('u', 1):[(2,'f',2),(1,'f',3),('a2','g',3)],
    ('u', 3):[(1,'g',0)],
}
BACK_END=[
    ('b3','g',3),(3,'f',0),(0,'g',2),('C','g',3),(2,'f',3),(1,'g',1),(3,'f',1),(1,'g',2),
    (0,'g',3),(1,'g',3),(2,'g',0),(3,'f',2),(2,'g',1),(3,'f',3),(3,'g',0),(2,'g',2),
    (3,'g',1),(2,'g',3),(3,'g',2),(3,'g',3),
]

def unpack_kernel(jobs,slots,*refs):
    src=refs[0]; n=max(j[2] for j in jobs)+1
    outs=refs[4:4+n]; raw,wide,in_sem,out_sem,r0,r1,r2,row_in,row_out=refs[4+n+3:]
    rows_in=[pltpu.make_async_copy(a,b,row_in.at[i]) for i,(a,b) in enumerate(zip(refs[1:4],(r0,r1,r2)))]
    rows_out=[pltpu.make_async_copy(b,a,row_out.at[i]) for i,(a,b) in enumerate(zip(refs[4+n:4+n+3],(r0,r1,r2)))]
    for c in rows_in: c.start()
    load=lambda i:pltpu.make_async_copy(src.at[pl.ds(jobs[i][0],jobs[i][1])],raw.at[i%slots,pl.ds(0,jobs[i][1])],in_sem.at[i%slots])
    def store(i):
        _,rows,out,row,col=jobs[i]
        return pltpu.make_async_copy(wide.at[i%slots,pl.ds(0,rows)],outs[out].at[pl.ds(row,rows),pl.ds(col*128,128)],out_sem.at[i%slots])
    for i in range(min(slots,len(jobs))): load(i).start()
    for i in range(len(jobs)):
        rows=jobs[i][1]
        load(i).wait()
        if i>=slots: store(i-slots).wait()
        wide[i%slots,0:rows,:]=raw[i%slots,0:rows,:].astype(jnp.float32)
        store(i).start()
        if i+slots<len(jobs): load(i+slots).start()
        if i==len(jobs)//4:
            for a,b in zip(rows_in,rows_out): a.wait(); b.start()
    for i in range(max(0,len(jobs)-slots),len(jobs)): store(i).wait()
    for c in rows_out: c.wait()

def unpack_all(buf,rows,D,FH,W):
    t=FH//128; n=W//128; d=D//128; slots=8
    jobs=[]; pos=0; first=0
    for m in passes_of(t):
        jobs+=[(pos+(j*m+c)*D,D,j,0,first+c) for j in range(2) for c in range(m)]; pos+=2*m*D
        jobs+=[(pos+c*128*m,128*m,2,first*128,c) for c in range(d)]; pos+=d*128*m
        first+=m
    jobs+=[(pos+c*W,W,3,0,c) for c in range(d)]; pos+=d*W
    jobs+=[(pos+(p*3+j)*D,D,4+j,0,p) for p in range(n) for j in range(3)]
    shapes=[(D,FH),(D,FH),(FH,D),(W,D),(D,W),(D,W),(D,W)]
    most=max(j[1] for j in jobs)
    anyb=pl.BlockSpec(memory_space=pl.ANY)
    return pl.pallas_call(functools.partial(unpack_kernel,jobs,slots),in_specs=[anyb]*4,out_specs=[anyb]*10,
        out_shape=[jax.ShapeDtypeStruct(s,jnp.float32) for s in shapes]+[jax.ShapeDtypeStruct(r.shape,r.dtype) for r in rows],
        scratch_shapes=[pltpu.VMEM((slots,most,128),jnp.bfloat16),pltpu.VMEM((slots,most,128),jnp.float32),pltpu.SemaphoreType.DMA((slots,)),pltpu.SemaphoreType.DMA((slots,))]
            +[pltpu.VMEM(r.shape,r.dtype) for r in rows]+[pltpu.SemaphoreType.DMA((3,)),pltpu.SemaphoreType.DMA((3,))],
        compiler_params=pltpu.CompilerParams(vmem_limit_bytes=60<<20),name="unpack")(buf,*rows)

def per_device(groups,tokens,first_values,out_grad,lengths,gain_attn,gain_mlp,w_query,w_key,w_value,w_out,w_gate,w_up,w_down):
    bf=jnp.bfloat16; f32=jnp.float32
    n=groups
    D=tokens.shape[1]
    g1=gain_attn.reshape(1,D); g2=gain_mlp.reshape(1,D)
    lanes=jnp.arange(128)%(HEAD_DIM//2)
    frequency=jnp.exp(lanes.astype(f32)*(-2.0*math.log(10000.0)/HEAD_DIM))
    coarse=(jnp.arange(SLOT//32)*32).astype(f32)[:,None]*frequency[None,:]
    fine=jnp.arange(32).astype(f32)[:,None]*frequency[None,:]
    tables=(jnp.cos(coarse),jnp.sin(coarse),jnp.cos(fine),jnp.sin(fine))
    length8=jnp.broadcast_to(lengths.reshape(1,1),(8,128))
    (tok,og,len_full,q,k,mixed,att,lse,pa,pb,w_q,w_k,w_v,w_o,w_g,w_u,w_d)=front(n,tokens,first_values,out_grad,length8,g1,tables,(w_query,w_key,w_value,w_out,w_gate,w_up,w_down))
    op,opr,gh,ghr,rest,leaf=mlp(n,len_full,tok,pa,pb,og,g2,(w_gate,w_up,w_down),(w_g,w_u,w_d))
    out,grad_tokens,grad_first,packed,gains=back(n,len_full,tok,pa,pb,og,op,opr,gh,ghr,att,rest,leaf,q,k,mixed,w_q,w_k,w_v,w_o,lse,g1,g2,tables,w_gate.shape[1]//128)
    gains=jnp.sum(gains.reshape(2,8,D),axis=1)
    FH=w_gate.shape[1]; W=w_query.shape[1]
    gwg,gwu,gwd,gwo,gwq,gwk,gwv,out,grad_tokens,grad_first=unpack_all(packed,(out,grad_tokens,grad_first),D,FH,W)
    return (out,grad_tokens,grad_first,gains[0],gains[1],gwq,gwk,gwv,gwo,gwg,gwu,gwd)

def solution(mesh):
    fine=Mesh(mesh.devices.reshape(-1,2,2),ALL)
    rows=P(ALL,None); slot=P(("zy","core"),"head"); col=P(None,"head"); row=P("head",None)
    return jax.shard_map(functools.partial(per_device,fine.devices.shape[0]),mesh=fine,
        in_specs=(rows,slot,rows,P(("zy","core")),P(),P(),col,col,col,row,col,col,row),
        out_specs=(rows,rows,slot,P(),P(),col,col,col,row,col,col,row),check_vma=False)
```

```python
import functools, math
import jax, jax.numpy as jnp
from jax import lax
from jax.experimental import pallas as pl
from jax.experimental.pallas import tpu as pltpu
from jax.sharding import Mesh, PartitionSpec as P
SLOT=2048; HEAD_DIM=64
C2=math.log2(math.e)/8.0
NT=(((1,),(1,)),((),()))
TN=(((0,),(0,)),((),()))
NN=(((1,),(0,)),((),()))
def dot(a,b,dims=NN): return lax.dot_general(a,b,dims,preferred_element_type=jnp.float32)

EPS=1e-5
R2=256
def norm_block(x,gain):
    r=lax.rsqrt(jnp.mean(x*x,axis=-1,keepdims=True)+EPS)
    n=x*r
    return n,r
def rot(x,cos,sin,lane_first):
    up=pltpu.roll(x,96,1)
    dn=pltpu.roll(x,32,1)
    return x*cos+jnp.where(lane_first,up,dn)*sin


ALL=("zy","core","head")

class Links:
    def __init__(self,send,recv,local):
        self.send,self.recv,self.local=send,recv,local
        self.remote_count=0; self.local_count=0
    def remote(self,src,dst,device):
        at=self.remote_count; self.remote_count+=1
        return pltpu.make_async_remote_copy(src_ref=src,dst_ref=dst,send_sem=self.send.at[at],recv_sem=self.recv.at[at],
            device_id=device,device_id_type=pl.DeviceIdType.MESH)
    def copy(self,src,dst):
        at=self.local_count; self.local_count+=1
        return pltpu.make_async_copy(src,dst,self.local.at[at])

def spread_bits(groups):
    count=min(groups,8); bits=[]
    while count>1:
        count//=2; bits.append(count)
    return bits

class Spread:
    def __init__(self,links,home,full,bits,zy,swap_dev,peer):
        m=2**len(bits); rows=home.shape[0]//m
        place=0
        for level,b in enumerate(bits): place=place+((zy//b)%2)*(2**level)
        one=pl.ds(pl.multiple_of(place*rows,rows),rows)
        self.steps=[links.remote(home.at[one],full.at[one],swap_dev)]
        for level,b in enumerate(bits):
            size=2**level
            block=pl.ds(pl.multiple_of((place//size)*size*rows,size*rows),size*rows)
            self.steps.append(links.remote(full.at[block],full.at[block],peer(b)))

def front_kernel(groups,
        tok_h,fv_h,og_h,len_h,g_ref,ch_ref,sh_ref,cl_ref,sl_ref,wq_h,wk_h,wv_h,wo_h,wg_h,wu_h,wd_h,
        tok_o,og_o,len_o,q_o,k_o,m_o,att_o,lse_o,pa_o,pb_o,wq_o,wk_o,wv_o,wo_o,wg_o,wu_o,wd_o,
        tok_v,len_v,fv_v,wq_v,wk_v,wv_v,wo_v,cos_v,sin_v,qs,ks,vp,ms,kb_ref,s_ref,att_v,lse_v,pa_v,
        send_sem,recv_sem,local_sem):
    zy=lax.axis_index("zy"); core=lax.axis_index("core"); x=lax.axis_index("head")
    off=core!=x; diag=core==x
    L=Links(send_sem,recv_sem,local_sem)
    swap_dev=(zy,1-core,1-x); core_dev=(zy,1-core,x)
    bits=spread_bits(groups)
    peer=lambda b:(zy+b-2*b*((zy//b)%2),core,x)
    barrier=pltpu.get_barrier_semaphore()
    MESH=pl.DeviceIdType.MESH
    half=tok_h.shape[0]; D=tok_h.shape[1]; W=wq_h.shape[1]; NP=W//128
    CH=256; NC=half//CH
    sp={n:Spread(L,h,f,bits,zy,swap_dev,peer) for n,h,f in (("q",wq_h,wq_v),("k",wk_h,wk_v),("v",wv_h,wv_v),("o",wo_h,wo_v),("g",wg_h,wg_o),("u",wu_h,wu_o),("d",wd_h,wd_o))}
    mine=lambda k:pl.ds(pl.multiple_of(core*half+k*CH,CH),CH)
    swap_len=L.remote(len_h,len_v,swap_dev)
    there=lambda k:pl.ds(pl.multiple_of((1-core)*half+k*CH,CH),CH)
    swap_tok=[L.remote(tok_h.at[pl.ds(k*CH,CH)],tok_v.at[there(k)],swap_dev) for k in range(NC)]
    core_tok=[L.remote(tok_v.at[mine(k)],tok_v.at[mine(k)],core_dev) for k in range(NC)]
    swap_fv=[L.remote(fv_h.at[:,pl.ds(p*128,128)],fv_v.at[p],swap_dev) for p in range(NP)]
    HH=half//2
    part=lambda c,j:pl.ds(pl.multiple_of(c*half+j*HH,HH),HH)
    swap_og=[L.remote(og_h.at[pl.ds(j*HH,HH)],og_o.at[part(1-core,j)],swap_dev) for j in range(2)]
    my_half=pl.ds(pl.multiple_of(core*half,half),half)
    core_og=[L.remote(og_o.at[part(core,j)],og_o.at[part(core,j)],core_dev) for j in range(2)]
    PR=512
    core_pa=[L.remote(pa_v.at[pl.ds(r*PR,PR)],pb_o.at[pl.ds(r*PR,PR)],core_dev) for r in range(SLOT//PR)]
    out_pa=[L.copy(pa_v.at[pl.ds(r*PR,PR)],pa_o.at[pl.ds(r*PR,PR)]) for r in range(SLOT//PR)]
    own_tok=L.copy(tok_h,tok_v.at[my_half])
    own_len=L.copy(len_h,len_v)
    own_fv=[L.copy(fv_h.at[:,pl.ds(p*128,128)],fv_v.at[p]) for p in range(NP)]
    own_og=[L.copy(og_h,pa_v.at[pl.ds(0,half)]),L.copy(pa_v.at[pl.ds(0,half)],og_o.at[my_half])]
    core_og_own=[L.remote(og_h.at[pl.ds(j*HH,HH)],og_o.at[part(core,j)],core_dev) for j in range(2)]
    own_qkv=[L.copy(h,v) for h,v in ((wq_h,wq_v),(wk_h,wk_v),(wv_h,wv_v))]
    own_o=L.copy(wo_h,wo_v)
    outs=[L.copy(a,b) for a,b in ((tok_v,tok_o),(len_v,len_o),(qs,q_o),(ks,k_o),(wq_v,wq_o),(wk_v,wk_o),(wv_v,wv_o))]
    outs2=[L.copy(a,b) for a,b in ((ms,m_o),(att_v,att_o),(lse_v,lse_o),(wo_v,wo_o))]

    pl.semaphore_signal(barrier,inc=1,device_id=core_dev,device_id_type=MESH)
    @pl.when(off)
    def _():
        pl.semaphore_signal(barrier,inc=1,device_id=swap_dev,device_id_type=MESH)
        for b in bits: pl.semaphore_signal(barrier,inc=1,device_id=peer(b),device_id_type=MESH)
        pl.semaphore_wait(barrier,2+len(bits))
        for n in "qkvg": sp[n].steps[0].start()
        swap_len.start()
        for c in swap_tok: c.start()
        for n in "oud": sp[n].steps[0].start()
        for c in swap_fv+swap_og: c.start()
    @pl.when(diag)
    def _():
        pl.semaphore_wait(barrier,1)
        own_tok.start(); own_len.start()
        for c in own_qkv: c.start()
        own_tok.wait()
        for k in range(NC): core_tok[k].start()
        own_len.wait()
        for c in own_fv: c.start()
        own_o.start(); own_og[0].start()
        for c in core_og_own: c.start()
    sign=jnp.where((lax.broadcasted_iota(jnp.int32,(1,128),1)%64)<32,-1.0,1.0)
    cl=cl_ref[...]; sl=sl_ref[...]
    def table(a,_):
        rows=pl.ds(pl.multiple_of(a*32,32),32)
        ch=ch_ref[pl.ds(a,1),:]; sh=sh_ref[pl.ds(a,1),:]
        cos_v[rows,:]=ch*cl-sh*sl
        sin_v[rows,:]=(sh*cl+ch*sl)*sign
        return 0
    lax.fori_loop(0,SLOT//32,table,0)
    nl=len(bits)
    def advance(n,level):
        if level<nl:
            sp[n].steps[level].wait_recv(); sp[n].steps[level+1].start()
    @pl.when(off)
    def _():
        for n,level in (("q",0),("k",0),("v",0),("q",1),("k",1),("g",0),("v",1),("q",2),("k",2),("v",2),("g",1)): advance(n,level)
        swap_len.wait_recv()
    @pl.when(diag)
    def _():
        for c in own_qkv: c.wait()
        own_og[0].wait(); own_og[1].start()
    gain=g_ref[...]
    lf=(lax.broadcasted_iota(jnp.int32,(CH,128),1)%64)<32
    def project(block):
        rows=pl.ds(pl.multiple_of(block*CH,CH),CH)
        t=tok_v[rows,:].astype(jnp.float32)
        n,_=norm_block(t,None)
        h=(n*gain).astype(jnp.bfloat16)
        cos=cos_v[rows,:]; sin=sin_v[rows,:]
        for w,o in ((wq_v,qs),(wk_v,ks)):
            y=dot(h,w[...])
            for c in range(NP):
                o[c,rows,:]=rot(y[:,c*128:(c+1)*128],cos,sin,lf).astype(jnp.bfloat16)
        y=dot(h,wv_v[...])
        for c in range(NP): vp[c,rows,:]=y[:,c*128:(c+1)*128]
    for k in range(NC):
        if k==0:
            @pl.when(off)
            def _():
                for n in "qkv": sp[n].steps[nl].wait_recv()
        @pl.when(off)
        def _():
            core_tok[k].wait_recv()
        project(x*NC+k)
        @pl.when(off)
        def _():
            if k==0: advance("g",2)
            if k==1: advance("u",0); advance("o",0)
            if k==3: advance("d",0)
    for k in range(NC):
        @pl.when(off)
        def _():
            swap_tok[k].wait_recv()
            core_tok[k].start()
            if k==3: advance("u",1)
        @pl.when(diag)
        def _():
            core_tok[k].wait_recv()
        project((1-x)*NC+k)
    for c in outs: c.start()
    plan={}
    todo=lambda slot,act: plan.setdefault(slot,[]).append(act)
    for slot,n,level in ((0,"o",1),(2,"d",1),(4,"u",2),(5,"o",2),(8,"d",2)): todo(slot,functools.partial(advance,n,level))
    todo(11,lambda:(swap_og[0].wait_recv(),core_og[0].start()))
    BQ,BK=512,512
    laneq=lax.broadcasted_iota(jnp.int32,(BQ,128),1)
    lane=lax.broadcasted_iota(jnp.int32,(SLOT,128),1)
    row=lax.broadcasted_iota(jnp.int32,(SLOT,128),0)
    def pair(p,_):
        for at in range(NP):
            @pl.when((p==at)&off)
            def _(): swap_fv[at].wait_recv()
            @pl.when((p==at)&diag)
            def _(): own_fv[at].wait()
        m=(0.5*vp[p]+0.5*fv_v[p].astype(jnp.float32)).astype(jnp.bfloat16)
        ms[p]=m
        k=ks[p]
        length=len_v[0:1,:]
        for h in range(2):
            own=(lane//64)==h
            first=lane==(64*(1-h))
            bias=jnp.where(first&(row>=length),-1e30,0.0).astype(jnp.bfloat16)
            kb_ref[h]=jnp.where(own,k,bias)
            kb_ref[2+h]=jnp.where(own,m,jnp.ones_like(m))
        for i in range(SLOT//BQ):
            for at in range(NP):
                acts=plan.get(at*4+i)
                if acts:
                    @pl.when((p==at)&off)
                    def _():
                        for a in acts: a()
            rows=slice(i*BQ,(i+1)*BQ)
            q=qs[p,rows,:]
            got=[]
            for h in range(2):
                own=(laneq//64)==h
                qh=jnp.where(own,q,jnp.ones_like(q))
                mx=None
                for j in range(i+1):
                    s=dot(qh,kb_ref[h,pl.ds(j*BK,BK),:],NT)
                    if j==i:
                        r=lax.broadcasted_iota(jnp.int32,(BQ,BK),0); c=lax.broadcasted_iota(jnp.int32,(BQ,BK),1)
                        s=jnp.where(c<=r,s,-1e30)
                    s_ref[h,:,pl.ds(j*BK,BK)]=s
                    m_=jnp.max(s,axis=-1,keepdims=True)
                    mx=m_ if mx is None else jnp.maximum(mx,m_)
                mc=mx*C2
                acc=None
                for j in range(i+1):
                    pr=jnp.exp2(s_ref[h,:,pl.ds(j*BK,BK)]*C2-mc).astype(jnp.bfloat16)
                    a=dot(pr,kb_ref[2+h,pl.ds(j*BK,BK),:])
                    acc=a if acc is None else acc+a
                other=64*(1-h)
                l=acc[:,other:other+1]
                got.append((acc/l,mc+jnp.log2(l)))
            att_v[rows,pl.ds(pl.multiple_of(p*128,128),128)]=jnp.where((laneq//64)==0,got[0][0],got[1][0]).astype(jnp.bfloat16)
            lse_v[p,:,i*BQ:(i+1)*BQ]=jnp.where(lax.broadcasted_iota(jnp.int32,(BQ,128),1)==0,got[0][1],got[1][1]).T[0:8]
        return 0
    lax.fori_loop(0,NP,pair,0)
    @pl.when(off)
    def _():
        sp["o"].steps[nl].wait_recv()
        swap_og[1].wait_recv(); core_og[1].start()
    @pl.when(diag)
    def _():
        own_o.wait(); own_og[1].wait()
    for c in outs2: c.start()
    for r in range(SLOT//PR):
        pa_v[r*PR:(r+1)*PR,:]=dot(att_v[r*PR:(r+1)*PR,:],wo_v[...]).astype(jnp.bfloat16)
        core_pa[r].start(); out_pa[r].start()
    for c in outs+outs2+out_pa: c.wait()
    for c in core_pa: c.wait()
    for k in range(NC): core_tok[k].wait_send()
    @pl.when(diag)
    def _():
        for c in core_og_own: c.wait_send()
        for c in core_og: c.wait_recv()
    @pl.when(off)
    def _():
        for c in core_og: c.wait_send()
        for c in core_og_own: c.wait_recv()
        for n in "gud": sp[n].steps[nl].wait_recv()
        for n in "qkvogud":
            for s in sp[n].steps: s.wait_send()
        swap_len.wait_send()
        for c in swap_tok+swap_fv+swap_og: c.wait_send()

def front(groups,tok,fv,og,length,gain,tables,ws):
    N=SLOT; D=tok.shape[1]; W=ws[0].shape[1]; NP=W//128; FH=ws[4].shape[1]
    bf=jnp.bfloat16; f32=jnp.float32
    S=jax.ShapeDtypeStruct
    outs=[S((N,D),bf),S((N,D),bf),S((8,128),jnp.int32),S((NP,N,128),bf),S((NP,N,128),bf),S((NP,N,128),bf),S((N,W),bf),S((NP,8,N),f32),S((N,D),bf),S((N,D),bf)]+[S(w.shape,bf) for w in ws]
    anyb=pl.BlockSpec(memory_space=pl.ANY); vm=pl.BlockSpec(memory_space=pltpu.VMEM)
    V=pltpu.VMEM
    scratch=[V((N,D),bf),V((8,128),jnp.int32),V((NP,N,128),bf),V((D,W),bf),V((D,W),bf),V((D,W),bf),V((W,D),bf),V((N,128),f32),V((N,128),f32),
        V((NP,N,128),bf),V((NP,N,128),bf),V((NP,N,128),f32),V((NP,N,128),bf),V((4,N,128),bf),V((2,512,N),f32),V((N,W),bf),V((NP,8,N),f32),V((N,D),bf),
        pltpu.SemaphoreType.DMA((56,)),pltpu.SemaphoreType.DMA((56,)),pltpu.SemaphoreType.DMA((32,))]
    return pl.pallas_call(functools.partial(front_kernel,groups),out_shape=outs,
        in_specs=[anyb]*4+[vm]*5+[anyb]*7,out_specs=[anyb]*len(outs),scratch_shapes=scratch,
        compiler_params=pltpu.CompilerParams(collective_id=0,has_side_effects=True,vmem_limit_bytes=58<<20),name="front")(tok,fv,og,length,gain,*tables,*ws)

class Reduce:
    def __init__(self,links,order,src,offset,rows,recv,recv_at,at,keep=None):
        self.order=order; self.rows=rows; self.offset=offset; self.at=at; self.then=None
        self.keep=src if keep is None else keep
        self.levels=len(order); self.leaf=rows>>self.levels; self.bufs=[]; self.sends=[]
        for level,name in enumerate(order):
            size=rows>>(level+1); bit=at.bit(name)
            self.bufs.append(recv.at[pl.ds(recv_at,size)]); recv_at+=size
            if level==0: source=src.at[pl.ds(pl.multiple_of(offset+(1-bit)*size,16),size)]
            else: source=self.bufs[level-1].at[pl.ds(pl.multiple_of((1-bit)*size,16),size)]
            self.sends.append(links.remote(source,self.bufs[level],at.partner(name)))
        self.recv_end=recv_at
    def start(self): self.sends[0].start()
    def finish(self,level):
        self.sends[level].wait_recv()
        size=self.rows>>(level+1); bit=self.at.bit(self.order[level])
        into=self.bufs[level]
        if level==0: mine=self.keep.at[pl.ds(pl.multiple_of(self.offset+bit*size,16),size)]
        else: mine=self.bufs[level-1].at[pl.ds(pl.multiple_of(bit*size,16),size)]
        step=math.gcd(size,512)
        def add(i,_):
            rows=pl.ds(pl.multiple_of(i*step,step),step)
            into[rows,:]=(into[rows,:].astype(jnp.float32)+mine[rows,:].astype(jnp.float32)).astype(jnp.bfloat16)
            return 0
        lax.fori_loop(0,size//step,add,0)
        if level+1<self.levels: self.sends[level+1].start()
        elif self.then is not None: self.then()
    def drain_sends(self):
        for c in self.sends: c.wait_send()

class Gather:
    def __init__(self,links,order,leaf,rows,result,result_at,at):
        self.at=at; self.steps=len(order); size=rows>>self.steps
        weight={name:rows>>(i+1) for i,name in enumerate(order)}
        own=sum(at.bit(name)*weight[name] for name in order)
        spot=result.at[pl.ds(pl.multiple_of(result_at+own,16),size)]
        self.swap=links.remote(leaf,spot,at.swap)
        self.keep=links.copy(leaf,spot)
        self.gathers=[]; gathered=[]
        for name in sorted([n for n in order if n!="x"],reverse=True)+["x"]:
            unit=size; apart=[]
            for w in sorted(gathered):
                if w==unit: unit*=2
                else: apart.append(w)
            base=sum((at.core if n=="x" else at.bit(n))*weight[n] for n in order if weight[n] not in gathered)
            combos=[0]
            for w in apart: combos=combos+[c+w for c in combos]
            device=at.core_dev if name=="x" else at.partner(name)
            step=[]
            for c in combos:
                block=result.at[pl.ds(pl.multiple_of(result_at+base+c,16),unit)]
                step.append(links.remote(block,block,device))
            self.gathers.append(step); gathered.append(weight[name])
    def begin(self):
        @pl.when(self.at.off)
        def _(): self.swap.start()
        @pl.when(self.at.diag)
        def _(): self.keep.start()
    def go(self,step):
        if step==0:
            @pl.when(self.at.off)
            def _(): self.swap.wait_recv()
            @pl.when(self.at.diag)
            def _(): self.keep.wait()
        else:
            for c in self.gathers[step-1]: c.wait_recv()
        for c in self.gathers[step]: c.start()
    def drain(self):
        for c in self.gathers[-1]: c.wait_recv()
        @pl.when(self.at.off)
        def _(): self.swap.wait_send()
        for s in self.gathers:
            for c in s: c.wait_send()

class Place: pass
def place_of(groups):
    at=Place()
    at.zy=lax.axis_index("zy"); at.core=lax.axis_index("core"); at.x=lax.axis_index("head")
    at.off=at.core!=at.x; at.diag=at.core==at.x
    at.bit=lambda name: at.x if name=="x" else (at.zy//name)%2
    at.partner=lambda name: (at.zy,at.core,1-at.x) if name=="x" else (at.zy+name-2*name*((at.zy//name)%2),at.core,at.x)
    at.swap=(at.zy,1-at.core,1-at.x); at.core_dev=(at.zy,1-at.core,at.x)
    at.bits=[]
    b=1
    while b<groups: at.bits.append(b); b*=2
    return at

def passes_of(tiles):
    a=(4*tiles+10)//11; b=(3*tiles+10)//11; c=(tiles-a-b+1)//2
    return (a,b,c,tiles-a-b-c)
def runs_of(tiles,d_tiles):
    KB=1024; pos=0; out=[]
    for t,n in enumerate(passes_of(tiles)):
        units=(2*n*d_tiles*128+d_tiles*128*n)//KB
        parts=[[units//3,units//3,units-2*(units//3)],[units//3,units//3,units-2*(units//3)],[units],[0,units]][t]
        for i,u in enumerate(parts):
            if u: out.append((t,"abc"[i]+str(t),i,pos,u*KB))
            pos+=u*KB
    return out
def orders_of(bits):
    return [["x"]+bits,bits[:1]+["x"]+bits[1:],bits[1:2]+bits[:1]+["x"]+bits[2:]]

MLP_PLAN={
    (1, 6):[('a0',0),('b0',0),('c0',0)],
    (2, 1):[('a0',1),('b0',1)],
    (2, 4):[('c0',1)],
    (2, 6):[('a1',0),('c1',0)],
    (2, 7):[('b1',0),('a0',2),('c0',2)],
    (3, 0):[('b0',2)],
    (3, 1):[('a1',1),('a0',3)],
    (3, 2):[('b1',1)],
    (3, 3):[('c1',1),('c0',3)],
    (3, 4):[('b0',3)],
    (3, 5):[('a1',2)],
    (3, 6):[('b1',2),('c1',2)],
    (3, 7):[('a1',3)],
}
def mlp_kernel(groups,len_ref,tok_h,pa_h,pb_h,og_h,g_ref,wg_h,wu_h,wd_h,wg_f,wu_f,wd_f,
        op_o,opr_o,gh_o,ghr_o,rest_o,leaf_o,
        tokb,pab,pbb,h_v,g_v,oacc,gacc,wgu,wd,agu,ad,comb,recv_v,
        send_sem,recv_sem,local_sem,blk_sem,w_sem,out_sem,ex_send,ex_recv):
    at=place_of(groups); core=at.core; diag=at.diag
    MESH=pl.DeviceIdType.MESH
    N,D=tok_h.shape; FH=wg_h.shape[1]; R=256; NB=N//R
    passes=passes_of(FH//128); T=len(passes)
    L=Links(send_sem,recv_sem,local_sem)
    orders=orders_of(at.bits)
    runs={}; rp=0; lp=0; leaves=[]
    for t,name,kind,pos,rows in runs_of(FH//128,D//128):
        if t<2:
            r=Reduce(L,orders[kind],comb,pos,rows,recv_v,rp,at); rp=r.recv_end
            runs[name]=(t,r)
            leaves.append(L.copy(r.bufs[-1],leaf_o.at[pl.ds(lp,r.leaf)])); lp+=r.leaf
    out_rest=L.copy(comb.at[pl.ds(comb.shape[0]-rest_o.shape[0],rest_o.shape[0])],rest_o)
    barrier=pltpu.get_barrier_semaphore()
    partners=[at.core_dev]+[at.partner(n) for n in ["x"]+at.bits]
    for d in partners: pl.semaphore_signal(barrier,inc=1,device_id=d,device_id_type=MESH)
    pl.semaphore_wait(barrier,len(partners))
    firsts=[sum(passes[:t]) for t in range(T)]
    def w_copies(t,src):
        n=passes[t]*128; f=firsts[t]*128; s=t%2
        a,b,c=src
        return [pltpu.make_async_copy(a.at[:,pl.ds(f,n)],wgu.at[s,:,pl.ds(0,n)],w_sem.at[0]),
            pltpu.make_async_copy(b.at[:,pl.ds(f,n)],wgu.at[s,:,pl.ds(n,n)],w_sem.at[1]),
            pltpu.make_async_copy(c.at[pl.ds(f,n)],wd.at[s,pl.ds(0,n)],w_sem.at[2])]
    def w_start(t):
        @pl.when(diag)
        def _():
            for c in w_copies(t,(wg_h,wu_h,wd_h)): c.start()
        @pl.when(at.off)
        def _():
            for c in w_copies(t,(wg_f,wu_f,wd_f)): c.start()
    def w_wait(t):
        for c in w_copies(t,(wg_h,wu_h,wd_h)): c.wait()
    w_start(0)
    rowsof=lambda b:pl.ds(pl.multiple_of(((core*(NB//2)+b)%NB)*R,R),R)
    def loads(b):
        s=b%2
        return [pltpu.make_async_copy(h.at[rowsof(b)],v.at[s],blk_sem.at[s,i]) for i,(h,v) in enumerate(((tok_h,tokb),(pa_h,pab),(pb_h,pbb)))]+[
            pltpu.make_async_copy(og_h.at[rowsof(b)],g_v.at[rowsof(b)],blk_sem.at[s,3])]
    for c in loads(0): c.start()
    w_wait(0)
    gain=g_ref[...]; length=len_ref[0:1,0:1]
    def to_partner(b):
        send=[pltpu.make_async_remote_copy(src_ref=g_v.at[rowsof(b)],dst_ref=ghr_o.at[rowsof(b)],send_sem=ex_send.at[0,b],recv_sem=ex_recv.at[0,b],device_id=at.core_dev,device_id_type=MESH)]
        k=b-NB//2
        last=pltpu.make_async_remote_copy(src_ref=h_v.at[rowsof(b)],dst_ref=opr_o.at[pl.ds(pl.multiple_of(k*R,R),R)],send_sem=ex_send.at[1,b],recv_sem=ex_recv.at[1,b],device_id=at.core_dev,device_id_type=MESH)
        return send,last
    def outs(b): return [pltpu.make_async_copy(h_v.at[rowsof(b)],op_o.at[rowsof(b)],out_sem.at[0,b]),pltpu.make_async_copy(g_v.at[rowsof(b)],gh_o.at[rowsof(b)],out_sem.at[1,b])]
    for t,n in enumerate(passes):
        s=t%2; w=n*128
        def block(b,_):
            for B in range(NB):
                acts=MLP_PLAN.get((t,B))
                if acts:
                    @pl.when(b==B)
                    def _():
                        for name,level in acts:
                            if name in runs and level<runs[name][1].levels: runs[name][1].finish(level)
            rows=rowsof(b)
            if t==0:
                @pl.when(b+1<NB)
                def _():
                    for c in loads(b+1): c.start()
                for c in loads(b): c.wait()
                i=b%2
                x=tokb[i].astype(jnp.float32)+(pab[i].astype(jnp.float32)+pbb[i].astype(jnp.float32))
                nn,_=norm_block(x,None)
                h=(nn*gain).astype(jnp.bfloat16)
                h_v[rows,:]=h
                row=lax.broadcasted_iota(jnp.int32,(R,1),0)+((core*(NB//2)+b)%NB)*R
                g=jnp.where(row<length,g_v[rows,:],jnp.zeros((),jnp.bfloat16))
                g_v[rows,:]=g
            else:
                h=h_v[rows,:]; g=g_v[rows,:]
            gu=dot(h,wgu[s,:,0:2*w])
            gate=gu[:,:w]; up=gu[:,w:]
            gh=dot(g,wd[s,0:w,:],NT)
            sg=0.5*jnp.tanh(0.5*gate)+0.5
            silu=gate*sg
            hid=(silu*up).astype(jnp.bfloat16)
            both=jnp.concatenate([(gh*up*(sg*(1.0+gate*(1.0-sg)))).astype(jnp.bfloat16),(gh*silu).astype(jnp.bfloat16)],axis=1)
            o=dot(hid,wd[s,0:w,:])
            q=dot(both,wgu[s,:,0:2*w],NT)
            da=dot(hid,g,TN); dg=dot(h,both,TN)
            if t==0: oacc[rows,:]=o; gacc[rows,:]=q
            elif t<T-1: oacc[rows,:]+=o; gacc[rows,:]+=q
            else:
                h_v[rows,:]=(oacc[rows,:]+o).astype(jnp.bfloat16)
                g_v[rows,:]=(gacc[rows,:]+q).astype(jnp.bfloat16)
                for c in outs(b): c.start()
                send,last=to_partner(b)
                for c in send: c.start()
                @pl.when(b>=NB//2)
                def _(): last.start()
            @pl.when(b==0)
            def _(): ad[0:w,:]=da; agu[:,0:2*w]=dg
            @pl.when(b>0)
            def _(): ad[0:w,:]+=da; agu[:,0:2*w]+=dg
            if t+1<T:
                @pl.when(b==NB-2)
                def _(): w_start(t+1)
            return 0
        lax.fori_loop(0,NB,block,0)
        base=firsts[t]*(2*D+D)
        for c in range(2*n): comb[base+c*D:base+(c+1)*D,:]=agu[:,c*128:(c+1)*128].astype(jnp.bfloat16)
        base+=2*n*D
        for c in range(D//128): comb[base+c*w:base+(c+1)*w,:]=ad[0:w,c*128:(c+1)*128].astype(jnp.bfloat16)
        for name,(rt,r) in runs.items():
            if rt==t: r.start()
        if t+1<T: w_wait(t+1)
    out_rest.start()
    planned={(a,l) for v in MLP_PLAN.values() for a,l in v}
    queues=[[(r,l) for l in range(r.levels) if (name,l) not in planned] for name,(rt,r) in runs.items()]
    while any(queues):
        for q in queues:
            if q:
                r,l=q.pop(0); r.finish(l)
    for c in leaves: c.start()
    def settle(b,_):
        for c in outs(b): c.wait()
        send,last=to_partner(b)
        for c in send: c.wait()
        @pl.when(b>=NB//2)
        def _(): last.wait()
        return 0
    lax.fori_loop(0,NB,settle,0)
    for c in leaves: c.wait()
    out_rest.wait()
    for _,r in runs.values(): r.drain_sends()

def mlp(groups,length8,tok,pa,pb,og,gain,ws,full):
    bf=jnp.bfloat16; f32=jnp.float32; S=jax.ShapeDtypeStruct; V=pltpu.VMEM
    N,D=tok.shape; FH=ws[0].shape[1]; R=256
    anyb=pl.BlockSpec(memory_space=pl.ANY); vm=pl.BlockSpec(memory_space=pltpu.VMEM)
    levels=1+int(math.log2(groups))
    all_runs=runs_of(FH//128,D//128)
    early=[r for r in all_runs if r[0]<2]
    recv=sum(r[4]>>(l+1) for r in early for l in range(levels))
    leaf=sum(r[4]>>levels for r in early)
    total=sum(r[4] for r in all_runs); rest=sum(r[4] for r in all_runs if r[0]>=2)
    w=max(passes_of(FH//128))*128
    outs=[S((N,D),bf),S((N//2,D),bf),S((N,D),bf),S((N,D),bf),S((rest,128),bf),S((leaf,128),bf)]
    DM=pltpu.SemaphoreType.DMA
    return pl.pallas_call(functools.partial(mlp_kernel,groups),out_shape=outs,in_specs=[vm]+[anyb]*4+[vm]+[anyb]*6,out_specs=[anyb]*6,
        scratch_shapes=[V((2,R,D),bf)]*3+[V((N,D),bf),V((N,D),bf),V((N,D),f32),V((N,D),f32),V((2,D,2*w),bf),V((2,w,D),bf),V((D,2*w),f32),V((w,D),f32),V((total,128),bf),V((recv,128),bf),
            DM((48,)),DM((48,)),DM((16,)),DM((2,4)),DM((3,)),DM((2,N//R)),DM((2,N//R)),DM((2,N//R))],
        compiler_params=pltpu.CompilerParams(collective_id=2,has_side_effects=True,vmem_limit_bytes=63<<20),name="mlp")(length8,tok,pa,pb,og,gain,*ws,*full)

def back_kernel(groups,
        len_ref,tok_h,pa_h,pb_h,og_h,op_h,opr_h,gh_h,ghr_h,att_h,rest_h,leaf_h,q_h,k_h,m_h,wq_h,wk_h,wv_h,wo_h,lse_ref,g1_ref,g2_ref,ch_ref,sh_ref,cl_ref,sl_ref,
        out_o,gt_o,gf_o,res_o,gains_o,
        tokb,pab,pbb,ogb,gab,grb,orb,atb,opb,oprv,ghb,h1_v,gm_v,gat_v,dl_v,qd,kd,md,ks,qs,vs,dqa,cos_v,sin_v,wo_v,acc,src_v,leaf_v,recv_v,gwo_v,gw_v,gain_v,
        send_sem,recv_sem,local_sem,blk_sem):
    at=place_of(groups); core=at.core; off=at.off; diag=at.diag
    L=Links(send_sem,recv_sem,local_sem)
    MESH=pl.DeviceIdType.MESH
    N,D=tok_h.shape; half=N//2; W=wo_h.shape[0]; NP=W//128; R=256; NB=N//R
    bits=at.bits
    orders=orders_of(bits); FH=rest_h.shape[0]; all_runs=runs_of(FF_TILES(res_o.shape[0],W,D),D//128)
    total=sum(r[4] for r in all_runs); rest_at=total-rest_h.shape[0]
    runs={}; gathers={}; rp=0; lp=0
    for t,name,kind,pos,rows in all_runs:
        if t<2:
            size=rows>>(1+len(bits))
            gathers[name]=Gather(L,orders[kind],leaf_v.at[pl.ds(lp,size)],rows,res_o,pos,at); lp+=size
        else: runs[name]=Reduce(L,orders[kind],rest_h,pos-rest_at,rows,recv_v,rp,at,keep=src_v); rp=runs[name].recv_end
    early=list(gathers); late=list(runs)
    runs["C"]=Reduce(L,orders[2],gwo_v,0,gwo_v.shape[0],recv_v,rp,at); rp=runs["C"].recv_end
    for p in range(NP): runs[p]=Reduce(L,orders[2],gw_v.at[p],0,gw_v.shape[1],recv_v,rp,at); rp=runs[p].recv_end
    places={name:(orders[kind],rows,pos) for t,name,kind,pos,rows in all_runs}
    places["C"]=(orders[2],gwo_v.shape[0],total)
    for p in range(NP): places[p]=(orders[2],gw_v.shape[1],total+gwo_v.shape[0]+p*gw_v.shape[1])
    for name,r in runs.items():
        order,rows,pos=places[name]
        gathers[name]=Gather(L,order,r.bufs[-1],rows,res_o,pos,at); r.then=gathers[name].begin
    first_rows=lambda b:pl.multiple_of(((core*(NB//2)+b)%NB)*R,R)
    blk=lambda b:pl.ds(first_rows(b),R)
    theirs=lambda b:pl.ds(pl.multiple_of((((1-core)*(NB//2)+b)%NB)*R,R),R)
    piece=half//8
    sw_out=[L.remote(opb.at[pl.ds(i*piece,piece)],out_o.at[pl.ds(i*piece,piece)],at.swap) for i in range(8)]
    lo_out=[L.copy(opb.at[pl.ds(i*piece,piece)],out_o.at[pl.ds(i*piece,piece)]) for i in range(8)]
    sw_gf=[[L.remote(md.at[p,pl.ds(i*half,half)],gf_o.at[pl.ds(i*half,half),pl.ds(p*128,128)],at.swap) for i in range(2)] for p in range(NP)]
    lo_gf=[[L.copy(md.at[p,pl.ds(i*half,half)],gf_o.at[pl.ds(i*half,half),pl.ds(p*128,128)]) for i in range(2)] for p in range(NP)]
    def home(name,i):
        a,b=(sw_out[i],lo_out[i]) if name=="out" else (sw_gf[name[1]][i],lo_gf[name[1]][i])
        @pl.when(off)
        def _(): a.start()
        @pl.when(diag)
        def _(): b.start()
    ex_g1=[L.remote(ghb.at[pl.ds(b*R,R)],oprv.at[pl.ds(b*R,R)],at.core_dev) for b in range(NB//2)]
    sw_gt=[L.remote(gm_v.at[pl.ds(b*R,R)],gt_o.at[pl.ds(b*R,R)],at.swap) for b in range(NB//2)]
    lo_gt=[L.copy(gm_v.at[pl.ds(b*R,R)],gt_o.at[pl.ds(b*R,R)]) for b in range(NB//2)]
    names=["c","x"]+bits
    ex_gain=[L.remote(gain_v.at[0] if i==0 else gain_v.at[2*i],gain_v.at[2*i+1],at.core_dev if n=="c" else at.partner(n)) for i,n in enumerate(names)]
    loads=[L.copy(a,b) for a,b in ((wo_h,wo_v),(q_h,qd),(k_h,kd),(m_h,md))]
    proj=[L.copy(w.at[pl.ds(i*256,256)],v.at[i//2,:,pl.ds((i%2)*W,W)]) for w,v in ((wq_h,pab),(wk_h,pbb),(wv_h,ogb)) for i in range(D//256)]
    barrier=pltpu.get_barrier_semaphore()
    for d in [at.core_dev]+[at.partner(n) for n in ["x"]+bits]:
        pl.semaphore_signal(barrier,inc=1,device_id=d,device_id_type=MESH)
    @pl.when(off)
    def _():
        pl.semaphore_signal(barrier,inc=1,device_id=at.swap,device_id_type=MESH)
        pl.semaphore_wait(barrier,3+len(bits))
    @pl.when(diag)
    def _(): pl.semaphore_wait(barrier,2+len(bits))
    for name in late: runs[name].start()
    own_rest=L.copy(rest_h,src_v); own_leaf=L.copy(leaf_h,leaf_v)
    own_leaf.start()
    def block_loads(b):
        s=b%2
        pairs=[(tok_h,tokb),(pa_h,pab),(pb_h,pbb),(og_h,ogb),(gh_h,gab),(ghr_h,grb),(att_h,atb)]
        cps=[pltpu.make_async_copy(h.at[blk(b)],v.at[s],blk_sem.at[s*9+i]) for i,(h,v) in enumerate(pairs)]
        if b<NB//2:
            cps.append(pltpu.make_async_copy(op_h.at[blk(b)],opb.at[pl.ds(b*R,R)],blk_sem.at[s*9+7]))
            cps.append(pltpu.make_async_copy(opr_h.at[pl.ds(b*R,R)],orb.at[s],blk_sem.at[s*9+8]))
        return cps
    for c in block_loads(0): c.start()
    for c in loads: c.start()
    own_rest.start()
    own_leaf.wait()
    for name in early: gathers[name].begin()
    sign=jnp.where((lax.broadcasted_iota(jnp.int32,(1,128),1)%64)<32,-1.0,1.0)
    cl=cl_ref[...]; sl=sl_ref[...]
    def table(a,_):
        rows=pl.ds(pl.multiple_of(a*32,32),32)
        ch=ch_ref[pl.ds(a,1),:]; sh=sh_ref[pl.ds(a,1),:]
        cos_v[rows,:]=ch*cl-sh*sl
        sin_v[rows,:]=(sh*cl+ch*sl)*sign
        return 0
    lax.fori_loop(0,N//32,table,0)
    g1=g1_ref[...]; g2=g2_ref[...]
    length=len_ref[0:1,0:1]
    hr=lax.broadcasted_iota(jnp.int32,(8*NP,W),0); ln=lax.broadcasted_iota(jnp.int32,(8*NP,W),1)
    ind=jnp.where(((ln//64)==((hr//8)*2+hr%8))&(hr%8<2),1.0,0.0).astype(jnp.bfloat16)
    loads[0].wait(); own_rest.wait()
    gsum=None
    plan={}
    todo=lambda t,*acts: plan.setdefault(t,[]).extend(acts)
    def action(name,what,level): return functools.partial(runs[name].finish if what=="f" else gathers[name].go,level)
    done=set()
    levels=1+len(bits)
    for key,items in BACK_PLAN.items():
        for item in items:
            if item[1]=="s": todo(key,functools.partial(home,item[0],item[2])); done.add(item)
            elif levels==4 or item[1]=="f": todo(key,action(*item)); done.add(item)
    left=[i for i in BACK_END if levels==4 and i not in done]
    done.update(left)
    for i in range(2*levels):
        for name in list(gathers):
            what,level=("f",i) if i<levels else ("g",i-levels)
            if (what=="g" or name in runs) and (name,what,level) not in done: left.append((name,what,level))
    for item in left: todo("end",action(*item))
    for name,i in [("out",i) for i in range(8)]+[(("gf",p),i) for p in range(NP) for i in range(2)]:
        if (name,"s",i) not in done: todo(("u",0),functools.partial(home,name,i))
    for b in range(NB):
        for a in plan.get(("m",b),[]): a()
        if b+1<NB:
            for c in block_loads(b+1): c.start()
        for c in block_loads(b): c.wait()
        s=b%2; r0=first_rows(b)
        t=tokb[s].astype(jnp.float32)
        n1,_=norm_block(t,None)
        h1_v[blk(b),:]=(n1*g1).astype(jnp.bfloat16)
        mid=t+(pab[s].astype(jnp.float32)+pbb[s].astype(jnp.float32))
        n,r=norm_block(mid,None)
        gh2=gab[s].astype(jnp.float32)+grb[s].astype(jnp.float32)
        row=lax.broadcasted_iota(jnp.int32,(R,1),0)+r0
        mg=jnp.where(row<length,ogb[s].astype(jnp.float32),0.0)
        gn=gh2*g2
        inner=jnp.mean(gn*n,axis=-1,keepdims=True)
        gm=(mg+r*(gn-n*inner)).astype(jnp.bfloat16)
        part=jnp.sum((gh2*n).reshape(R//8,8,D),axis=0)
        gsum=part if gsum is None else gsum+part
        if b<NB//2:
            gm_v[b*R:(b+1)*R,:]=gm
            mine=slice(b*R,(b+1)*R)
            opb[mine,:]=(mid+(opb[mine,:].astype(jnp.float32)+orb[s].astype(jnp.float32))).astype(jnp.bfloat16)
        at_b=atb[s]
        ga=dot(gm,wo_v[...],NT).astype(jnp.bfloat16)
        for p in range(NP): gat_v[p,blk(b),:]=ga[:,p*128:(p+1)*128]
        xx=ga.astype(jnp.float32)*at_b.astype(jnp.float32)
        hi=xx.astype(jnp.bfloat16); lo=(xx-hi.astype(jnp.float32)).astype(jnp.bfloat16)
        dl_v[:,:,blk(b)]=(dot(ind,hi,NT)+dot(ind,lo,NT)).reshape(NP,8,R)
        w=dot(at_b,gm,TN)
        if b==0: acc[...]=w
        else: acc[...]+=w
    for c in range(D//128): gwo_v[c*W:(c+1)*W,:]=acc[:,c*128:(c+1)*128].astype(jnp.bfloat16)
    gain_v[0,8:16,:]=gsum*0.5
    runs["C"].start()
    for c in proj: c.start()
    for c in loads[1:]: c.wait()
    BQ=BK=512
    lane=lax.broadcasted_iota(jnp.int32,(N,128),1)
    rowi=lax.broadcasted_iota(jnp.int32,(N,128),0)
    lf=(lax.broadcasted_iota(jnp.int32,(BK,128),1)%64)<32
    def pair(p,_):
        k=kd[p]; q=qd[p]; do=gat_v[p]
        for h in range(2):
            own=(lane//64)==h
            first=lane==(64*(1-h))
            bias=jnp.where(first&(rowi>=length),-1e30,0.0).astype(jnp.bfloat16)
            ks[h]=jnp.where(own,k,bias)
            ks[2+h]=jnp.where(own,k,jnp.zeros_like(k))
            qs[h]=jnp.where(own,q,jnp.ones_like(q))
            qs[2+h]=jnp.where(own,q,jnp.zeros_like(q))
            vs[h]=jnp.where(own,do,jnp.zeros_like(do))
        dqa[...]=jnp.zeros_like(dqa)
        hook=0
        for j in range(N//BK):
            cols=slice(j*BK,(j+1)*BK)
            v=md[p,cols,:]
            dk=dv=None
            for i in range(j,N//BQ):
                for P_ in range(NP):
                    acts=plan.get((P_,hook))
                    if acts:
                        @pl.when(p==P_)
                        def _():
                            for a in acts: a()
                hook+=1
                rows=slice(i*BQ,(i+1)*BQ)
                for h in range(2):
                    st=dot(ks[h,cols,:],qs[h,rows,:],NT)
                    if i==j:
                        c=lax.broadcasted_iota(jnp.int32,(BK,BQ),0); r=lax.broadcasted_iota(jnp.int32,(BK,BQ),1)
                        st=jnp.where(c<=r,st,-1e30)
                    pt=jnp.exp2(st*C2-lse_ref[p,h:h+1,rows])
                    dpt=dot(v,vs[h,rows,:],NT)
                    dst=(pt*(dpt-dl_v[p,h:h+1,rows])).astype(jnp.bfloat16)
                    a=dot(pt.astype(jnp.bfloat16),vs[h,rows,:])
                    dv=a if dv is None else dv+a
                    b_=dot(dst,qs[2+h,rows,:])
                    dk=b_ if dk is None else dk+b_
                    dqa[rows,:]+=dot(dst,ks[2+h,cols,:],TN)
            kd[p,cols,:]=rot(dk*0.125,cos_v[cols,:],-sin_v[cols,:],lf).astype(jnp.bfloat16)
            md[p,cols,:]=(dv*0.5).astype(jnp.bfloat16)
        for j in range(N//BK):
            cols=slice(j*BK,(j+1)*BK)
            qd[p,cols,:]=rot(dqa[cols,:]*0.125,cos_v[cols,:],-sin_v[cols,:],lf).astype(jnp.bfloat16)
        joint=jnp.concatenate([qd[p],kd[p],md[p]],axis=1)
        g=dot(h1_v[...],joint,TN)
        for c in range(3): gw_v[p,c*D:(c+1)*D,:]=g[:,c*128:(c+1)*128].astype(jnp.bfloat16)
        for P_ in range(NP):
            @pl.when(p==P_)
            def _():
                runs[P_].start()
        return 0
    lax.fori_loop(0,NP,pair,0)
    for c in proj: c.wait()
    def tok_load(b): return pltpu.make_async_copy(tok_h.at[blk(b)],tokb.at[b%2],blk_sem.at[b%2])
    tok_load(0).start(); tok_load(1).start()
    def input_grad(b,rows):
        gs=[jnp.concatenate([d[p,rows,:] for p in range(NP)],axis=1) for d in (qd,kd,md)]
        out=[]
        for i in range(D//256):
            ws=[v[i//2,:,(i%2)*W:(i%2+1)*W] for v in (pab,pbb,ogb)]
            out.append(dot(gs[0],ws[0],NT)+dot(gs[1],ws[1],NT)+dot(gs[2],ws[2],NT))
        return jnp.concatenate(out,axis=1)
    for b in range(NB//2):
        ghb[b*R:(b+1)*R,:]=input_grad(b,theirs(b)).astype(jnp.bfloat16)
        ex_g1[b].start()
        for a in plan.get(("t",b),[]): a()
    gsum=None
    for b in range(NB//2):
        mine=input_grad(b,blk(b)).astype(jnp.bfloat16).astype(jnp.float32)
        for a in plan.get(("u",b),[]): a()
        ex_g1[b].wait_recv()
        gh=mine+oprv[b*R:(b+1)*R,:].astype(jnp.float32)
        tok_load(b).wait()
        t=tokb[b%2].astype(jnp.float32)
        n,r=norm_block(t,None)
        gn=gh*g1
        part=jnp.sum((gh*n).reshape(R//8,8,D),axis=0)
        gsum=part if gsum is None else gsum+part
        gm_v[b*R:(b+1)*R,:]=(gm_v[b*R:(b+1)*R,:].astype(jnp.float32)+r*(gn-n*jnp.mean(gn*n,axis=-1,keepdims=True))).astype(jnp.bfloat16)
        if b+2<NB//2: tok_load(b+2).start()
        @pl.when(off)
        def _(): sw_gt[b].start()
        @pl.when(diag)
        def _(): lo_gt[b].start()
    gain_v[0,0:8,:]=gsum
    ex_gain[0].start()
    last=plan.get("end",[])
    gain_steps=len(names)
    def gain_step(i):
        ex_gain[i].wait_recv()
        prev=gain_v[0] if i==0 else gain_v[2*i]
        gain_v[2*i+2]=prev+gain_v[2*i+1]
        if i+1<gain_steps: ex_gain[i+1].start()
    gi=0
    for i,a in enumerate(last):
        a()
        if i%3==2 and gi<gain_steps: gain_step(gi); gi+=1
    while gi<gain_steps: gain_step(gi); gi+=1
    gout=pltpu.make_async_copy(gain_v.at[2*gain_steps],gains_o,blk_sem.at[0])
    gout.start()
    for g in gathers.values(): g.drain()
    for r in runs.values(): r.drain_sends()
    gout.wait()
    for c in ex_g1+ex_gain: c.wait_send()
    @pl.when(off)
    def _():
        for c in sw_out+sum(sw_gf,[])+sw_gt: c.wait()
    @pl.when(diag)
    def _():
        for c in lo_out+sum(lo_gf,[])+lo_gt: c.wait()

def FF_TILES(rows,W,D):
    return (rows-4*W*D//128)//(3*D)

def back(groups,length8,tok,pa,pb,og,op,opr,gh,ghr,att,rest,leaf,q,k,m,wq,wk,wv,wo,lse,g1,g2,tables,tiles):
    bf=jnp.bfloat16; f32=jnp.float32; S=jax.ShapeDtypeStruct; V=pltpu.VMEM
    N,D=tok.shape; half=N//2; W=wo.shape[0]; NP=W//128; R=256
    rows=3*tiles*D+W*D//128+3*W*D//128
    levels=1+int(math.log2(groups))
    per=lambda n:sum(n>>(l+1) for l in range(levels))
    recv=sum(per(r[4]) for r in runs_of(tiles,D//128) if r[0]>=2)+per(W*D//128)+NP*per(3*D)
    anyb=pl.BlockSpec(memory_space=pl.ANY); vm=pl.BlockSpec(memory_space=pltpu.VMEM)
    outs=[S((half,D),bf),S((half,D),bf),S((N,W),bf),S((rows,128),bf),S((16,D),f32)]
    gains=2*(2+levels-1)+1
    scratch=[V((2,R,D),bf)]*7+[V((2,R,W),bf),V((half,D),bf),V((half,D),bf),V((half,D),bf),V((N,D),bf),V((half,D),bf),V((NP,N,128),bf),V((NP,8,N),f32),
        V((NP,N,128),bf),V((NP,N,128),bf),V((NP,N,128),bf),V((4,N,128),bf),V((4,N,128),bf),V((2,N,128),bf),V((N,128),f32),V((N,128),f32),V((N,128),f32),
        V((W,D),bf),V((W,D),f32),V(rest.shape,bf),V(leaf.shape,bf),V((recv,128),bf),V((W*D//128,128),bf),V((NP,3*D,128),bf),V((gains,16,D),f32),
        pltpu.SemaphoreType.DMA((192,)),pltpu.SemaphoreType.DMA((192,)),pltpu.SemaphoreType.DMA((64,)),pltpu.SemaphoreType.DMA((18,))]
    return pl.pallas_call(functools.partial(back_kernel,groups),out_shape=outs,
        in_specs=[vm]+[anyb]*18+[vm]*7,out_specs=[anyb]*5,scratch_shapes=scratch,
        compiler_params=pltpu.CompilerParams(collective_id=1,has_side_effects=True,vmem_limit_bytes=63<<20),name="back")(
        length8,tok,pa,pb,og,op,opr,gh,ghr,att,rest,leaf,q,k,m,wq,wk,wv,wo,lse,g1,g2,*tables)

BACK_PLAN={
    ('m', 6):[('a0','g',0)],
    (0, 0):[('a2','f',0),('b3','f',0),('b0','g',0),('c0','g',0)],
    (0, 1):[('c1','g',0)],
    (0, 2):[('b1','g',0)],
    (0, 3):[('out','s',0)],
    (0, 4):[('out','s',1)],
    (0, 5):[('out','s',2)],
    (0, 6):[('b3','f',1),('a0','g',1),('out','s',3)],
    (0, 7):[('C','f',0),('a1','g',0),('out','s',4)],
    (0, 8):[('b0','g',1),('out','s',5)],
    (0, 9):[('c0','g',1),('out','s',6)],
    (1, 0):[('C','f',1),('c1','g',1),('out','s',7)],
    (1, 1):[(('gf',0),'s',0)],
    (1, 2):[('a0','g',2),(('gf',0),'s',1)],
    (1, 3):[('b3','f',2),('a1','g',1),('b1','g',1)],
    (1, 4):[('a2','f',1)],
    (1, 5):[('b0','g',2),('a0','g',3)],
    (1, 6):[('C','f',2)],
    (1, 9):[('b0','g',3)],
    (2, 1):[(0,'f',0),('c0','g',2),(('gf',1),'s',0)],
    (2, 2):[('a2','f',2),(('gf',1),'s',1)],
    (2, 5):[('b3','f',3),('c1','g',2),('c0','g',3)],
    (2, 6):[('C','f',3),('b1','g',2)],
    (2, 7):[('a2','f',3),('b3','g',0)],
    (2, 8):[(0,'f',1),('C','g',0),('a1','g',2)],
    (2, 9):[('a2','g',0),('c1','g',3)],
    (3, 0):[(1,'f',0)],
    (3, 1):[('a1','g',3),(('gf',2),'s',0)],
    (3, 2):[(0,'f',2),('b1','g',3),(('gf',2),'s',1)],
    (3, 3):[(1,'f',1),('C','g',1),('b3','g',1)],
    (3, 5):[('a2','g',1)],
    (3, 7):[(1,'f',2)],
    (3, 8):[(2,'f',0)],
    ('t', 0):[(2,'f',1),(0,'f',3),('b3','g',2),(('gf',3),'s',0)],
    ('t', 1):[(1,'f',3),(('gf',3),'s',1)],
    ('t', 2):[(0,'g',0)],
    ('t', 3):[('C','g',2)],
    ('u', 0):[(2,'f',2)],
    ('u', 2):[('a2','g',2)],
    ('u', 3):[(0,'g',1)],
}
BACK_END=[
    ('b3','g',3),(3,'f',0),(0,'g',2),('C','g',3),(1,'g',0),(1,'g',1),(2,'f',3),(3,'f',1),
    (0,'g',3),(1,'g',2),(2,'g',0),(1,'g',3),(3,'f',2),(2,'g',1),(3,'f',3),(3,'g',0),
    (2,'g',2),(3,'g',1),(2,'g',3),(3,'g',2),('a2','g',3),(3,'g',3),
]

def unpack_kernel(jobs,slots,*refs):
    src=refs[0]; n=max(j[2] for j in jobs)+1
    outs=refs[4:4+n]; raw,wide,in_sem,out_sem,r0,r1,r2,row_in,row_out=refs[4+n+3:]
    rows_in=[pltpu.make_async_copy(a,b,row_in.at[i]) for i,(a,b) in enumerate(zip(refs[1:4],(r0,r1,r2)))]
    rows_out=[pltpu.make_async_copy(b,a,row_out.at[i]) for i,(a,b) in enumerate(zip(refs[4+n:4+n+3],(r0,r1,r2)))]
    for c in rows_in: c.start()
    load=lambda i:pltpu.make_async_copy(src.at[pl.ds(jobs[i][0],jobs[i][1])],raw.at[i%slots,pl.ds(0,jobs[i][1])],in_sem.at[i%slots])
    def store(i):
        _,rows,out,row,col=jobs[i]
        return pltpu.make_async_copy(wide.at[i%slots,pl.ds(0,rows)],outs[out].at[pl.ds(row,rows),pl.ds(col*128,128)],out_sem.at[i%slots])
    for i in range(min(slots,len(jobs))): load(i).start()
    for i in range(len(jobs)):
        rows=jobs[i][1]
        load(i).wait()
        if i>=slots: store(i-slots).wait()
        wide[i%slots,0:rows,:]=raw[i%slots,0:rows,:].astype(jnp.float32)
        store(i).start()
        if i+slots<len(jobs): load(i+slots).start()
        if i==len(jobs)//4:
            for a,b in zip(rows_in,rows_out): a.wait(); b.start()
    for i in range(max(0,len(jobs)-slots),len(jobs)): store(i).wait()
    for c in rows_out: c.wait()

def unpack_all(buf,rows,D,FH,W):
    t=FH//128; n=W//128; d=D//128; slots=8
    jobs=[]; pos=0; first=0
    for m in passes_of(t):
        jobs+=[(pos+(j*m+c)*D,D,j,0,first+c) for j in range(2) for c in range(m)]; pos+=2*m*D
        jobs+=[(pos+c*128*m,128*m,2,first*128,c) for c in range(d)]; pos+=d*128*m
        first+=m
    jobs+=[(pos+c*W,W,3,0,c) for c in range(d)]; pos+=d*W
    jobs+=[(pos+(p*3+j)*D,D,4+j,0,p) for p in range(n) for j in range(3)]
    shapes=[(D,FH),(D,FH),(FH,D),(W,D),(D,W),(D,W),(D,W)]
    most=max(j[1] for j in jobs)
    anyb=pl.BlockSpec(memory_space=pl.ANY)
    return pl.pallas_call(functools.partial(unpack_kernel,jobs,slots),in_specs=[anyb]*4,out_specs=[anyb]*10,
        out_shape=[jax.ShapeDtypeStruct(s,jnp.float32) for s in shapes]+[jax.ShapeDtypeStruct(r.shape,r.dtype) for r in rows],
        scratch_shapes=[pltpu.VMEM((slots,most,128),jnp.bfloat16),pltpu.VMEM((slots,most,128),jnp.float32),pltpu.SemaphoreType.DMA((slots,)),pltpu.SemaphoreType.DMA((slots,))]
            +[pltpu.VMEM(r.shape,r.dtype) for r in rows]+[pltpu.SemaphoreType.DMA((3,)),pltpu.SemaphoreType.DMA((3,))],
        compiler_params=pltpu.CompilerParams(vmem_limit_bytes=60<<20),name="unpack")(buf,*rows)

def per_device(groups,tokens,first_values,out_grad,lengths,gain_attn,gain_mlp,w_query,w_key,w_value,w_out,w_gate,w_up,w_down):
    bf=jnp.bfloat16; f32=jnp.float32
    n=groups
    D=tokens.shape[1]
    g1=gain_attn.reshape(1,D); g2=gain_mlp.reshape(1,D)
    lanes=jnp.arange(128)%(HEAD_DIM//2)
    frequency=jnp.exp(lanes.astype(f32)*(-2.0*math.log(10000.0)/HEAD_DIM))
    coarse=(jnp.arange(SLOT//32)*32).astype(f32)[:,None]*frequency[None,:]
    fine=jnp.arange(32).astype(f32)[:,None]*frequency[None,:]
    tables=(jnp.cos(coarse),jnp.sin(coarse),jnp.cos(fine),jnp.sin(fine))
    length8=jnp.broadcast_to(lengths.reshape(1,1),(8,128))
    (tok,og,len_full,q,k,mixed,att,lse,pa,pb,w_q,w_k,w_v,w_o,w_g,w_u,w_d)=front(n,tokens,first_values,out_grad,length8,g1,tables,(w_query,w_key,w_value,w_out,w_gate,w_up,w_down))
    op,opr,gh,ghr,rest,leaf=mlp(n,len_full,tok,pa,pb,og,g2,(w_gate,w_up,w_down),(w_g,w_u,w_d))
    out,grad_tokens,grad_first,packed,gains=back(n,len_full,tok,pa,pb,og,op,opr,gh,ghr,att,rest,leaf,q,k,mixed,w_q,w_k,w_v,w_o,lse,g1,g2,tables,w_gate.shape[1]//128)
    gains=jnp.sum(gains.reshape(2,8,D),axis=1)
    FH=w_gate.shape[1]; W=w_query.shape[1]
    gwg,gwu,gwd,gwo,gwq,gwk,gwv,out,grad_tokens,grad_first=unpack_all(packed,(out,grad_tokens,grad_first),D,FH,W)
    return (out,grad_tokens,grad_first,gains[0],gains[1],gwq,gwk,gwv,gwo,gwg,gwu,gwd)

def solution(mesh):
    fine=Mesh(mesh.devices.reshape(-1,2,2),ALL)
    rows=P(ALL,None); slot=P(("zy","core"),"head"); col=P(None,"head"); row=P("head",None)
    return jax.shard_map(functools.partial(per_device,fine.devices.shape[0]),mesh=fine,
        in_specs=(rows,slot,rows,P(("zy","core")),P(),P(),col,col,col,row,col,col,row),
        out_specs=(rows,rows,slot,P(),P(),col,col,col,row,col,col,row),check_vma=False)
```
